32 devices in a mesh: grp: 2 (over x), tok: 16 (over z, y, core).
Axes of the slice: x: 2, y: 2, z: 4, core: 2. Of those that a mesh axis runs over, the one named last changes fastest.
Arguments:
- tokens: bfloat16 [4096, 3584], P(('grp', 'tok')), parts along dimension 0, may hold values from -6 to 6
- route_ids: int32 [4096, 8], P(('grp', 'tok')), parts along dimension 0, may hold values from 0 to 255, as said below
- route_weights: float32 [4096, 8], P(('grp', 'tok')), parts along dimension 0, may hold values from 0.05 to 2.5
Outputs:
- expert_hessian: float32 [57344, 3584], P(('grp', 'tok')), parts along dimension 0
- shared_hessian: float32 [32, 896, 896], P(('grp', 'tok')), parts along dimension 0
The draws below stay inside these ranges and needn't reach their ends.
There are 2 independent parts, one for each index of `grp`. The reference program is written for one: setup_inputs(seed, part) draws one part's arguments, and reference() takes and returns one part's arrays. A program takes and returns all parts, laid end to end along the dimension named above; each array names one. Nothing has to cross between parts.
Inputs may be any that keep to these rules, and one draw needn't show every extreme that they name: `route_ids`: ids below 8 name the window experts. Each token names 8 different ids. Among the tokens of one device at most 32 name any one window expert, and in every draw some window expert is named by exactly 32 tokens of every device.
All inputs are finite; a program needn't handle non-finite values.
Results may differ from the reference program's by a relative error of at most 0.004.
Values may be sent and summed in bfloat16 or wider, within the bound.
No kernel may reach another device: no remote copies, remote signals or barrier semaphores. Data moves between devices by JAX's collectives and lax.ppermute only.
A program may use at most 128 MiB of HBM per device.

```python
import math
import jax
import jax.numpy as jnp
from jax import lax

D = 3584
NUM_EXPERTS = 256
TOPK = 8
EXP = 8
CAP = 32
TOK_DEV = 128
TOKENS = 2048
TGRID = 4
TILE = 896
ROUTE_SLOTS = 512


def draw_route_ids(key, part):
    key = jax.random.fold_in(key, 11)
    keys = jax.random.split(key, 6)
    blocks = TOKENS // TOK_DEV
    heavy = jax.random.randint(keys[0], (), 0, EXP)
    levels = jax.random.randint(keys[1], (EXP,), CAP // 4, CAP + 1)
    raw = jax.random.randint(keys[2], (blocks, EXP), 0, CAP + 1)
    scaled_counts = raw * (levels[None, :] + 1) // (CAP + 1)
    is_heavy = jnp.arange(EXP, dtype=jnp.int32)[None, :] == heavy
    counts = jnp.where(is_heavy, CAP, scaled_counts)
    scores = jax.random.randint(keys[3], (blocks, EXP, TOK_DEV), 0, 2 ** 20) * TOK_DEV + jnp.arange(TOK_DEV, dtype=jnp.int32)
    ranks = jnp.argsort(jnp.argsort(scores, axis=2, stable=True), axis=2, stable=True)
    member = ranks < counts[:, :, None]
    member = member.transpose(0, 2, 1).reshape(TOKENS, EXP)
    spread = (NUM_EXPERTS - EXP) // TOPK
    others = EXP + jnp.arange(TOPK, dtype=jnp.int32)[None, :] * spread + jax.random.randint(keys[4], (TOKENS, TOPK), 0, spread)
    base = jnp.where(member, jnp.arange(EXP, dtype=jnp.int32)[None, :], others)
    shuffle = jax.random.randint(keys[5], (TOKENS, TOPK), 0, 2 ** 20) * TOPK + jnp.arange(TOPK, dtype=jnp.int32)
    order = jnp.argsort(shuffle, axis=1, stable=True)
    return jnp.take_along_axis(base, order, axis=1).astype(jnp.int32)


def spiked(drawn, own_key, source, target, parts, factor):
    def block_of(axis_at):
        return (jnp.arange(drawn.shape[axis_at]) // (drawn.shape[axis_at] // parts)).reshape((-1,) + (1,) * (drawn.ndim - 1 - axis_at))

    near = jax.random.permutation(own_key, parts)[block_of(target)]
    other_side = (block_of(target) + parts // 2) % parts
    return jnp.where((block_of(source) == near) | (block_of(source) == other_side), factor * drawn, drawn)


def block_scale(key, shape, cuts, smallest, largest):
    factor_of, own = 1.0, jax.random.fold_in(key, 6)
    for position, parts in cuts:
        steps = jnp.exp(jax.random.uniform(jax.random.fold_in(own, position), (parts,), jnp.float32, smallest / len(cuts), largest / len(cuts)))
        factor_of = factor_of * jnp.repeat(steps, shape[position] // parts).reshape([-1 if axis == position else 1 for axis in range(len(shape))])
    return factor_of


def bell_draw_with(stream_key, extent, scale, bound, cuts, heavy, kind=jnp.bfloat16):
    values = scale * jax.random.normal(stream_key, extent, jnp.float32)
    if cuts:
        values = values * block_scale(stream_key, extent, cuts, -0.22, 0.18)
    return jnp.clip(spiked(values, jax.random.fold_in(stream_key, 3), *heavy), -bound, bound).astype(kind)


def setup_inputs(seed: int = 0, part: int = 0) -> dict:
    key_list = jax.random.split(jax.random.key(seed), 4)
    part_keys = jax.random.split(jax.random.fold_in(key_list[3], part), 4)
    tokens = bell_draw_with(part_keys[0], (TOKENS, D), 1.0, 6.0, ((0, 16),), (0, 1, 16, 2.0))
    route_ids = draw_route_ids(jax.random.fold_in(jax.random.fold_in(key_list[3], part), 71), part)
    route_weights = jnp.clip(jnp.exp(math.log(2.5) - 3.912023 * jax.random.uniform(part_keys[2], (TOKENS, TOPK), jnp.float32) ** block_scale(part_keys[2], (TOKENS, TOPK), ((0, 16),), -0.2, 0.2)), 0.05, 2.5)
    return dict(tokens=tokens, route_ids=route_ids, route_weights=route_weights)


def window_weights(route_ids, route_weights):
    hits = route_ids[:, :, None] == jnp.arange(EXP, dtype=jnp.int32)[None, None, :]
    return lax.optimization_barrier(jnp.sum(jnp.where(hits, route_weights[:, :, None], jnp.zeros_like(route_weights)[:, :, None]), axis=1))

def reference(tokens, route_ids, route_weights):
    weight_table = window_weights(route_ids, route_weights)
    blocks = []
    for expert in range(EXP):
        member = jnp.any(route_ids == expert, axis=1).astype(jnp.int32)
        order = jnp.argsort(1 - member, stable=True)[:ROUTE_SLOTS].astype(jnp.int32)
        rows = jnp.take(tokens, order, axis=0)
        roots = jnp.sqrt(jnp.take(weight_table[:, expert], order, axis=0))
        scaled = (rows.astype(jnp.float32) * roots[:, None]).astype(jnp.bfloat16)
        hessian = jnp.dot(scaled.T, scaled, preferred_element_type=jnp.float32) / (16.0 * CAP)
        blocks.append(hessian)
    expert_hessian = jnp.concatenate(blocks, axis=0)
    full = jnp.dot(tokens.T, tokens, preferred_element_type=jnp.float32) / float(TOKENS)
    tiles = full.reshape(TGRID, TILE, TGRID, TILE).transpose(0, 2, 1, 3).reshape(TGRID * TGRID, TILE, TILE)
    return (expert_hessian, tiles)
```

```python
import math

import jax
import jax.numpy as jnp
from jax import lax
from jax.sharding import PartitionSpec as P

EXP = 8
CAP = 32


def weight_table(route_ids, route_weights):
    hits = route_ids[:, :, None] == jnp.arange(EXP, dtype=jnp.int32)[None, None, :]
    return jnp.sum(
        jnp.where(hits, route_weights[:, :, None], jnp.zeros_like(route_weights)[:, :, None]),
        axis=1,
    )


def pack_rows(rows, weights):
    member = weights > 0
    places = jnp.cumsum(member.astype(jnp.int32), axis=1) - 1
    slots = jnp.arange(CAP, dtype=jnp.int32)
    select = jnp.logical_and(member[:, None, :], places[:, None, :] == slots[None, :, None])
    packed = jnp.einsum(
        "bct,btd->bcd", select.astype(jnp.bfloat16), rows, preferred_element_type=jnp.float32
    )
    roots = jnp.sqrt(jnp.sum(jnp.where(select, weights[:, None, :], 0.0), axis=2))
    return (packed * roots[:, :, None]).astype(jnp.bfloat16)


def on_device(tokens, route_ids, route_weights):
    devices = lax.axis_size("tok")
    position = lax.axis_index("tok")
    tok_rows, width = tokens.shape
    grid = math.isqrt(devices)
    edge = width // grid
    group = devices // EXP
    slab_rows = width // group
    table = lax.all_gather(weight_table(route_ids, route_weights), "tok", tiled=True)
    everyone = lax.all_gather(tokens, "tok", tiled=True)
    own = lax.dynamic_slice_in_dim(table, position // group, 1, 1).reshape(devices, tok_rows)
    all_rows = pack_rows(everyone.reshape(devices, tok_rows, width), own).reshape(-1, width)
    left_rows = lax.dynamic_slice_in_dim(all_rows, (position % group) * slab_rows, slab_rows, 1)
    expert_part = lax.dot_general(
        left_rows, all_rows, (((0,), (0,)), ((), ())), preferred_element_type=jnp.float32
    ) / (16.0 * CAP)
    left = lax.dynamic_slice_in_dim(everyone, (position // grid) * edge, edge, 1)
    right = lax.dynamic_slice_in_dim(everyone, (position % grid) * edge, edge, 1)
    tile = lax.dot_general(
        left, right, (((0,), (0,)), ((), ())), preferred_element_type=jnp.float32
    ) / float(devices * tok_rows)
    return (expert_part, tile[None])


def solution(mesh):
    in_specs = (P(("grp", "tok"), None), P(("grp", "tok"), None), P(("grp", "tok"), None))
    out_specs = (P(("grp", "tok"), None), P(("grp", "tok"), None, None))
    return jax.shard_map(
        on_device, mesh=mesh, in_specs=in_specs, out_specs=out_specs, check_vma=False
    )
```

```python
import math

import jax
import jax.numpy as jnp
from jax import lax
from jax.sharding import PartitionSpec as P

EXP = 8
CAP = 32
CORES = 2
PARTS = 2


def weight_table(route_ids, route_weights):
    hits = route_ids[:, :, None] == jnp.arange(EXP, dtype=jnp.int32)[None, None, :]
    return jnp.sum(
        jnp.where(hits, route_weights[:, :, None], jnp.zeros_like(route_weights)[:, :, None]),
        axis=1,
    )


def selection(weights):
    member = weights > 0
    places = jnp.cumsum(member.astype(jnp.int32), axis=1) - 1
    slots = jnp.arange(CAP, dtype=jnp.int32)
    select = jnp.logical_and(member[:, None, :], places[:, None, :] == slots[None, :, None])
    roots = jnp.sqrt(jnp.sum(jnp.where(select, weights[:, None, :], 0.0), axis=2))
    return select.astype(jnp.bfloat16), roots


def ring_of(chips):
    return list(range(0, chips, 2)) + list(range(chips - 1, 0, -2))


def gather_tokens(tokens, devices):
    chips = devices // CORES
    ring = ring_of(chips)
    ahead = [
        (ring[i] * CORES + c, ring[(i + 1) % chips] * CORES + c)
        for i in range(chips)
        for c in range(CORES)
    ]
    back = [(b, a) for a, b in ahead]
    pair = [(d, d ^ 1) for d in range(devices)]
    position = lax.axis_index("tok")
    core = position % CORES
    place = jnp.array([ring.index(q) for q in range(chips)], jnp.int32)[position // CORES]
    ring_at = jnp.array(ring, jnp.int32)
    width = tokens.shape[1] // PARTS
    own = [tokens[:, h * width : (h + 1) * width] for h in range(PARTS)]
    pieces = [[rows] for rows in own]
    distances = [0]
    going, coming = list(own), list(own)
    for step in range(1, chips // 2):
        for h in range(PARTS):
            going[h] = lax.ppermute(going[h], "tok", ahead)
            coming[h] = lax.ppermute(coming[h], "tok", back)
            pieces[h] += [going[h], coming[h]]
        distances += [-step, step]
    for h in range(PARTS):
        pieces[h].append(
            lax.ppermute(going[h], "tok", ahead) if h % 2 == 0 else lax.ppermute(coming[h], "tok", back)
        )
    distances.append(chips // 2)
    pieces = [p + [lax.ppermute(rows, "tok", pair) for rows in p] for p in pieces]
    chip_ids = ring_at[(place + chips + jnp.array(distances, jnp.int32)) % chips]
    senders = jnp.concatenate([chip_ids * CORES + core, chip_ids * CORES + 1 - core])
    return pieces, senders


def on_device(tokens, route_ids, route_weights):
    devices = lax.axis_size("tok")
    position = lax.axis_index("tok")
    tok_rows, width = tokens.shape
    grid = math.isqrt(devices)
    edge = width // grid
    group = devices // EXP
    slab_rows = width // group
    pieces, senders = gather_tokens(tokens, devices)
    table = lax.all_gather(weight_table(route_ids, route_weights), "tok", tiled=True)
    own = lax.dynamic_slice_in_dim(table, position // group, 1, 1).reshape(devices, tok_rows)
    select, roots = selection(own[senders])
    everyone = [jnp.stack(p) for p in pieces]
    packed = [
        jnp.einsum("bct,btd->bcd", select, rows, preferred_element_type=jnp.float32)
        for rows in everyone
    ]
    all_rows = jnp.concatenate(
        [(rows * roots[:, :, None]).astype(jnp.bfloat16) for rows in packed], axis=2
    ).reshape(-1, width)
    left_rows = lax.dynamic_slice_in_dim(all_rows, (position % group) * slab_rows, slab_rows, 1)
    expert_part = lax.dot_general(
        left_rows, all_rows, (((0,), (0,)), ((), ())), preferred_element_type=jnp.float32
    ) / (16.0 * CAP)
    in_part = grid // PARTS

    def block(index):
        cuts = [
            lax.dynamic_slice_in_dim(rows.reshape(-1, width // PARTS), (index % in_part) * edge, edge, 1)
            for rows in everyone
        ]
        return jnp.where(index // in_part == 0, cuts[0], cuts[1])

    tile = lax.dot_general(
        block(position // grid), block(position % grid), (((0,), (0,)), ((), ())),
        preferred_element_type=jnp.float32,
    ) / float(devices * tok_rows)
    return (expert_part, tile[None])


def solution(mesh):
    in_specs = (P(("grp", "tok"), None), P(("grp", "tok"), None), P(("grp", "tok"), None))
    out_specs = (P(("grp", "tok"), None), P(("grp", "tok"), None, None))
    return jax.shard_map(
        on_device, mesh=mesh, in_specs=in_specs, out_specs=out_specs, check_vma=False
    )
```

```python
import functools
import math

import jax
import jax.numpy as jnp
from jax import lax
from jax.experimental import pallas as pl
from jax.experimental.pallas import tpu as pltpu
from jax.sharding import PartitionSpec as P

EXP = 8
CAP = 32
CORES = 2
TABLE = 128
VMEM = pl.BlockSpec(memory_space=pltpu.VMEM)
SMEM = pl.BlockSpec(memory_space=pltpu.SMEM)
F32 = jnp.float32
BF16 = jnp.bfloat16


def params(mib):
    return pltpu.CompilerParams(vmem_limit_bytes=mib * 2**20)


def message_kernel(tokens, ids, weights, out):
    rows, width = tokens.shape
    out[:, :width] = tokens[...]
    lane = lax.broadcasted_iota(jnp.int32, (rows, TABLE), 1)
    roots = jnp.zeros((rows, TABLE), F32)
    for e in range(EXP):
        root = jnp.sqrt(jnp.sum(jnp.where(ids[...] == e, weights[...], 0.0), axis=1, keepdims=True))
        roots = jnp.where(lane % EXP == e, root, roots)
    high = roots.astype(BF16).astype(F32)
    middle = (roots - high).astype(BF16).astype(F32)
    low = roots - high - middle
    table = jnp.where(lane < EXP, high, jnp.where(lane < 2 * EXP, middle, low))
    out[:, width:] = jnp.where(lane < 3 * EXP, table, 0.0).astype(BF16)


def make_message(tokens, ids, weights):
    rows, width = tokens.shape
    return pl.pallas_call(
        message_kernel,
        out_shape=jax.ShapeDtypeStruct((rows, width + TABLE), BF16),
        in_specs=[VMEM] * 3,
        out_specs=VMEM,
        compiler_params=params(16),
        name="make_message",
    )(tokens, ids, weights)


def absorb_kernel(counts, grid, first, *refs):
    scalars, refs = refs[0], refs[1:]
    total = sum(counts)
    flat, refs = refs[:total], refs[total:]
    if first:
        tile, packed, left, right = refs
    else:
        before, tile, packed, left, right = refs
    pieces, at = [], 0
    for count in counts:
        pieces.append(flat[at : at + count])
        at += count
    width = packed.shape[1]
    edge = tile.shape[0]
    tok_rows = sum(ref.shape[0] for ref in pieces[0])
    expert = scalars[0]
    for slot, which in ((1, left), (2, right)):
        for b in range(grid):

            @pl.when(scalars[slot] == b)
            def _(b=b, which=which):
                row = 0
                for ref in flat:
                    which[row : row + ref.shape[0], :] = ref[:, b * edge : (b + 1) * edge]
                    row += ref.shape[0]

    update = lax.dot_general(
        left[...], right[...], (((0,), (0,)), ((), ())), preferred_element_type=F32
    )
    tile[...] = update if first else before[...] + update
    lane = lax.broadcasted_iota(jnp.int32, (tok_rows, TABLE), 1)
    ours = jnp.logical_and(lane % EXP == expert, lane < 3 * EXP)
    row_at = lax.broadcasted_iota(jnp.int32, (tok_rows, tok_rows), 0)
    column_at = lax.broadcasted_iota(jnp.int32, (tok_rows, tok_rows), 1)
    upto = (column_at <= row_at).astype(F32).astype(BF16)
    slot_at = lax.broadcasted_iota(jnp.int32, (tok_rows, CAP), 1)
    for k, parts in enumerate(pieces):
        table = jnp.concatenate([ref[:, width:].astype(F32) for ref in parts], axis=0)
        root = jnp.sum(jnp.where(ours, table, 0.0), axis=1, keepdims=True)
        member = root > 0.0
        counted = jnp.dot(
            upto,
            jnp.broadcast_to(member.astype(F32), (tok_rows, TABLE)).astype(BF16),
            preferred_element_type=F32,
        )
        place = counted[:, :CAP].astype(jnp.int32) - 1
        select = jnp.logical_and(member, place == slot_at).astype(F32).astype(BF16)
        row, result = 0, None
        for ref in parts:
            rows = ref.shape[0]
            scaled = (ref[:, :width].astype(F32) * root[row : row + rows]).astype(BF16)
            term = lax.dot_general(
                select[row : row + rows], scaled, (((0,), (0,)), ((), ())),
                preferred_element_type=F32,
            )
            result = term if result is None else result + term
            row += rows
        packed[k * CAP : (k + 1) * CAP, :] = result.astype(BF16)


def absorb(scalars, pieces, tile, grid, edge, width):
    flat = [ref for parts in pieces for ref in parts]
    rows = sum(ref.shape[0] for ref in flat)
    first = tile is None
    return pl.pallas_call(
        functools.partial(absorb_kernel, [len(parts) for parts in pieces], grid, first),
        out_shape=(
            jax.ShapeDtypeStruct((edge, edge), F32),
            jax.ShapeDtypeStruct((len(pieces) * CAP, width), BF16),
        ),
        in_specs=[SMEM] + [VMEM] * (len(flat) + (0 if first else 1)),
        out_specs=(VMEM, VMEM),
        scratch_shapes=[pltpu.VMEM((rows, edge), BF16)] * 2,
        cost_estimate=pl.CostEstimate(
            flops=2 * rows * edge * edge + 2 * CAP * rows * width,
            bytes_accessed=2 * rows * width + 8 * edge * edge,
            transcendentals=0,
        ),
        input_output_aliases={} if first else {1 + len(flat): 0},
        compiler_params=params(32),
        name="absorb",
    )(scalars, *flat, *([] if first else [tile]))


def expert_kernel(scalars, *refs):
    *packs, out, across, rows = refs
    slab = out.shape[0]
    slabs = rows.shape[1] // slab

    @pl.when(pl.program_id(0) == 0)
    def _():
        at = 0
        for pack in packs:
            rows[at : at + pack.shape[0], :] = pack[...]
            at += pack.shape[0]
        for s in range(slabs):

            @pl.when(scalars[3] == s)
            def _(s=s):
                across[...] = rows[:, s * slab : (s + 1) * slab].T

    step = out.shape[1]
    start = pl.multiple_of(pl.program_id(0) * step, 128)
    out[...] = jnp.dot(
        across[...], rows[:, pl.ds(start, step)], preferred_element_type=F32
    ) * (1.0 / (16.0 * CAP))


def expert_product(scalars, packs, slab):
    width = packs[0].shape[1]
    total = sum(pack.shape[0] for pack in packs)
    step = 256
    return pl.pallas_call(
        expert_kernel,
        grid=(width // step,),
        out_shape=jax.ShapeDtypeStruct((slab, width), F32),
        in_specs=[SMEM] + [VMEM] * len(packs),
        out_specs=pl.BlockSpec((slab, step), lambda n: (0, n)),
        scratch_shapes=[pltpu.VMEM((slab, total), BF16), pltpu.VMEM((total, width), BF16)],
        cost_estimate=pl.CostEstimate(
            flops=2 * slab * total * width, bytes_accessed=4 * slab * width, transcendentals=0
        ),
        compiler_params=params(44),
        name="expert_product",
    )(scalars, *packs)


def ring_of(chips):
    return list(range(0, chips, 2)) + list(range(chips - 1, 0, -2))


def on_device(tokens, route_ids, route_weights):
    devices = lax.axis_size("tok")
    position = lax.axis_index("tok")
    tok_rows, width = tokens.shape
    grid = math.isqrt(devices)
    edge = width // grid
    group = devices // EXP
    slab_rows = width // group
    chips = devices // CORES
    ring = ring_of(chips)
    ahead = [
        (ring[i] * CORES + c, ring[(i + 1) % chips] * CORES + c)
        for i in range(chips)
        for c in range(CORES)
    ]
    back = [(b, a) for a, b in ahead]
    pair = [(d, d ^ 1) for d in range(devices)]
    scalars = jnp.stack(
        [position // group, position // grid, position % grid, position % group]
    ).astype(jnp.int32)

    def other_core(parts):
        return [lax.ppermute(rows, "tok", pair) for rows in parts]

    own = make_message(tokens, route_ids, route_weights)
    going, coming = own, own
    arrived = [[own]]
    tile, packs = None, []
    for step in range(1, chips // 2 + 1):
        if step < chips // 2:
            going = lax.ppermute(going, "tok", ahead)
            coming = lax.ppermute(coming, "tok", back)
            new = [[going], [coming]]
        else:
            half = tok_rows // 2
            new = [
                [
                    lax.ppermute(going[:half], "tok", ahead),
                    lax.ppermute(coming[half:], "tok", back),
                ]
            ]
        pieces = arrived + [other_core(parts) for parts in arrived]
        tile, packed = absorb(scalars, pieces, tile, grid, edge, width)
        packs.append(packed)
        arrived = new
    pieces = arrived + [other_core(parts) for parts in arrived]
    tile, packed = absorb(scalars, pieces, tile, grid, edge, width)
    packs.append(packed)
    expert_part = expert_product(scalars, packs, slab_rows)
    return (expert_part, (tile * (1.0 / (devices * tok_rows)))[None])


def solution(mesh):
    in_specs = (P(("grp", "tok"), None), P(("grp", "tok"), None), P(("grp", "tok"), None))
    out_specs = (P(("grp", "tok"), None), P(("grp", "tok"), None, None))
    return jax.shard_map(
        on_device, mesh=mesh, in_specs=in_specs, out_specs=out_specs, check_vma=False
    )
```

```python
import functools
import math

import jax
import jax.numpy as jnp
from jax import lax
from jax.experimental import pallas as pl
from jax.experimental.pallas import tpu as pltpu
from jax.sharding import PartitionSpec as P

EXP = 8
CAP = 32
CORES = 2
TABLE = 128
STEP = 256
BUFFERS = 3
VMEM = pl.BlockSpec(memory_space=pltpu.VMEM)
SMEM = pl.BlockSpec(memory_space=pltpu.SMEM)
ANY = pl.BlockSpec(memory_space=pl.ANY)
F32 = jnp.float32
BF16 = jnp.bfloat16
ROWS_WITH_ROWS = (((0,), (0,)), ((), ()))


def params(mib):
    return pltpu.CompilerParams(vmem_limit_bytes=mib * 2**20)


def message_kernel(tokens, ids, weights, out, arrived):
    rows, width = tokens.shape
    copy = pltpu.make_async_copy(tokens, out.at[:, :width], arrived)
    copy.start()
    row_at = lax.broadcasted_iota(jnp.int32, (TABLE, rows), 0)
    roots = jnp.zeros((TABLE, rows), F32)
    for e in range(EXP):
        root = jnp.sqrt(jnp.sum(jnp.where(ids[...] == e, weights[...], 0.0), axis=0, keepdims=True))
        roots = jnp.where(row_at % EXP == e, root, roots)
    high = roots.astype(BF16).astype(F32)
    middle = (roots - high).astype(BF16).astype(F32)
    low = roots - high - middle
    table = jnp.where(row_at < EXP, high, jnp.where(row_at < 2 * EXP, middle, low))
    out[:, width:] = jnp.where(row_at < 3 * EXP, table, 0.0).T.astype(BF16)
    copy.wait()


def make_message(tokens, ids, weights):
    rows, width = tokens.shape
    return pl.pallas_call(
        message_kernel,
        out_shape=jax.ShapeDtypeStruct((rows, width + TABLE), BF16),
        in_specs=[ANY, VMEM, VMEM],
        out_specs=VMEM,
        scratch_shapes=[pltpu.SemaphoreType.DMA],
        compiler_params=params(16),
        name="make_message",
    )(tokens, ids.T, weights.T)


def absorb_kernel(counts, grid, received, final, *refs):
    scalars, refs = refs[0], refs[1:]
    total = sum(counts)
    flat, refs = refs[:total], refs[total:]
    before, refs = refs[:received], refs[received:]
    tiles, packed, scratch = refs[: 1 if final else 2], refs[1 if final else 2], refs[-3:]
    if final:
        scratch = refs[-2:]
    pieces, at = [], 0
    for count in counts:
        pieces.append(flat[at : at + count])
        at += count
    width = packed.shape[1]
    edge = tiles[0].shape[-1]
    tok_rows = sum(ref.shape[0] for ref in pieces[0])
    expert = scalars[0]
    for slot, which in enumerate(scratch, start=1):
        for b in range(grid):

            @pl.when(scalars[slot] == b)
            def _(b=b, which=which):
                row = 0
                for ref in flat:
                    which[row : row + ref.shape[0], :] = ref[:, b * edge : (b + 1) * edge]
                    row += ref.shape[0]

    for k, tile in enumerate(tiles):
        update = lax.dot_general(
            scratch[0][...], scratch[1 + k][...], ROWS_WITH_ROWS, preferred_element_type=F32
        )
        if final:
            for ref in before:
                update = update + ref[...]
            tile[0, :, :] = update * final
        else:
            tile[...] = before[k][...] + update if before else update
    lane = lax.broadcasted_iota(jnp.int32, (tok_rows, TABLE), 1)
    ours = jnp.logical_and(lane % EXP == expert, lane < 3 * EXP)
    row_at = lax.broadcasted_iota(jnp.int32, (tok_rows, tok_rows), 0)
    column_at = lax.broadcasted_iota(jnp.int32, (tok_rows, tok_rows), 1)
    upto = (column_at <= row_at).astype(F32).astype(BF16)
    slot_at = lax.broadcasted_iota(jnp.int32, (tok_rows, CAP), 1)
    for k, parts in enumerate(pieces):
        table = jnp.concatenate([ref[:, width:].astype(F32) for ref in parts], axis=0)
        root = jnp.sum(jnp.where(ours, table, 0.0), axis=1, keepdims=True)
        member = root > 0.0
        counted = jnp.dot(
            upto,
            jnp.broadcast_to(member.astype(F32), (tok_rows, TABLE)).astype(BF16),
            preferred_element_type=F32,
        )
        place = counted[:, :CAP].astype(jnp.int32) - 1
        select = jnp.logical_and(member, place == slot_at).astype(F32).astype(BF16)
        row, result = 0, None
        for ref in parts:
            rows = ref.shape[0]
            scaled = (ref[:, :width].astype(F32) * root[row : row + rows]).astype(BF16)
            term = lax.dot_general(
                select[row : row + rows], scaled, ROWS_WITH_ROWS, preferred_element_type=F32
            )
            result = term if result is None else result + term
            row += rows
        packed[k * CAP : (k + 1) * CAP, :] = result.astype(BF16)


def absorb(scalars, pieces, before, grid, edge, width, final=None):
    flat = [ref for parts in pieces for ref in parts]
    rows = sum(ref.shape[0] for ref in flat)
    tiles = 1 if final else 2
    tile_shape = (1, edge, edge) if final else (edge, edge)
    return pl.pallas_call(
        functools.partial(
            absorb_kernel, [len(parts) for parts in pieces], grid, len(before), final
        ),
        out_shape=[jax.ShapeDtypeStruct(tile_shape, F32)] * tiles
        + [jax.ShapeDtypeStruct((len(pieces) * CAP, width), BF16)],
        in_specs=[SMEM] + [VMEM] * (len(flat) + len(before)),
        out_specs=[VMEM] * (tiles + 1),
        scratch_shapes=[pltpu.VMEM((rows, edge), BF16)] * (tiles + 1),
        cost_estimate=pl.CostEstimate(
            flops=2 * tiles * rows * edge * edge + 2 * CAP * rows * width,
            bytes_accessed=2 * rows * width + 8 * edge * edge,
            transcendentals=0,
        ),
        input_output_aliases={} if final or not before else {1 + len(flat): 0, 2 + len(flat): 1},
        compiler_params=params(32),
        name="absorb",
    )(scalars, *flat, *before)


def place_rows(scalars, pack, at, rows, across, slab):
    rows[at : at + pack.shape[0], :] = pack[...]
    for s in range(rows.shape[1] // slab):

        @pl.when(scalars[4] == s)
        def _(s=s):
            across[:, at : at + pack.shape[0]] = pack[:, s * slab : (s + 1) * slab].T


def prepare_kernel(scalars, *refs):
    *packs, rows, across = refs
    at = 0
    for pack in packs:
        place_rows(scalars, pack, at, rows, across, across.shape[0])
        at += pack.shape[0]


def expert_kernel(scalars, rows_in, across_in, pack, out, rows, across, block, sent):
    slab, width = out.shape
    total = rows.shape[0]
    first = total - pack.shape[0]
    place_rows(scalars, pack, first, rows, across, slab)

    def copy(n, slot):
        start = pl.multiple_of(n * STEP, STEP)
        return pltpu.make_async_copy(
            block.at[slot], out.at[:, pl.ds(start, STEP)], sent.at[slot]
        )

    def body(n, _):
        slot = lax.rem(n, BUFFERS)

        @pl.when(n >= BUFFERS)
        def _():
            copy(n - BUFFERS, slot).wait()

        start = pl.multiple_of(n * STEP, STEP)
        block[slot] = jnp.dot(
            across[...], rows[:, pl.ds(start, STEP)], preferred_element_type=F32
        ) * (1.0 / (16.0 * CAP))
        copy(n, slot).start()
        return 0

    count = width // STEP
    lax.fori_loop(0, count, body, 0)
    for n in range(max(count - BUFFERS, 0), count):
        copy(n, n % BUFFERS).wait()


def expert_product(scalars, packs, last, slab):
    width = last.shape[1]
    ready = sum(pack.shape[0] for pack in packs)
    total = ready + last.shape[0]
    shapes = [jax.ShapeDtypeStruct((total, width), BF16), jax.ShapeDtypeStruct((slab, total), BF16)]
    rows, across = pl.pallas_call(
        prepare_kernel,
        out_shape=shapes,
        in_specs=[SMEM] + [VMEM] * len(packs),
        out_specs=[VMEM] * 2,
        compiler_params=params(32),
        name="prepare_rows",
    )(scalars, *packs)
    return pl.pallas_call(
        expert_kernel,
        out_shape=[jax.ShapeDtypeStruct((slab, width), F32)] + shapes,
        in_specs=[SMEM] + [VMEM] * 3,
        out_specs=[ANY, VMEM, VMEM],
        scratch_shapes=[
            pltpu.VMEM((BUFFERS, slab, STEP), F32),
            pltpu.SemaphoreType.DMA((BUFFERS,)),
        ],
        input_output_aliases={1: 1, 2: 2},
        cost_estimate=pl.CostEstimate(
            flops=2 * slab * total * width, bytes_accessed=4 * slab * width, transcendentals=0
        ),
        compiler_params=params(40),
        name="expert_product",
    )(scalars, rows, across, last)[0]


def ring_of(chips):
    return list(range(0, chips, 2)) + list(range(chips - 1, 0, -2))


def on_device(tokens, route_ids, route_weights):
    devices = lax.axis_size("tok")
    position = lax.axis_index("tok")
    tok_rows, width = tokens.shape
    grid = math.isqrt(devices)
    edge = width // grid
    group = devices // EXP
    slab_rows = width // group
    chips = devices // CORES
    ring = ring_of(chips)
    ahead = [
        (ring[i] * CORES + c, ring[(i + 1) % chips] * CORES + c)
        for i in range(chips)
        for c in range(CORES)
    ]
    back = [(b, a) for a, b in ahead]
    pair = [(d, d ^ 1) for d in range(devices)]
    column = position % grid
    scalars = jnp.stack(
        [
            position // group,
            position // grid,
            column,
            column + 1 - 2 * (column % 2),
            position % group,
        ]
    ).astype(jnp.int32)

    own = make_message(tokens, route_ids, route_weights)
    going, coming = own, own
    arrived = [[own]]
    tiles, packs, exchanged = [], [], []
    for step in range(1, chips // 2):
        going = lax.ppermute(going, "tok", ahead)
        coming = lax.ppermute(coming, "tok", back)
        *tiles, packed = absorb(scalars, arrived, tiles, grid, edge, width)
        going, coming, packed, *tiles = lax.optimization_barrier((going, coming, packed, *tiles))
        packs.append(packed)
        exchanged.append(lax.ppermute(packed, "tok", pair))
        arrived = [[going], [coming]]
    half = tok_rows // 2
    last = [
        lax.ppermute(going[:half], "tok", ahead),
        lax.ppermute(coming[half:], "tok", back),
    ]
    *tiles, packed = absorb(scalars, arrived, tiles, grid, edge, width)
    other_tile = lax.ppermute(tiles[1], "tok", pair)
    packs.append(packed)
    exchanged.append(lax.ppermute(packed, "tok", pair))
    pieces = [last, [lax.ppermute(rows, "tok", pair) for rows in last]]
    tile, packed = absorb(
        scalars, pieces, [tiles[0], other_tile], grid, edge, width, 1.0 / (devices * tok_rows)
    )
    return (expert_product(scalars, packs + exchanged, packed, slab_rows), tile)


def solution(mesh):
    in_specs = (P(("grp", "tok"), None), P(("grp", "tok"), None), P(("grp", "tok"), None))
    out_specs = (P(("grp", "tok"), None), P(("grp", "tok"), None, None))
    return jax.shard_map(
        on_device, mesh=mesh, in_specs=in_specs, out_specs=out_specs, check_vma=False
    )
```

```python
import functools
import math

import jax
import jax.numpy as jnp
from jax import lax
from jax.experimental import pallas as pl
from jax.experimental.pallas import tpu as pltpu
from jax.sharding import PartitionSpec as P

EXP = 8
CAP = 32
CORES = 2
TABLE = 128
VMEM = pl.BlockSpec(memory_space=pltpu.VMEM)
SMEM = pl.BlockSpec(memory_space=pltpu.SMEM)
ANY = pl.BlockSpec(memory_space=pl.ANY)
F32 = jnp.float32
BF16 = jnp.bfloat16
ROWS_WITH_ROWS = (((0,), (0,)), ((), ()))
INVERSE = 1.0 / (16.0 * CAP)
SMALL = pl.CostEstimate(flops=1, bytes_accessed=1, transcendentals=0)


def params(mib):
    return pltpu.CompilerParams(vmem_limit_bytes=mib * 2**20)


def cuts_of(edge):
    first = edge * 4 // 7
    return [(0, first), (first, edge - first)] if edge % 896 == 0 else [(0, edge)]


def message_kernel(cuts, edge, *refs):
    tokens, ids_from, weights_from, *outs = refs
    *outs, ids, weights, small, arrived = outs
    tables = [
        pltpu.make_async_copy(ids_from, ids, small.at[0]),
        pltpu.make_async_copy(weights_from, weights, small.at[1]),
    ]
    for copy in tables:
        copy.start()
    rows, width = tokens.shape
    copies = []
    if len(cuts) == 1:
        copies = [pltpu.make_async_copy(tokens, outs[0].at[:, :width], arrived.at[0])]
    else:
        for (start, length), out in zip(cuts, outs):
            for b in range(width // edge):
                copies.append(
                    pltpu.make_async_copy(
                        tokens.at[:, b * edge + start : b * edge + start + length],
                        out.at[:, b * length : (b + 1) * length],
                        arrived.at[len(copies)],
                    )
                )
    for copy in copies:
        copy.start()
    for copy in tables:
        copy.wait()
    row_at = lax.broadcasted_iota(jnp.int32, (TABLE, rows), 0)
    roots = jnp.zeros((TABLE, rows), F32)
    for e in range(EXP):
        root = jnp.sqrt(jnp.sum(jnp.where(ids[...] == e, weights[...], 0.0), axis=0, keepdims=True))
        roots = jnp.where(row_at % EXP == e, root, roots)
    high = roots.astype(BF16).astype(F32)
    middle = (roots - high).astype(BF16).astype(F32)
    low = roots - high - middle
    table = jnp.where(row_at < EXP, high, jnp.where(row_at < 2 * EXP, middle, low))
    at = width // edge * cuts[0][1]
    outs[0][:, at : at + TABLE] = jnp.where(row_at < 3 * EXP, table, 0.0).T.astype(BF16)
    for copy in copies:
        copy.wait()


def make_message(tokens, ids, weights, cuts, edge):
    rows, width = tokens.shape
    grid = width // edge
    extra = [TABLE] + [0] * (len(cuts) - 1)
    return pl.pallas_call(
        functools.partial(message_kernel, cuts, edge),
        out_shape=[
            jax.ShapeDtypeStruct((rows, grid * length + more), BF16)
            for (_, length), more in zip(cuts, extra)
        ],
        in_specs=[ANY] * 3,
        out_specs=[VMEM] * len(cuts),
        scratch_shapes=[
            pltpu.VMEM(ids.shape[::-1], jnp.int32),
            pltpu.VMEM(ids.shape[::-1], F32),
            pltpu.SemaphoreType.DMA((2,)),
            pltpu.SemaphoreType.DMA((len(cuts) * grid,)),
        ],
        compiler_params=params(16),
        cost_estimate=SMALL,
        name="make_message",
    )(tokens, ids.T, weights.T)


def choose(expert, first, width):
    rows = first.shape[0]
    lane = lax.broadcasted_iota(jnp.int32, (rows, TABLE), 1)
    ours = jnp.logical_and(lane % EXP == expert, lane < 3 * EXP)
    table = first[:, width : width + TABLE].astype(F32)
    root = jnp.sum(jnp.where(ours, table, 0.0), axis=1, keepdims=True)
    member = root > 0.0
    row_at = lax.broadcasted_iota(jnp.int32, (rows, rows), 0)
    column_at = lax.broadcasted_iota(jnp.int32, (rows, rows), 1)
    upto = (column_at <= row_at).astype(F32).astype(BF16)
    counted = jnp.dot(
        upto,
        jnp.broadcast_to(member.astype(F32), (rows, TABLE)).astype(BF16),
        preferred_element_type=F32,
    )
    place = counted[:, :CAP].astype(jnp.int32) - 1
    slot_at = lax.broadcasted_iota(jnp.int32, (rows, CAP), 1)
    return root, jnp.logical_and(member, place == slot_at).astype(F32).astype(BF16)


def pack(root, select, piece, width):
    scaled = (piece[:, :width].astype(F32) * root).astype(BF16)
    return lax.dot_general(
        select, scaled, ROWS_WITH_ROWS, preferred_element_type=F32
    ).astype(BF16)


def fetch_tile(index, pieces, cuts, grid, scratch):
    for b in range(grid):

        @pl.when(index == b)
        def _(b=b):
            row = 0
            for piece in pieces:
                rows = piece[0].shape[0]
                for (start, length), part in zip(cuts, piece):
                    scratch[row : row + rows, start : start + length] = part[
                        :, b * length : (b + 1) * length
                    ]
                row += rows


def pack_kernel(*refs):
    scalars, *firsts, out = refs
    width = out.shape[1]
    for k, first in enumerate(firsts):
        root, select = choose(scalars[0], first, width)
        out[k * CAP : (k + 1) * CAP, :] = pack(root, select, first, width)


def pack_first(scalars, firsts):
    rows, width = firsts[0].shape
    width -= TABLE
    return pl.pallas_call(
        pack_kernel,
        out_shape=jax.ShapeDtypeStruct((len(firsts) * CAP, width), BF16),
        in_specs=[SMEM] + [VMEM] * len(firsts),
        out_specs=VMEM,
        cost_estimate=SMALL,
        compiler_params=params(12),
        name="pack_first",
    )(scalars, *firsts)


def absorb_kernel(cuts, grid, count, started, chosen, *refs):
    scalars, refs = refs[0], refs[1:]
    parts = len(cuts)
    pieces = [refs[k * parts : (k + 1) * parts] for k in range(count)]
    refs = refs[count * parts :]
    before, refs = refs[: 2 * started], refs[2 * started :]
    tiles, packed, scratch = refs[:2], refs[2:-3], refs[-3:]
    for slot, which in enumerate(scratch, start=1):
        fetch_tile(scalars[slot], pieces, cuts, grid, which)
    for k, tile in enumerate(tiles):
        update = lax.dot_general(
            scratch[0][...], scratch[1 + k][...], ROWS_WITH_ROWS, preferred_element_type=F32
        )
        tile[...] = before[k][...] + update if started else update
    if chosen:
        for k, piece in enumerate(pieces):
            root, select = choose(scalars[0], piece[0], grid * cuts[0][1])
            at = 0
            for p in chosen:
                size = grid * cuts[p][1]
                packed[0][k * CAP : (k + 1) * CAP, at : at + size] = pack(
                    root, select, piece[p], size
                )
                at += size


def absorb(scalars, pieces, before, cuts, grid, chosen):
    edge = sum(length for _, length in cuts)
    flat = [part for piece in pieces for part in piece]
    rows = sum(piece[0].shape[0] for piece in pieces)
    width = sum(grid * cuts[p][1] for p in chosen)
    shapes = [jax.ShapeDtypeStruct((edge, edge), F32)] * 2
    if chosen:
        shapes.append(jax.ShapeDtypeStruct((len(pieces) * CAP, width), BF16))
    out = pl.pallas_call(
        functools.partial(absorb_kernel, cuts, grid, len(pieces), bool(before), chosen),
        out_shape=shapes,
        in_specs=[SMEM] + [VMEM] * (len(flat) + len(before)),
        out_specs=[VMEM] * len(shapes),
        scratch_shapes=[pltpu.VMEM((rows, edge), BF16)] * 3,
        cost_estimate=SMALL,
        input_output_aliases={1 + len(flat): 0, 2 + len(flat): 1} if before else {},
        compiler_params=params(14),
        name="absorb",
    )(scalars, *flat, *before)
    return out[:2], out[2:]


def place_rows(slab_at, slabs, packed, begin, at, rows, across):
    count = packed.shape[0]
    width, share = rows.shape[1], across.shape[0]
    rows[at : at + count, :] = packed[:, begin : begin + width]
    for s in range(slabs):

        @pl.when(slab_at == s)
        def _(s=s):
            first = begin + s * share
            across[:, at : at + count] = packed[:, first : first + share].T


def prepare_kernel(slabs, places, *refs):
    scalars, *refs = refs
    rows, across = refs[-2:]
    for (at, begin), packed in zip(places, refs):
        place_rows(scalars[4], slabs, packed, begin, at, rows, across)


def prepare(scalars, packs, places, operands, shape, slabs):
    total, width = shape
    return pl.pallas_call(
        functools.partial(prepare_kernel, slabs, places),
        out_shape=[
            jax.ShapeDtypeStruct((total, width), BF16),
            jax.ShapeDtypeStruct((width // slabs, total), BF16),
        ],
        in_specs=[SMEM] + [VMEM] * (len(packs) + len(operands)),
        out_specs=[VMEM] * 2,
        input_output_aliases={1 + len(packs) + k: k for k in range(len(operands))},
        cost_estimate=SMALL,
        compiler_params=params(12),
        name="prepare_rows",
    )(scalars, *packs, *operands)


def pack_last(scalars, slabs, firsts, parts, rows, across):
    at = rows.shape[0] - CAP * len(parts)
    for first, part in zip(firsts, parts):
        root, select = choose(scalars[0], first, first.shape[1] - TABLE)
        packed = pack(root, select, part, rows.shape[1])
        rows[at : at + CAP, :] = packed
        share = across.shape[0]
        for s in range(slabs):

            @pl.when(scalars[4] == s)
            def _(s=s, at=at, packed=packed):
                across[:, at : at + CAP] = packed[:, s * share : (s + 1) * share].T

        at += CAP


def finish_first_kernel(cuts, grid, slabs, *refs):
    scalars, mine, other, _, _, out, rows, across, staging, sent = refs
    edge = sum(length for _, length in cuts)
    length = cuts[0][1]
    pack_last(scalars, slabs, [mine, other], [mine, other], rows, across)
    left = across[...]
    jobs = []
    if len(cuts) == 1:
        step = staging.shape[2]
        for n in range(staging.shape[0]):
            span = slice(n * step, (n + 1) * step)
            jobs.append(
                (left, rows.at[:, span], staging.at[n], [(slice(None), slice(None), span)])
            )
    else:
        for b in range(grid):
            places = [
                (
                    slice(i * length, (i + 1) * length),
                    slice(i * edge, i * edge + length),
                    slice(b * edge, b * edge + length),
                )
                for i in range(grid // slabs)
            ]
            jobs.append(
                (left, rows.at[:, b * length : (b + 1) * length], staging.at[b], places)
            )
    copies = []
    for left, right, stage, places in jobs:
        stage[...] = jnp.dot(left, right[...], preferred_element_type=F32) * INVERSE
        for source, rows_to, columns_to in places:
            copy = pltpu.make_async_copy(
                stage.at[source], out.at[rows_to, columns_to], sent.at[len(copies)]
            )
            copy.start()
            copies.append(copy)
    for copy in copies:
        copy.wait()


def finish_first(scalars, mine, other, operands, cuts, grid, slabs):
    edge = sum(length for _, length in cuts)
    slab, width = edge * grid // slabs, edge * grid
    rows, across = operands
    if len(cuts) == 1:
        step = 512
        staging = (width // step, slab, step)
        writes = width // step
    else:
        staging = (grid, across.shape[0], cuts[0][1])
        writes = grid * (grid // slabs)
    return pl.pallas_call(
        functools.partial(finish_first_kernel, cuts, grid, slabs),
        out_shape=[
            jax.ShapeDtypeStruct((slab, width), F32),
            jax.ShapeDtypeStruct(rows.shape, BF16),
            jax.ShapeDtypeStruct(across.shape, BF16),
        ],
        in_specs=[SMEM] + [VMEM] * 4,
        out_specs=[ANY, VMEM, VMEM],
        scratch_shapes=[pltpu.VMEM(staging, F32), pltpu.SemaphoreType.DMA((writes,))],
        input_output_aliases={3: 1, 4: 2},
        cost_estimate=SMALL,
        compiler_params=params(20),
        name="finish_first",
    )(scalars, mine, other, rows, across)


def finish_second_kernel(cuts, grid, slabs, final, *refs):
    parts = len(cuts)
    scalars, refs = refs[0], refs[1:]
    mine, refs = refs[:parts], refs[parts:]
    other, refs = refs[:parts], refs[parts:]
    before, refs = refs[:2], refs[2:]
    edge = sum(length for _, length in cuts)
    copies = []
    if parts == 2:
        rows_a, across_a, _, _, _, tile, out, rows_b, across_b = refs[:9]
        left, right, stage_ab, stage_ba, stage_bb, sent = refs[9:]
        pack_last(scalars, slabs, [mine[0], other[0]], [mine[1], other[1]], rows_b, across_b)
        (_, first), (start, length) = cuts
        tiles = grid // slabs

        def write(stage, source, rows_to, columns_to):
            copy = pltpu.make_async_copy(
                stage.at[source], out.at[rows_to, columns_to], sent.at[len(copies)]
            )
            copy.start()
            copies.append(copy)

        for pair in range(grid // 2):
            span = slice(2 * pair * length, 2 * (pair + 1) * length)
            for stage, across, begin, size in (
                (stage_ab.at[pair], across_a, 0, first),
                (stage_bb.at[pair], across_b, start, length),
            ):
                stage[...] = (
                    jnp.dot(across[...], rows_b[:, span], preferred_element_type=F32) * INVERSE
                )
                for j in range(2):
                    column = (2 * pair + j) * edge + start
                    for i in range(tiles):
                        write(
                            stage,
                            (slice(i * size, (i + 1) * size), slice(j * length, (j + 1) * length)),
                            slice(i * edge + begin, i * edge + begin + size),
                            slice(column, column + length),
                        )
        for b in range(grid):
            stage = stage_ba.at[b]
            stage[...] = (
                jnp.dot(
                    across_b[...], rows_a[:, b * first : (b + 1) * first],
                    preferred_element_type=F32,
                )
                * INVERSE
            )
            for i in range(tiles):
                write(
                    stage,
                    slice(i * length, (i + 1) * length),
                    slice(i * edge + start, i * edge + edge),
                    slice(b * edge, b * edge + first),
                )
    else:
        tile, left, right = refs
    pieces = [mine, other]
    fetch_tile(scalars[1], pieces, cuts, grid, left)
    fetch_tile(scalars[2], pieces, cuts, grid, right)
    update = lax.dot_general(left[...], right[...], ROWS_WITH_ROWS, preferred_element_type=F32)
    tile[0, :, :] = (before[0][...] + before[1][...] + update) * final
    for copy in copies:
        copy.wait()


def finish_second(scalars, mine, other, before, hessian, operands, cuts, grid, slabs, final):
    edge = sum(length for _, length in cuts)
    count = 2 * mine[0].shape[0]
    tile = jax.ShapeDtypeStruct((1, edge, edge), F32)
    scratch = [pltpu.VMEM((count, edge), BF16)] * 2
    inputs = [scalars, *mine, *other, *before]
    kernel = functools.partial(finish_second_kernel, cuts, grid, slabs, final)
    if len(cuts) == 1:
        return hessian, pl.pallas_call(
            kernel,
            out_shape=tile,
            in_specs=[SMEM] + [VMEM] * (len(inputs) - 1),
            out_specs=VMEM,
            scratch_shapes=scratch,
            compiler_params=params(20),
            name="finish_tile",
        )(*inputs)
    rows_a, across_a, rows_b, across_b = operands
    length = cuts[1][1]
    at = len(inputs)
    scratch += [
        pltpu.VMEM((grid // 2, across_a.shape[0], 2 * length), F32),
        pltpu.VMEM((grid, across_b.shape[0], cuts[0][1]), F32),
        pltpu.VMEM((grid // 2, across_b.shape[0], 2 * length), F32),
        pltpu.SemaphoreType.DMA((3 * grid * (grid // slabs),)),
    ]
    tile, hessian, _, _ = pl.pallas_call(
        kernel,
        out_shape=[
            tile,
            jax.ShapeDtypeStruct(hessian.shape, F32),
            jax.ShapeDtypeStruct(rows_b.shape, BF16),
            jax.ShapeDtypeStruct(across_b.shape, BF16),
        ],
        in_specs=[SMEM] + [VMEM] * (len(inputs) + 3) + [ANY],
        out_specs=[VMEM, ANY, VMEM, VMEM],
        scratch_shapes=scratch,
        input_output_aliases={at + 4: 1, at + 2: 2, at + 3: 3},
        compiler_params=params(32),
        cost_estimate=SMALL,
        name="finish_second",
    )(*inputs, rows_a, across_a, rows_b, across_b, hessian)
    return hessian, tile


def ring_of(chips):
    return list(range(0, chips, 2)) + list(range(chips - 1, 0, -2))


def on_device(tokens, route_ids, route_weights):
    devices = lax.axis_size("tok")
    position = lax.axis_index("tok")
    tok_rows, width = tokens.shape
    grid = math.isqrt(devices)
    edge = width // grid
    group = devices // EXP
    chips = devices // CORES
    cuts = cuts_of(edge)
    ring = ring_of(chips)
    ahead = [(ring[i], ring[(i + 1) % chips]) for i in range(chips)]
    streams = [
        [(a * CORES + s, b * CORES + s) for a, b in ahead]
        + [(b * CORES + 1 - s, a * CORES + 1 - s) for a, b in ahead]
        for s in range(CORES)
    ]
    pair = [(d, d ^ 1) for d in range(devices)]
    column = position % grid
    scalars = jnp.stack(
        [
            position // group,
            position // grid,
            column,
            column + 1 - 2 * (column % 2),
            position % group,
        ]
    ).astype(jnp.int32)

    def swap(array):
        return lax.ppermute(array, "tok", pair)

    def advance(held, count):
        return [lax.ppermute(held[k], "tok", streams[k]) for k in range(count)]

    def offset(index):
        return 4 * CAP * (index - 1) if index else total - 4 * CAP

    def prepared(packs, begins, operands, part):
        arrays, places = [], []
        for index in sorted(packs):
            for k, array in enumerate(packs[index]):
                arrays.append(array)
                places.append((offset(index) + k * array.shape[0], begins[index]))
        shape = (total, grid * cuts[part][1])
        return prepare(scalars, arrays, places, operands, shape, group)

    rounds = chips // 2
    total = 4 * CAP * rounds
    parts = len(cuts)
    own = make_message(tokens, route_ids, route_weights, cuts, edge)
    firsts = {0: [own[0]]}
    seconds = {0: [own[-1]]}
    packs, late, tiles, waiting = {}, {}, [], None

    def absorbed(index, chosen):
        pieces = [list(piece) for piece in zip(firsts[index], seconds[index])]
        pieces = [piece[:parts] for piece in pieces]
        return absorb(scalars, pieces, tiles, cuts, grid, chosen)

    every = list(range(parts))
    lag = parts - 1
    for step in range(1, rounds + 1 + lag):
        new_first, new_second, made, operands = [], [], {}, []
        if step <= rounds:
            sources = firsts[step - 1] * (CORES if step == 1 else 1)
            new_first = advance(sources, CORES if step < rounds else 1)
        if lag and step > 1:
            sources = seconds[step - 2] * (CORES if step == 2 else 1)
            new_second = advance(sources, CORES if step - 1 < rounds else 1)
        if waiting is not None:
            packs[waiting].append(swap(packs[waiting][0]))
            waiting = None
        if step == rounds:
            late_first = pack_first(scalars, firsts[step - 1])
            late[0] = [late_first, swap(late_first)]
            packs, tiles = lax.optimization_barrier((packs, tiles))
        ready = 0 if step == 1 else step - 1 - lag if step > 1 + lag else None
        if ready is not None and ready < rounds - 1:
            tiles, packed = absorbed(ready, every)
            packs[ready] = list(packed)
            waiting = ready
            if step == rounds:
                packs[ready] = [*packed, swap(packed[0])]
                waiting = None
        elif ready == rounds - 1:
            tiles, packed = absorbed(ready, every[1:])
            if lag:
                late[1] = [*packed, swap(packed[0])]
        if step == rounds:
            begins = [0] * rounds
            joined = {**packs, rounds - 1: late[0]}
            operands = [prepared(joined, begins, [], 0)]
            if lag:
                begins = [grid * cuts[0][1]] * rounds
                operands.append(prepared(packs, begins, [], 1))
        elif step > rounds:
            operands = [held[0], prepared({rounds - 1: late[1]}, [0] * rounds, held[1], 1)]
            made["other"] = swap(firsts[rounds][0])
        state = (new_first, new_second, packs, late, tiles, operands, made)
        state = lax.optimization_barrier(state)
        new_first, new_second, packs, late, tiles, held, made = state
        if step <= rounds:
            firsts[step] = new_first
        if not lag:
            seconds[step] = new_first
        elif step > 1:
            seconds[step - 1] = new_second
    mine = [firsts[rounds][0], seconds[rounds][0]][:parts]
    other = [made["other"] if lag else swap(mine[0])] + [swap(part) for part in mine[1:]]
    other_tile = swap(tiles[1])
    hessian, *first_operands = finish_first(
        scalars, mine[0], other[0], held[0], cuts, grid, group
    )
    hessian, tile = finish_second(
        scalars, mine, other, [tiles[0], other_tile], hessian,
        first_operands + [array for pair_of in held[1:] for array in pair_of],
        cuts, grid, group, 1.0 / (devices * tok_rows),
    )
    return (hessian, tile)


def solution(mesh):
    in_specs = (P(("grp", "tok"), None), P(("grp", "tok"), None), P(("grp", "tok"), None))
    out_specs = (P(("grp", "tok"), None), P(("grp", "tok"), None, None))
    return jax.shard_map(
        on_device, mesh=mesh, in_specs=in_specs, out_specs=out_specs, check_vma=False
    )
```

```python
import functools
import math

import jax
import jax.numpy as jnp
from jax import lax
from jax.experimental import pallas as pl
from jax.experimental.pallas import tpu as pltpu
from jax.sharding import PartitionSpec as P

EXP = 8
CAP = 32
CORES = 2
STEP = 256
HALVES = 2
VMEM = pl.BlockSpec(memory_space=pltpu.VMEM)
SMEM = pl.BlockSpec(memory_space=pltpu.SMEM)
ANY = pl.BlockSpec(memory_space=pl.ANY)
F32 = jnp.float32
BF16 = jnp.bfloat16
ROWS_WITH_ROWS = (((0,), (0,)), ((), ()))
INVERSE = 1.0 / (16.0 * CAP)
SMALL = pl.CostEstimate(flops=1, bytes_accessed=1, transcendentals=0)


def params(mib):
    return pltpu.CompilerParams(vmem_limit_bytes=mib * 2**20)


def table_kernel(ids, weights, roots):
    row_at = lax.broadcasted_iota(jnp.int32, roots.shape, 0)
    table = jnp.zeros(roots.shape, F32)
    for e in range(EXP):
        weight = jnp.sum(jnp.where(ids[...] == e, weights[...], 0.0), axis=0, keepdims=True)
        table = jnp.where(row_at == e, weight, table)
    roots[...] = jnp.sqrt(table)


def make_table(ids, weights):
    return pl.pallas_call(
        table_kernel,
        out_shape=jax.ShapeDtypeStruct((EXP, ids.shape[0]), F32),
        in_specs=[VMEM] * 2,
        out_specs=VMEM,
        cost_estimate=SMALL,
        compiler_params=params(8),
        name="make_table",
    )(ids.T, weights.T)


def choose(expert, roots):
    rows = roots.shape[1]
    row_at = lax.broadcasted_iota(jnp.int32, roots.shape, 0)
    root = jnp.sum(jnp.where(row_at == expert, roots[...], 0.0), axis=0, keepdims=True)
    root = jnp.broadcast_to(root, (CAP, rows))
    member = root > 0.0
    from_at = lax.broadcasted_iota(jnp.int32, (rows, rows), 0)
    to_at = lax.broadcasted_iota(jnp.int32, (rows, rows), 1)
    upto = (from_at <= to_at).astype(F32).astype(BF16)
    counted = jnp.dot(member.astype(F32).astype(BF16), upto, preferred_element_type=F32)
    place = counted.astype(jnp.int32) - 1
    slot_at = lax.broadcasted_iota(jnp.int32, (CAP, rows), 0)
    select = jnp.logical_and(member, place == slot_at)
    scale = jnp.sum(jnp.where(select, root, 0.0), axis=1, keepdims=True)
    return select.astype(F32).astype(BF16), scale


def pack(expert, roots, piece):
    select, scale = choose(expert, roots)
    picked = jnp.dot(select, piece[...], preferred_element_type=F32)
    return (picked * scale).astype(BF16)


def fetch_tile(index, pieces, scratch):
    edge = scratch.shape[1]
    for b in range(pieces[0].shape[1] // edge):

        @pl.when(index == b)
        def _(b=b):
            row = 0
            for piece in pieces:
                rows = piece.shape[0]
                scratch[row : row + rows, :] = piece[:, b * edge : (b + 1) * edge]
                row += rows


def absorb_kernel(count, started, *refs):
    scalars, refs = refs[0], refs[1:]
    pieces, tables, refs = refs[:count], refs[count : 2 * count], refs[2 * count :]
    sums = 1 + HALVES
    before, refs = refs[: sums * started], refs[sums * started :]
    tiles, packed, scratch = refs[:sums], refs[sums], refs[sums + 1 :]
    for slot, which in enumerate(scratch, start=1):
        fetch_tile(scalars[slot], pieces, which)
    for k, own in enumerate((tiles[:1], tiles[1:])):
        update = lax.dot_general(
            scratch[0][...], scratch[1 + k][...], ROWS_WITH_ROWS, preferred_element_type=F32
        )
        rows = update.shape[0] // len(own)
        for h, tile in enumerate(own):
            part = update[h * rows : (h + 1) * rows]
            tile[...] = before[k + h][...] + part if started else part
    for k in range(count):
        packed[k * CAP : (k + 1) * CAP, :] = pack(scalars[0], tables[k], pieces[k])


def absorb(scalars, pieces, tables, before, edge):
    rows, width = pieces[0].shape
    count = len(pieces)
    *tiles, packed = pl.pallas_call(
        functools.partial(absorb_kernel, count, bool(before)),
        out_shape=[jax.ShapeDtypeStruct((edge, edge), F32)]
        + [jax.ShapeDtypeStruct((edge // HALVES, edge), F32)] * HALVES
        + [jax.ShapeDtypeStruct((count * CAP, width), BF16)],
        in_specs=[SMEM] + [VMEM] * (2 * count + len(before)),
        out_specs=[VMEM] * (2 + HALVES),
        scratch_shapes=[pltpu.VMEM((count * rows, edge), BF16)] * 3,
        cost_estimate=SMALL,
        input_output_aliases={1 + 2 * count + k: k for k in range(len(before))},
        compiler_params=params(14),
        name="absorb",
    )(scalars, *pieces, *tables, *before)
    return tiles, packed


def place_rows(slab_at, packed, at, rows, across):
    count, width = packed.shape
    slab = across.shape[0]
    rows[at : at + count, :] = packed
    for s in range(width // slab):

        @pl.when(slab_at == s)
        def _():
            across[:, at : at + count] = packed[:, s * slab : (s + 1) * slab].T


def prepare_kernel(places, *refs):
    scalars, *refs = refs
    rows, across = refs[-2:]
    for at, packed in zip(places, refs):
        place_rows(scalars[4], packed[...], at, rows, across)


def prepare(scalars, packs, places, operands, total, slab):
    width = packs[0].shape[1]
    return pl.pallas_call(
        functools.partial(prepare_kernel, places),
        out_shape=[
            jax.ShapeDtypeStruct((total, width), BF16),
            jax.ShapeDtypeStruct((slab, total), BF16),
        ],
        in_specs=[SMEM] + [VMEM] * (len(packs) + len(operands)),
        out_specs=[VMEM] * 2,
        input_output_aliases={1 + len(packs) + k: k for k in range(len(operands))},
        cost_estimate=SMALL,
        compiler_params=params(12),
        name="prepare_rows",
    )(scalars, *packs, *operands)


def finish_kernel(final, *refs):
    scalars, *refs = refs
    pieces, tables, refs = refs[:2], refs[2:4], refs[4:]
    before, refs = refs[: 1 + HALVES], refs[3 + HALVES :]
    hessian, tile, rows, across, staging, sum_of_tile, left, right, sent = refs
    at = rows.shape[0] - CAP * len(pieces)
    packed = jnp.concatenate(
        [pack(scalars[0], table, piece) for piece, table in zip(pieces, tables)], axis=0
    )
    place_rows(scalars[4], packed, at, rows, across)
    copies = []
    for n in range(staging.shape[0]):
        span = slice(n * STEP, (n + 1) * STEP)
        staging[n, :, :] = (
            jnp.dot(across[...], rows[:, span], preferred_element_type=F32) * INVERSE
        )
        copies.append(pltpu.make_async_copy(staging.at[n], hessian.at[:, span], sent.at[n]))
        copies[-1].start()
    fetch_tile(scalars[1], pieces, left)
    fetch_tile(scalars[2], pieces, right)
    update = lax.dot_general(left[...], right[...], ROWS_WITH_ROWS, preferred_element_type=F32)
    received = jnp.concatenate([part[...] for part in before[1:]], axis=0)
    sum_of_tile[...] = (before[0][...] + received + update) * final
    copies.append(pltpu.make_async_copy(sum_of_tile, tile.at[0], sent.at[len(copies)]))
    copies[-1].start()
    for copy in copies:
        copy.wait()


def finish(scalars, pieces, tables, before, operands, final):
    edge = before[0].shape[0]
    rows, across = operands
    slab, width = across.shape[0], rows.shape[1]
    count = sum(piece.shape[0] for piece in pieces)
    blocks = width // STEP
    return pl.pallas_call(
        functools.partial(finish_kernel, final),
        out_shape=[
            jax.ShapeDtypeStruct((slab, width), F32),
            jax.ShapeDtypeStruct((1, edge, edge), F32),
            jax.ShapeDtypeStruct(rows.shape, BF16),
            jax.ShapeDtypeStruct(across.shape, BF16),
        ],
        in_specs=[SMEM] + [VMEM] * (7 + HALVES),
        out_specs=[ANY, ANY, VMEM, VMEM],
        scratch_shapes=[
            pltpu.VMEM((blocks, slab, STEP), F32),
            pltpu.VMEM((edge, edge), F32),
            pltpu.VMEM((count, edge), BF16),
            pltpu.VMEM((count, edge), BF16),
            pltpu.SemaphoreType.DMA((blocks + 1,)),
        ],
        input_output_aliases={6 + HALVES: 2, 7 + HALVES: 3},
        cost_estimate=SMALL,
        compiler_params=params(38),
        name="finish",
    )(scalars, *pieces, *tables, *before, rows, across)[:2]


def ring_of(chips):
    return list(range(0, chips, 2)) + list(range(chips - 1, 0, -2))


def on_device(tokens, route_ids, route_weights):
    devices = lax.axis_size("tok")
    position = lax.axis_index("tok")
    tok_rows, width = tokens.shape
    grid = math.isqrt(devices)
    edge = width // grid
    group = devices // EXP
    slab = width // group
    chips = devices // CORES
    ring = ring_of(chips)
    ahead = [(ring[i], ring[(i + 1) % chips]) for i in range(chips)]
    streams = [
        [(a * CORES + s, b * CORES + s) for a, b in ahead]
        + [(b * CORES + 1 - s, a * CORES + 1 - s) for a, b in ahead]
        for s in range(CORES)
    ]
    pair = [(d, d ^ 1) for d in range(devices)]
    column = position % grid
    scalars = jnp.stack(
        [
            position // group,
            position // grid,
            column,
            column + 1 - 2 * (column % 2),
            position % group,
        ]
    ).astype(jnp.int32)

    def swap(array):
        return lax.ppermute(array, "tok", pair)

    def advance(held, count):
        return [lax.ppermute(held[k], "tok", streams[k]) for k in range(count)]

    rounds = chips // 2
    total = 4 * CAP * rounds

    def place(index):
        at = 4 * CAP * (index - 1) if index else total - 4 * CAP
        return [at, at + (2 if index else 1) * CAP]

    roots = make_table(route_ids, route_weights)
    pieces, tables = [tokens], [roots]
    packs, tiles = {}, []
    for step in range(1, rounds + 1):
        count = CORES if step < rounds else 1
        repeat = CORES if step == 1 else 1
        new_pieces = advance(pieces * repeat, count)
        new_tables = advance(tables * repeat, count)
        if step > 1:
            packs[step - 2] = [packs[step - 2][0], swap(packs[step - 2][0])]
        tiles, packed = absorb(scalars, pieces, tables, tiles, edge)
        packs[step - 1] = [packed]
        if step < rounds:
            state = (new_pieces, new_tables, packs, tiles)
            new_pieces, new_tables, packs, tiles = lax.optimization_barrier(state)
        pieces, tables = new_pieces, new_tables
    packs[rounds - 1].append(swap(packs[rounds - 1][0]))
    other_sums = [swap(part) for part in tiles[1:]]
    tables = [tables[0], swap(tables[0])]
    operands = []
    for chosen in (range(rounds - 1), [rounds - 1]):
        operands = prepare(
            scalars,
            [array for index in chosen for array in packs[index]],
            [at for index in chosen for at in place(index)],
            operands, total, slab,
        )
    pieces, tables, operands = lax.optimization_barrier((pieces, tables, operands))
    return tuple(
        finish(
            scalars, [pieces[0], swap(pieces[0])], tables, [tiles[0], *other_sums], operands,
            1.0 / (devices * tok_rows),
        )
    )


def solution(mesh):
    in_specs = (P(("grp", "tok"), None), P(("grp", "tok"), None), P(("grp", "tok"), None))
    out_specs = (P(("grp", "tok"), None), P(("grp", "tok"), None, None))
    return jax.shard_map(
        on_device, mesh=mesh, in_specs=in_specs, out_specs=out_specs, check_vma=False
    )
```

```python
import functools
import math

import jax
import jax.numpy as jnp
from jax import lax
from jax.experimental import pallas as pl
from jax.experimental.pallas import tpu as pltpu
from jax.sharding import PartitionSpec as P

EXP = 8
CAP = 32
CORES = 2
TABLE = 128
STEP = 256
HALVES = 2
VMEM = pl.BlockSpec(memory_space=pltpu.VMEM)
SMEM = pl.BlockSpec(memory_space=pltpu.SMEM)
ANY = pl.BlockSpec(memory_space=pl.ANY)
F32 = jnp.float32
BF16 = jnp.bfloat16
ROWS_WITH_ROWS = (((0,), (0,)), ((), ()))
INVERSE = 1.0 / (16.0 * CAP)
SMALL = pl.CostEstimate(flops=1, bytes_accessed=1, transcendentals=0)


def params(mib):
    return pltpu.CompilerParams(vmem_limit_bytes=mib * 2**20)


def message_kernel(tokens, ids_from, weights_from, out, ids, weights, table, arrived):
    rows, width = tokens.shape
    copies = [
        pltpu.make_async_copy(source, target, arrived.at[k])
        for k, (source, target) in enumerate(
            [
                (ids_from, ids),
                (weights_from, weights),
                (tokens, out.at[:, :width]),
                (table, out.at[:, width:]),
            ]
        )
    ]
    for copy in copies[:3]:
        copy.start()
    for copy in copies[:2]:
        copy.wait()
    row_at = lax.broadcasted_iota(jnp.int32, (TABLE, rows), 0)
    roots = jnp.zeros((TABLE, rows), F32)
    for e in range(EXP):
        weight = jnp.sum(jnp.where(ids[...] == e, weights[...], 0.0), axis=0, keepdims=True)
        roots = jnp.where(row_at % EXP == e, jnp.sqrt(weight), roots)
    high = roots.astype(BF16).astype(F32)
    middle = (roots - high).astype(BF16).astype(F32)
    low = roots - high - middle
    terms = jnp.where(row_at < EXP, high, jnp.where(row_at < 2 * EXP, middle, low))
    table[...] = jnp.where(row_at < 3 * EXP, terms, 0.0).T.astype(BF16)
    copies[3].start()
    for copy in copies[2:]:
        copy.wait()


def make_message(tokens, ids, weights):
    rows, width = tokens.shape
    return pl.pallas_call(
        message_kernel,
        out_shape=jax.ShapeDtypeStruct((rows, width + TABLE), BF16),
        in_specs=[ANY] * 3,
        out_specs=ANY,
        scratch_shapes=[
            pltpu.VMEM(ids.shape[::-1], jnp.int32),
            pltpu.VMEM(ids.shape[::-1], F32),
            pltpu.VMEM((rows, TABLE), BF16),
            pltpu.SemaphoreType.DMA((4,)),
        ],
        cost_estimate=SMALL,
        compiler_params=params(57),
        name="make_message",
    )(tokens, ids.T, weights.T)


def choose(expert, table):
    rows = table.shape[0]
    row_at = lax.broadcasted_iota(jnp.int32, (TABLE, rows), 0)
    ours = jnp.logical_and(row_at % EXP == expert, row_at < 3 * EXP)
    root = jnp.sum(jnp.where(ours, table.astype(F32).T, 0.0), axis=0, keepdims=True)
    root = jnp.broadcast_to(root, (CAP, rows))
    member = root > 0.0
    from_at = lax.broadcasted_iota(jnp.int32, (rows, rows), 0)
    to_at = lax.broadcasted_iota(jnp.int32, (rows, rows), 1)
    upto = (from_at <= to_at).astype(F32).astype(BF16)
    counted = jnp.dot(member.astype(F32).astype(BF16), upto, preferred_element_type=F32)
    place = counted.astype(jnp.int32) - 1
    slot_at = lax.broadcasted_iota(jnp.int32, (CAP, rows), 0)
    select = jnp.logical_and(member, place == slot_at)
    scale = jnp.sum(jnp.where(select, root, 0.0), axis=1, keepdims=True)
    return select.astype(F32).astype(BF16), scale


def pack(expert, piece):
    width = piece.shape[1] - TABLE
    select, scale = choose(expert, piece[:, width:])
    picked = jnp.dot(select, piece[:, :width], preferred_element_type=F32)
    return (picked * scale).astype(BF16)


def fetch_tile(index, pieces, scratch):
    edge = scratch.shape[1]
    for b in range((pieces[0].shape[1] - TABLE) // edge):

        @pl.when(index == b)
        def _(b=b):
            row = 0
            for piece in pieces:
                rows = piece.shape[0]
                scratch[row : row + rows, :] = piece[:, b * edge : (b + 1) * edge]
                row += rows


def absorb_kernel(count, started, *refs):
    scalars, refs = refs[0], refs[1:]
    pieces, refs = refs[:count], refs[count:]
    sums = 1 + HALVES
    before, refs = refs[: sums * started], refs[sums * started :]
    tiles, packed, scratch = refs[:sums], refs[sums], refs[sums + 1 :]
    for slot, which in enumerate(scratch, start=1):
        fetch_tile(scalars[slot], pieces, which)
    for k, own in enumerate((tiles[:1], tiles[1:])):
        update = lax.dot_general(
            scratch[0][...], scratch[1 + k][...], ROWS_WITH_ROWS, preferred_element_type=F32
        )
        rows = update.shape[0] // len(own)
        for h, tile in enumerate(own):
            part = update[h * rows : (h + 1) * rows]
            tile[...] = before[k + h][...] + part if started else part
    for k in range(count):
        packed[k * CAP : (k + 1) * CAP, :] = pack(scalars[0], pieces[k])


def absorb(scalars, pieces, before, edge):
    rows, width = pieces[0].shape
    width -= TABLE
    count = len(pieces)
    *tiles, packed = pl.pallas_call(
        functools.partial(absorb_kernel, count, bool(before)),
        out_shape=[jax.ShapeDtypeStruct((edge, edge), F32)]
        + [jax.ShapeDtypeStruct((edge // HALVES, edge), F32)] * HALVES
        + [jax.ShapeDtypeStruct((count * CAP, width), BF16)],
        in_specs=[SMEM] + [VMEM] * (count + len(before)),
        out_specs=[VMEM] * (2 + HALVES),
        scratch_shapes=[pltpu.VMEM((count * rows, edge), BF16)] * 3,
        cost_estimate=SMALL,
        input_output_aliases={1 + count + k: k for k in range(len(before))},
        compiler_params=params(14),
        name="absorb",
    )(scalars, *pieces, *before)
    return tiles, packed


def place_rows(slab_at, packed, at, rows, across):
    count, width = packed.shape
    slab = across.shape[0]
    rows[at : at + count, :] = packed
    for s in range(width // slab):

        @pl.when(slab_at == s)
        def _():
            across[:, at : at + count] = packed[:, s * slab : (s + 1) * slab].T


def prepare_kernel(places, *refs):
    scalars, *refs = refs
    rows, across = refs[-2:]
    for at, packed in zip(places, refs):
        place_rows(scalars[4], packed[...], at, rows, across)


def prepare(scalars, packs, places, operands, total, slab):
    width = packs[0].shape[1]
    return pl.pallas_call(
        functools.partial(prepare_kernel, places),
        out_shape=[
            jax.ShapeDtypeStruct((total, width), BF16),
            jax.ShapeDtypeStruct((slab, total), BF16),
        ],
        in_specs=[SMEM] + [VMEM] * (len(packs) + len(operands)),
        out_specs=[VMEM] * 2,
        input_output_aliases={1 + len(packs) + k: k for k in range(len(operands))},
        cost_estimate=SMALL,
        compiler_params=params(12),
        name="prepare_rows",
    )(scalars, *packs, *operands)


def finish_kernel(final, *refs):
    scalars, *refs = refs
    pieces, refs = refs[:2], refs[2:]
    before, refs = refs[: 1 + HALVES], refs[3 + HALVES :]
    hessian, tile, rows, across, staging, sum_of_tile, left, right, sent = refs
    at = rows.shape[0] - CAP * len(pieces)
    packed = jnp.concatenate(
        [pack(scalars[0], piece) for piece in pieces], axis=0
    )
    place_rows(scalars[4], packed, at, rows, across)
    copies = []
    for n in range(staging.shape[0]):
        span = slice(n * STEP, (n + 1) * STEP)
        staging[n, :, :] = (
            jnp.dot(across[...], rows[:, span], preferred_element_type=F32) * INVERSE
        )
        copies.append(pltpu.make_async_copy(staging.at[n], hessian.at[:, span], sent.at[n]))
        copies[-1].start()
    fetch_tile(scalars[1], pieces, left)
    fetch_tile(scalars[2], pieces, right)
    update = lax.dot_general(left[...], right[...], ROWS_WITH_ROWS, preferred_element_type=F32)
    received = jnp.concatenate([part[...] for part in before[1:]], axis=0)
    sum_of_tile[...] = (before[0][...] + received + update) * final
    copies.append(pltpu.make_async_copy(sum_of_tile, tile.at[0], sent.at[len(copies)]))
    copies[-1].start()
    for copy in copies:
        copy.wait()


def finish(scalars, pieces, before, operands, final):
    edge = before[0].shape[0]
    rows, across = operands
    slab, width = across.shape[0], rows.shape[1]
    count = sum(piece.shape[0] for piece in pieces)
    blocks = width // STEP
    return pl.pallas_call(
        functools.partial(finish_kernel, final),
        out_shape=[
            jax.ShapeDtypeStruct((slab, width), F32),
            jax.ShapeDtypeStruct((1, edge, edge), F32),
            jax.ShapeDtypeStruct(rows.shape, BF16),
            jax.ShapeDtypeStruct(across.shape, BF16),
        ],
        in_specs=[SMEM] + [VMEM] * (5 + HALVES),
        out_specs=[ANY, ANY, VMEM, VMEM],
        scratch_shapes=[
            pltpu.VMEM((blocks, slab, STEP), F32),
            pltpu.VMEM((edge, edge), F32),
            pltpu.VMEM((count, edge), BF16),
            pltpu.VMEM((count, edge), BF16),
            pltpu.SemaphoreType.DMA((blocks + 1,)),
        ],
        input_output_aliases={4 + HALVES: 2, 5 + HALVES: 3},
        cost_estimate=SMALL,
        compiler_params=params(38),
        name="finish",
    )(scalars, *pieces, *before, rows, across)[:2]


def ring_of(chips):
    return list(range(0, chips, 2)) + list(range(chips - 1, 0, -2))


def on_device(tokens, route_ids, route_weights):
    devices = lax.axis_size("tok")
    position = lax.axis_index("tok")
    tok_rows, width = tokens.shape
    grid = math.isqrt(devices)
    edge = width // grid
    group = devices // EXP
    slab = width // group
    chips = devices // CORES
    ring = ring_of(chips)
    ahead = [(ring[i], ring[(i + 1) % chips]) for i in range(chips)]
    streams = [
        [(a * CORES + s, b * CORES + s) for a, b in ahead]
        + [(b * CORES + 1 - s, a * CORES + 1 - s) for a, b in ahead]
        for s in range(CORES)
    ]
    pair = [(d, d ^ 1) for d in range(devices)]
    column = position % grid
    scalars = jnp.stack(
        [
            position // group,
            position // grid,
            column,
            column + 1 - 2 * (column % 2),
            position % group,
        ]
    ).astype(jnp.int32)

    def swap(array):
        return lax.ppermute(array, "tok", pair)

    def advance(held, count):
        return [lax.ppermute(held[k], "tok", streams[k]) for k in range(count)]

    rounds = chips // 2
    total = 4 * CAP * rounds

    def place(index):
        at = 4 * CAP * (index - 1) if index else total - 4 * CAP
        return [at, at + (2 if index else 1) * CAP]

    pieces = [make_message(tokens, route_ids, route_weights)]
    packs, tiles = {}, []
    for step in range(1, rounds + 1):
        count = CORES if step < rounds else 1
        repeat = CORES if step == 1 else 1
        new_pieces = advance(pieces * repeat, count)
        if step > 1:
            packs[step - 2] = [packs[step - 2][0], swap(packs[step - 2][0])]
        tiles, packed = absorb(scalars, pieces, tiles, edge)
        packs[step - 1] = [packed]
        if step < rounds:
            state = (new_pieces, packs, tiles)
            new_pieces, packs, tiles = lax.optimization_barrier(state)
        pieces = new_pieces
    packs[rounds - 1].append(swap(packs[rounds - 1][0]))
    other_sums = [swap(part) for part in tiles[1:]]
    operands = []
    for chosen in (range(rounds - 1), [rounds - 1]):
        operands = prepare(
            scalars,
            [array for index in chosen for array in packs[index]],
            [at for index in chosen for at in place(index)],
            operands, total, slab,
        )
    pieces, operands = lax.optimization_barrier((pieces, operands))
    return tuple(
        finish(
            scalars, [pieces[0], swap(pieces[0])], [tiles[0], *other_sums], operands,
            1.0 / (devices * tok_rows),
        )
    )


def solution(mesh):
    in_specs = (P(("grp", "tok"), None), P(("grp", "tok"), None), P(("grp", "tok"), None))
    out_specs = (P(("grp", "tok"), None), P(("grp", "tok"), None, None))
    return jax.shard_map(
        on_device, mesh=mesh, in_specs=in_specs, out_specs=out_specs, check_vma=False
    )
```

```python
import functools
import math

import jax
import jax.numpy as jnp
from jax import lax
from jax.experimental import pallas as pl
from jax.experimental.pallas import tpu as pltpu
from jax.sharding import PartitionSpec as P

EXP = 8
CAP = 32
CORES = 2
TABLE = 128
STEP = 256
VMEM = pl.BlockSpec(memory_space=pltpu.VMEM)
SMEM = pl.BlockSpec(memory_space=pltpu.SMEM)
ANY = pl.BlockSpec(memory_space=pl.ANY)
F32 = jnp.float32
BF16 = jnp.bfloat16
ROWS_WITH_ROWS = (((0,), (0,)), ((), ()))
INVERSE = 1.0 / (16.0 * CAP)
SMALL = pl.CostEstimate(flops=1, bytes_accessed=1, transcendentals=0)


def params(mib):
    return pltpu.CompilerParams(vmem_limit_bytes=mib * 2**20)


def message_kernel(tokens, ids, weights, out, arrived):
    rows, width = tokens.shape
    copy = pltpu.make_async_copy(tokens, out.at[:, :width], arrived)
    copy.start()
    row_at = lax.broadcasted_iota(jnp.int32, (TABLE, rows), 0)
    roots = jnp.zeros((TABLE, rows), F32)
    for e in range(EXP):
        weight = jnp.sum(jnp.where(ids[...] == e, weights[...], 0.0), axis=0, keepdims=True)
        roots = jnp.where(row_at % EXP == e, jnp.sqrt(weight), roots)
    high = roots.astype(BF16).astype(F32)
    middle = (roots - high).astype(BF16).astype(F32)
    low = roots - high - middle
    terms = jnp.where(row_at < EXP, high, jnp.where(row_at < 2 * EXP, middle, low))
    out[:, width:] = jnp.where(row_at < 3 * EXP, terms, 0.0).T.astype(BF16)
    copy.wait()


def make_message(tokens, ids, weights):
    rows, width = tokens.shape
    return pl.pallas_call(
        message_kernel,
        out_shape=jax.ShapeDtypeStruct((rows, width + TABLE), BF16),
        in_specs=[ANY, VMEM, VMEM],
        out_specs=VMEM,
        scratch_shapes=[pltpu.SemaphoreType.DMA],
        cost_estimate=SMALL,
        compiler_params=params(8),
        name="make_message",
    )(tokens, ids.T, weights.T)


def choose(expert, table):
    rows = table.shape[0]
    row_at = lax.broadcasted_iota(jnp.int32, (TABLE, rows), 0)
    ours = jnp.logical_and(row_at % EXP == expert, row_at < 3 * EXP)
    root = jnp.sum(jnp.where(ours, table.astype(F32).T, 0.0), axis=0, keepdims=True)
    root = jnp.broadcast_to(root, (CAP, rows))
    member = root > 0.0
    from_at = lax.broadcasted_iota(jnp.int32, (rows, rows), 0)
    to_at = lax.broadcasted_iota(jnp.int32, (rows, rows), 1)
    upto = (from_at <= to_at).astype(F32).astype(BF16)
    counted = jnp.dot(member.astype(F32).astype(BF16), upto, preferred_element_type=F32)
    place = counted.astype(jnp.int32) - 1
    slot_at = lax.broadcasted_iota(jnp.int32, (CAP, rows), 0)
    select = jnp.logical_and(member, place == slot_at)
    scale = jnp.sum(jnp.where(select, root, 0.0), axis=1, keepdims=True)
    return select.astype(F32).astype(BF16), scale


def pack(expert, piece):
    width = piece.shape[1] - TABLE
    select, scale = choose(expert, piece[:, width:])
    picked = jnp.dot(select, piece[:, :width], preferred_element_type=F32)
    return (picked * scale).astype(BF16)


def fetch_tile(index, pieces, scratch):
    edge = scratch.shape[1]
    for b in range((pieces[0].shape[1] - TABLE) // edge):

        @pl.when(index == b)
        def _(b=b):
            row = 0
            for piece in pieces:
                rows = piece.shape[0]
                scratch[row : row + rows, :] = piece[:, b * edge : (b + 1) * edge]
                row += rows


def place_rows(slab_at, packed, at, rows, across):
    count, width = packed.shape
    slab = across.shape[0]
    rows[at : at + count, :] = packed
    for s in range(width // slab):

        @pl.when(slab_at == s)
        def _():
            across[:, at : at + count] = packed[:, s * slab : (s + 1) * slab].T


def take_in(scalars, pieces, left, right):
    fetch_tile(scalars[1], pieces, left)
    fetch_tile(scalars[2], pieces, right)
    packed = jnp.concatenate([pack(scalars[0], piece) for piece in pieces], axis=0)
    update = lax.dot_general(left[...], right[...], ROWS_WITH_ROWS, preferred_element_type=F32)
    return packed, update


def absorb_kernel(count, started, at, *refs):
    scalars, refs = refs[0], refs[1:]
    pieces, before, (tile, rows, across, left, right) = refs[:count], refs[count:-5], refs[-5:]
    packed, update = take_in(scalars, pieces, left, right)
    place_rows(scalars[3], packed, at, rows, across)
    tile[...] = before[0][...] + update if started else update


def absorb(scalars, pieces, at, before, shapes):
    rows, edge, count = pieces[0].shape[0], shapes[0].shape[0], len(pieces)
    return pl.pallas_call(
        functools.partial(absorb_kernel, count, bool(before), at),
        out_shape=shapes,
        in_specs=[SMEM] + [VMEM] * (count + len(before)),
        out_specs=[VMEM] * 3,
        scratch_shapes=[pltpu.VMEM((count * rows, edge), BF16)] * 2,
        cost_estimate=SMALL,
        input_output_aliases={1 + count + k: k for k in range(len(before))},
        compiler_params=params(14),
        name="absorb",
    )(scalars, *pieces, *before)


def finish_kernel(final, *refs):
    scalars, mine, other, before, _, _, hessian, tile, rows, across, *scratch = refs
    staging, sums, left, right, sent = scratch
    pieces = [mine, other]
    packed, update = take_in(scalars, pieces, left, right)
    place_rows(scalars[3], packed, rows.shape[0] - packed.shape[0], rows, across)
    copies = []
    for n in range(staging.shape[0]):
        span = slice(n * STEP, (n + 1) * STEP)
        staging[n, :, :] = (
            jnp.dot(across[...], rows[:, span], preferred_element_type=F32) * INVERSE
        )
        copies.append(pltpu.make_async_copy(staging.at[n], hessian.at[:, span], sent.at[n]))
        copies[-1].start()
    sums[...] = (before[...] + update) * final
    copies.append(pltpu.make_async_copy(sums, tile.at[0], sent.at[len(copies)]))
    copies[-1].start()
    for copy in copies:
        copy.wait()


def finish(scalars, pieces, before, final):
    tile, rows, across = before
    edge, slab, width = tile.shape[0], across.shape[0], rows.shape[1]
    count = sum(piece.shape[0] for piece in pieces)
    blocks = width // STEP
    return pl.pallas_call(
        functools.partial(finish_kernel, final),
        out_shape=[
            jax.ShapeDtypeStruct((slab, width), F32),
            jax.ShapeDtypeStruct((1, edge, edge), F32),
            jax.ShapeDtypeStruct(rows.shape, BF16),
            jax.ShapeDtypeStruct(across.shape, BF16),
        ],
        in_specs=[SMEM] + [VMEM] * 5,
        out_specs=[ANY, ANY, VMEM, VMEM],
        scratch_shapes=[
            pltpu.VMEM((blocks, slab, STEP), F32),
            pltpu.VMEM((edge, edge), F32),
            pltpu.VMEM((count, edge), BF16),
            pltpu.VMEM((count, edge), BF16),
            pltpu.SemaphoreType.DMA((blocks + 1,)),
        ],
        input_output_aliases={4: 2, 5: 3},
        cost_estimate=SMALL,
        compiler_params=params(40),
        name="finish",
    )(scalars, *pieces, *before)[:2]


def ring_of(chips):
    return list(range(0, chips, 2)) + list(range(chips - 1, 0, -2))


def on_device(tokens, route_ids, route_weights):
    devices = lax.axis_size("tok")
    position = lax.axis_index("tok")
    tok_rows, width = tokens.shape
    grid = math.isqrt(devices)
    edge = width // grid
    group = devices // EXP
    slab = width // group
    chips = devices // CORES
    ring = ring_of(chips)
    ahead = [
        (ring[i] * CORES + c, ring[(i + 1) % chips] * CORES + c)
        for i in range(chips)
        for c in range(CORES)
    ]
    streams = [ahead, [(b, a) for a, b in ahead]]
    pair = [(d, d ^ 1) for d in range(devices)]
    scalars = jnp.stack(
        [position // group, position // grid, position % grid, position % group]
    ).astype(jnp.int32)
    core = position % CORES
    last_hop = [hop for k in range(CORES) for hop in streams[k][k::CORES]]

    def swap(array):
        return lax.ppermute(array, "tok", pair)

    def advance(held):
        return [lax.ppermute(array, "tok", stream) for array, stream in zip(held, streams)]

    rounds = chips // 2
    total = 4 * CAP * rounds
    shapes = [
        jax.ShapeDtypeStruct((edge, edge), F32),
        jax.ShapeDtypeStruct((total, width), BF16),
        jax.ShapeDtypeStruct((slab, total), BF16),
    ]
    pieces = [make_message(tokens, route_ids, route_weights)]
    sums, waiting = [], []
    for step in range(1, rounds + 1):
        held = pieces * CORES if step == 1 else pieces
        if step < rounds:
            moved = advance(held)
        else:
            moved = [lax.ppermute(jnp.where(core == 0, *held), "tok", last_hop)]
        at = 4 * CAP * (step - 2) if step > 1 else total - 4 * CAP
        waiting.append((at, pieces + [swap(piece) for piece in pieces]))
        while len(waiting) > (1 if step < rounds else 0):
            at, both = waiting.pop(0)
            sums = absorb(scalars, both, at, sums, shapes)
        moved, sums, arrays = lax.optimization_barrier(
            (moved, sums, [both for _, both in waiting])
        )
        waiting = [(at, both) for (at, _), both in zip(waiting, arrays)]
        pieces = moved
    pieces = pieces + [swap(piece) for piece in pieces]
    return tuple(finish(scalars, pieces, sums, 1.0 / (devices * tok_rows)))


def solution(mesh):
    in_specs = (P(("grp", "tok"), None), P(("grp", "tok"), None), P(("grp", "tok"), None))
    out_specs = (P(("grp", "tok"), None), P(("grp", "tok"), None, None))
    return jax.shard_map(
        on_device, mesh=mesh, in_specs=in_specs, out_specs=out_specs, check_vma=False
    )
```

```python
import functools
import math

import jax
import jax.numpy as jnp
from jax import lax
from jax.experimental import pallas as pl
from jax.experimental.pallas import tpu as pltpu
from jax.sharding import PartitionSpec as P

EXP = 8
CAP = 32
CORES = 2
TABLE = 128
STEP = 256
VMEM = pl.BlockSpec(memory_space=pltpu.VMEM)
SMEM = pl.BlockSpec(memory_space=pltpu.SMEM)
ANY = pl.BlockSpec(memory_space=pl.ANY)
F32 = jnp.float32
BF16 = jnp.bfloat16
ROWS_WITH_ROWS = (((0,), (0,)), ((), ()))
INVERSE = 1.0 / (16.0 * CAP)
SMALL = pl.CostEstimate(flops=1, bytes_accessed=1, transcendentals=0)


def params(mib):
    return pltpu.CompilerParams(vmem_limit_bytes=mib * 2**20)


def message_kernel(tokens, ids, weights, out, arrived):
    rows, width = tokens.shape
    copy = pltpu.make_async_copy(tokens, out.at[:, :width], arrived)
    copy.start()
    row_at = lax.broadcasted_iota(jnp.int32, (TABLE, rows), 0)
    roots = jnp.zeros((TABLE, rows), F32)
    for e in range(EXP):
        weight = jnp.sum(jnp.where(ids[...] == e, weights[...], 0.0), axis=0, keepdims=True)
        roots = jnp.where(row_at % EXP == e, jnp.sqrt(weight), roots)
    high = roots.astype(BF16).astype(F32)
    middle = (roots - high).astype(BF16).astype(F32)
    low = roots - high - middle
    terms = jnp.where(row_at < EXP, high, jnp.where(row_at < 2 * EXP, middle, low))
    out[:, width:] = jnp.where(row_at < 3 * EXP, terms, 0.0).T.astype(BF16)
    copy.wait()


def make_message(tokens, ids, weights):
    rows, width = tokens.shape
    return pl.pallas_call(
        message_kernel,
        out_shape=jax.ShapeDtypeStruct((rows, width + TABLE), BF16),
        in_specs=[ANY, VMEM, VMEM],
        out_specs=VMEM,
        scratch_shapes=[pltpu.SemaphoreType.DMA],
        cost_estimate=SMALL,
        compiler_params=params(8),
        name="make_message",
    )(tokens, ids.T, weights.T)


def choose(expert, table):
    rows = table.shape[0]
    row_at = lax.broadcasted_iota(jnp.int32, (TABLE, rows), 0)
    ours = jnp.logical_and(row_at % EXP == expert, row_at < 3 * EXP)
    root = jnp.sum(jnp.where(ours, table.astype(F32).T, 0.0), axis=0, keepdims=True)
    root = jnp.broadcast_to(root, (CAP, rows))
    member = root > 0.0
    from_at = lax.broadcasted_iota(jnp.int32, (rows, rows), 0)
    to_at = lax.broadcasted_iota(jnp.int32, (rows, rows), 1)
    upto = (from_at <= to_at).astype(F32).astype(BF16)
    counted = jnp.dot(member.astype(F32).astype(BF16), upto, preferred_element_type=F32)
    place = counted.astype(jnp.int32) - 1
    slot_at = lax.broadcasted_iota(jnp.int32, (CAP, rows), 0)
    select = jnp.logical_and(member, place == slot_at)
    scale = jnp.sum(jnp.where(select, root, 0.0), axis=1, keepdims=True)
    return select.astype(F32).astype(BF16), scale


def pack(expert, piece):
    width = piece.shape[1] - TABLE
    select, scale = choose(expert, piece[:, width:])
    picked = jnp.dot(select, piece[:, :width], preferred_element_type=F32)
    return (picked * scale).astype(BF16)


def fetch_tile(index, pieces, scratch):
    edge = scratch.shape[1]
    for b in range((pieces[0].shape[1] - TABLE) // edge):

        @pl.when(index == b)
        def _(b=b):
            row = 0
            for piece in pieces:
                rows = piece.shape[0]
                scratch[row : row + rows, :] = piece[:, b * edge : (b + 1) * edge]
                row += rows


def product(left, right):
    return lax.dot_general(left[...], right[...], ROWS_WITH_ROWS, preferred_element_type=F32)


def absorb_kernel(count, started, *refs):
    scalars, refs = refs[0], refs[1:]
    pieces, before, refs = refs[:count], refs[count : count + 3 * started], refs[count + 3 * started :]
    tile, left, theirs, *packs, mine = refs
    for slot, which in enumerate((left, mine, theirs), start=1):
        fetch_tile(scalars[slot], pieces, which)
    update = product(left, mine)
    if started:
        update = before[0][...] + update + product(before[1], before[2])
    tile[...] = update
    for piece, packed in zip(pieces, packs):
        packed[...] = pack(scalars[0], piece)


def absorb(scalars, pieces, before, edge):
    rows, width = pieces[0].shape
    width -= TABLE
    count = len(pieces)
    columns = jax.ShapeDtypeStruct((count * rows, edge), BF16)
    out = pl.pallas_call(
        functools.partial(absorb_kernel, count, bool(before)),
        out_shape=[jax.ShapeDtypeStruct((edge, edge), F32), columns, columns]
        + [jax.ShapeDtypeStruct((CAP, width), BF16)] * count,
        in_specs=[SMEM] + [VMEM] * (count + len(before)),
        out_specs=[VMEM] * (3 + count),
        scratch_shapes=[pltpu.VMEM((count * rows, edge), BF16)],
        cost_estimate=SMALL,
        input_output_aliases={1 + count: 0} if before else {},
        compiler_params=params(14),
        name="absorb",
    )(scalars, *pieces, *before)
    return out[0], out[1:3], out[3:]


def place_rows(slab_at, packed, at, rows, across):
    count, width = packed.shape
    slab = across.shape[0]
    rows[at : at + count, :] = packed
    for s in range(width // slab):

        @pl.when(slab_at == s)
        def _():
            across[:, at : at + count] = packed[:, s * slab : (s + 1) * slab].T


def prepare_kernel(places, *refs):
    scalars, *refs = refs
    rows, across = refs[-2:]
    for at, packed in zip(places, refs):
        place_rows(scalars[4], packed[...], at, rows, across)


def prepare(scalars, packs, places, operands, total, slab):
    width = packs[0].shape[1]
    return pl.pallas_call(
        functools.partial(prepare_kernel, places),
        out_shape=[
            jax.ShapeDtypeStruct((total, width), BF16),
            jax.ShapeDtypeStruct((slab, total), BF16),
        ],
        in_specs=[SMEM] + [VMEM] * (len(packs) + len(operands)),
        out_specs=[VMEM] * 2,
        input_output_aliases={1 + len(packs) + k: k for k in range(len(operands))},
        cost_estimate=SMALL,
        compiler_params=params(12),
        name="prepare_rows",
    )(scalars, *packs, *operands)


def finish_kernel(final, *refs):
    scalars, halves, refs = refs[0], refs[1:5], refs[5:]
    before, (hessian, tile, rows, across, *scratch) = refs[:3], refs[5:]
    staging, sums, left, right, sent = scratch
    pieces = [
        jnp.concatenate([halves[k][...], halves[k + 1][...]], axis=0) for k in range(0, 4, 2)
    ]
    packed = jnp.concatenate([pack(scalars[0], piece) for piece in pieces], axis=0)
    place_rows(scalars[4], packed, rows.shape[0] - packed.shape[0], rows, across)
    copies = []
    for n in range(staging.shape[0]):
        span = slice(n * STEP, (n + 1) * STEP)
        staging[n, :, :] = (
            jnp.dot(across[...], rows[:, span], preferred_element_type=F32) * INVERSE
        )
        copies.append(pltpu.make_async_copy(staging.at[n], hessian.at[:, span], sent.at[n]))
        copies[-1].start()
    fetch_tile(scalars[1], halves, left)
    fetch_tile(scalars[2], halves, right)
    sums[...] = (
        before[0][...] + product(before[1], before[2]) + product(left, right)
    ) * final
    copies.append(pltpu.make_async_copy(sums, tile.at[0], sent.at[len(copies)]))
    copies[-1].start()
    for copy in copies:
        copy.wait()


def finish(scalars, halves, before, operands, final):
    edge = before[0].shape[0]
    rows, across = operands
    slab, width = across.shape[0], rows.shape[1]
    count = sum(half.shape[0] for half in halves)
    blocks = width // STEP
    return pl.pallas_call(
        functools.partial(finish_kernel, final),
        out_shape=[
            jax.ShapeDtypeStruct((slab, width), F32),
            jax.ShapeDtypeStruct((1, edge, edge), F32),
            jax.ShapeDtypeStruct(rows.shape, BF16),
            jax.ShapeDtypeStruct(across.shape, BF16),
        ],
        in_specs=[SMEM] + [VMEM] * 9,
        out_specs=[ANY, ANY, VMEM, VMEM],
        scratch_shapes=[
            pltpu.VMEM((blocks, slab, STEP), F32),
            pltpu.VMEM((edge, edge), F32),
            pltpu.VMEM((count, edge), BF16),
            pltpu.VMEM((count, edge), BF16),
            pltpu.SemaphoreType.DMA((blocks + 1,)),
        ],
        input_output_aliases={8: 2, 9: 3},
        cost_estimate=SMALL,
        compiler_params=params(38),
        name="finish",
    )(scalars, *halves, *before, rows, across)[:2]


def ring_of(chips):
    return list(range(0, chips, 2)) + list(range(chips - 1, 0, -2))


def on_device(tokens, route_ids, route_weights):
    devices = lax.axis_size("tok")
    position = lax.axis_index("tok")
    tok_rows, width = tokens.shape
    grid = math.isqrt(devices)
    edge = width // grid
    group = devices // EXP
    slab = width // group
    chips = devices // CORES
    ring = ring_of(chips)
    ahead = [
        (ring[i] * CORES + c, ring[(i + 1) % chips] * CORES + c)
        for i in range(chips)
        for c in range(CORES)
    ]
    streams = [ahead, [(b, a) for a, b in ahead]]
    pair = [(d, d ^ 1) for d in range(devices)]
    column = position % grid
    scalars = jnp.stack(
        [
            position // group,
            position // grid,
            column,
            column + 1 - 2 * (column % 2),
            position % group,
        ]
    ).astype(jnp.int32)

    def swap(array):
        return lax.ppermute(array, "tok", pair)

    def advance(held):
        return [lax.ppermute(array, "tok", stream) for array, stream in zip(held, streams)]

    rounds = chips // 2
    total = 4 * CAP * rounds

    def place(index):
        at = 4 * CAP * (index - 1) if index else total - 4 * CAP
        return [at + k * CAP for k in range(4 if index else 2)]

    pieces = [make_message(tokens, route_ids, route_weights)]
    packs, sums = {}, []
    half = tok_rows // 2
    for step in range(1, rounds + 1):
        held = pieces * CORES if step == 1 else pieces
        if step == rounds:
            held = [held[0][:half], held[1][half:]]
        moved = advance(held)
        tile, columns, packed = absorb(scalars, pieces, sums, edge)
        packs[step - 1] = list(packed) + [swap(array) for array in packed]
        sums = [tile] + [swap(array) for array in columns]
        if step < rounds:
            moved, packs, sums = lax.optimization_barrier((moved, packs, sums))
        pieces = moved
    operands = []
    for chosen in (range(rounds - 1), [rounds - 1]):
        operands = prepare(
            scalars,
            [array for index in chosen for array in packs[index]],
            [at for index in chosen for at in place(index)],
            operands, total, slab,
        )
    pieces, operands, sums = lax.optimization_barrier((pieces, operands, sums))
    others = [swap(piece) for piece in pieces]
    return tuple(finish(scalars, pieces + others, sums, operands, 1.0 / (devices * tok_rows)))


def solution(mesh):
    in_specs = (P(("grp", "tok"), None), P(("grp", "tok"), None), P(("grp", "tok"), None))
    out_specs = (P(("grp", "tok"), None), P(("grp", "tok"), None, None))
    return jax.shard_map(
        on_device, mesh=mesh, in_specs=in_specs, out_specs=out_specs, check_vma=False
    )
```

```python
import functools
import math

import jax
import jax.numpy as jnp
from jax import lax
from jax.experimental import pallas as pl
from jax.experimental.pallas import tpu as pltpu
from jax.sharding import PartitionSpec as P

EXP = 8
CAP = 32
CORES = 2
TABLE = 128
STEP = 512
VMEM = pl.BlockSpec(memory_space=pltpu.VMEM)
SMEM = pl.BlockSpec(memory_space=pltpu.SMEM)
ANY = pl.BlockSpec(memory_space=pl.ANY)
F32 = jnp.float32
BF16 = jnp.bfloat16
ROWS_WITH_ROWS = (((0,), (0,)), ((), ()))
INVERSE = 1.0 / (16.0 * CAP)
SMALL = pl.CostEstimate(flops=1, bytes_accessed=1, transcendentals=0)


def params(mib):
    return pltpu.CompilerParams(vmem_limit_bytes=mib * 2**20)


def message_kernel(tokens, ids, weights, out, arrived):
    rows, width = tokens.shape
    copy = pltpu.make_async_copy(tokens, out.at[:, :width], arrived)
    copy.start()
    row_at = lax.broadcasted_iota(jnp.int32, (TABLE, rows), 0)
    roots = jnp.zeros((TABLE, rows), F32)
    for e in range(EXP):
        weight = jnp.sum(jnp.where(ids[...] == e, weights[...], 0.0), axis=0, keepdims=True)
        roots = jnp.where(row_at % EXP == e, jnp.sqrt(weight), roots)
    high = roots.astype(BF16).astype(F32)
    middle = (roots - high).astype(BF16).astype(F32)
    low = roots - high - middle
    terms = jnp.where(row_at < EXP, high, jnp.where(row_at < 2 * EXP, middle, low))
    out[:, width:] = jnp.where(row_at < 3 * EXP, terms, 0.0).T.astype(BF16)
    copy.wait()


def make_message(tokens, ids, weights):
    rows, width = tokens.shape
    return pl.pallas_call(
        message_kernel,
        out_shape=jax.ShapeDtypeStruct((rows, width + TABLE), BF16),
        in_specs=[ANY, VMEM, VMEM],
        out_specs=VMEM,
        scratch_shapes=[pltpu.SemaphoreType.DMA],
        cost_estimate=SMALL,
        compiler_params=params(8),
        name="make_message",
    )(tokens, ids.T, weights.T)


def choose(expert, table):
    rows = table.shape[0]
    row_at = lax.broadcasted_iota(jnp.int32, (TABLE, rows), 0)
    ours = jnp.logical_and(row_at % EXP == expert, row_at < 3 * EXP)
    root = jnp.sum(jnp.where(ours, table.astype(F32).T, 0.0), axis=0, keepdims=True)
    root = jnp.broadcast_to(root, (CAP, rows))
    member = root > 0.0
    from_at = lax.broadcasted_iota(jnp.int32, (rows, rows), 0)
    to_at = lax.broadcasted_iota(jnp.int32, (rows, rows), 1)
    upto = (from_at <= to_at).astype(F32).astype(BF16)
    counted = jnp.dot(member.astype(F32).astype(BF16), upto, preferred_element_type=F32)
    place = counted.astype(jnp.int32) - 1
    slot_at = lax.broadcasted_iota(jnp.int32, (CAP, rows), 0)
    select = jnp.logical_and(member, place == slot_at)
    scale = jnp.sum(jnp.where(select, root, 0.0), axis=1, keepdims=True)
    return select.astype(F32).astype(BF16), scale


def pack(expert, piece):
    width = piece.shape[1] - TABLE
    select, scale = choose(expert, piece[:, width:])
    picked = jnp.dot(select, piece[:, :width], preferred_element_type=F32)
    return (picked * scale).astype(BF16)


def fetch_tile(index, pieces, scratch):
    edge = scratch.shape[1]
    for b in range((pieces[0].shape[1] - TABLE) // edge):

        @pl.when(index == b)
        def _(b=b):
            row = 0
            for piece in pieces:
                rows = piece.shape[0]
                scratch[row : row + rows, :] = piece[:, b * edge : (b + 1) * edge]
                row += rows


def product(left, right):
    return lax.dot_general(left[...], right[...], ROWS_WITH_ROWS, preferred_element_type=F32)


def absorb_kernel(count, started, *refs):
    scalars, refs = refs[0], refs[1:]
    pieces, before, refs = refs[:count], refs[count : count + 3 * started], refs[count + 3 * started :]
    tile, left, theirs, *packs, mine = refs
    for slot, which in enumerate((left, mine, theirs), start=1):
        fetch_tile(scalars[slot], pieces, which)
    update = product(left, mine)
    if started:
        update = before[0][...] + update + product(before[1], before[2])
    tile[...] = update
    for piece, packed in zip(pieces, packs):
        packed[...] = pack(scalars[0], piece)


def absorb(scalars, pieces, before, edge):
    rows, width = pieces[0].shape
    width -= TABLE
    count = len(pieces)
    columns = jax.ShapeDtypeStruct((count * rows, edge), BF16)
    out = pl.pallas_call(
        functools.partial(absorb_kernel, count, bool(before)),
        out_shape=[jax.ShapeDtypeStruct((edge, edge), F32), columns, columns]
        + [jax.ShapeDtypeStruct((CAP, width), BF16)] * count,
        in_specs=[SMEM] + [VMEM] * (count + len(before)),
        out_specs=[VMEM] * (3 + count),
        scratch_shapes=[pltpu.VMEM((count * rows, edge), BF16)],
        cost_estimate=SMALL,
        input_output_aliases={1 + count: 0} if before else {},
        compiler_params=params(14),
        name="absorb",
    )(scalars, *pieces, *before)
    return out[0], out[1:3], out[3:]


def place_rows(slab_at, packed, at, rows, across):
    count, width = packed.shape
    slab = across.shape[0]
    rows[at : at + count, :] = packed
    for s in range(width // slab):

        @pl.when(slab_at == s)
        def _():
            across[:, at : at + count] = packed[:, s * slab : (s + 1) * slab].T


def prepare_kernel(count, at, *refs):
    scalars, packs, (rows, across) = refs[0], refs[1 : 1 + count], refs[-2:]
    packed = jnp.concatenate([array[...] for array in packs], axis=0)
    place_rows(scalars[4], packed, at, rows, across)


def prepare(scalars, packs, at, operands, total, slab):
    width = packs[0].shape[1]
    return pl.pallas_call(
        functools.partial(prepare_kernel, len(packs), at),
        out_shape=[
            jax.ShapeDtypeStruct((total, width), BF16),
            jax.ShapeDtypeStruct((slab, total), BF16),
        ],
        in_specs=[SMEM] + [VMEM] * (len(packs) + len(operands)),
        out_specs=[VMEM] * 2,
        input_output_aliases={1 + len(packs) + k: k for k in range(len(operands))},
        cost_estimate=SMALL,
        compiler_params=params(12),
        name="prepare_rows",
    )(scalars, *packs, *operands)


def finish_kernel(final, *refs):
    scalars, halves, refs = refs[0], refs[1:5], refs[5:]
    before, (hessian, tile, rows, across, *scratch) = refs[:3], refs[5:]
    staging, sums, left, right, sent = scratch
    pieces = [
        jnp.concatenate([halves[k][...], halves[k + 1][...]], axis=0) for k in range(0, 4, 2)
    ]
    packed = jnp.concatenate([pack(scalars[0], piece) for piece in pieces], axis=0)
    place_rows(scalars[4], packed, rows.shape[0] - packed.shape[0], rows, across)
    copies = []
    for n in range(staging.shape[0]):
        span = slice(n * STEP, (n + 1) * STEP)
        staging[n, :, :] = (
            jnp.dot(across[...], rows[:, span], preferred_element_type=F32) * INVERSE
        )
        copies.append(pltpu.make_async_copy(staging.at[n], hessian.at[:, span], sent.at[n]))
        copies[-1].start()
    fetch_tile(scalars[1], halves, left)
    fetch_tile(scalars[2], halves, right)
    sums[...] = (
        before[0][...] + product(before[1], before[2]) + product(left, right)
    ) * final
    copies.append(pltpu.make_async_copy(sums, tile.at[0], sent.at[len(copies)]))
    copies[-1].start()
    for copy in copies:
        copy.wait()


def finish(scalars, halves, before, operands, final):
    edge = before[0].shape[0]
    rows, across = operands
    slab, width = across.shape[0], rows.shape[1]
    count = sum(half.shape[0] for half in halves)
    blocks = width // STEP
    return pl.pallas_call(
        functools.partial(finish_kernel, final),
        out_shape=[
            jax.ShapeDtypeStruct((slab, width), F32),
            jax.ShapeDtypeStruct((1, edge, edge), F32),
            jax.ShapeDtypeStruct(rows.shape, BF16),
            jax.ShapeDtypeStruct(across.shape, BF16),
        ],
        in_specs=[SMEM] + [VMEM] * 9,
        out_specs=[ANY, ANY, VMEM, VMEM],
        scratch_shapes=[
            pltpu.VMEM((blocks, slab, STEP), F32),
            pltpu.VMEM((edge, edge), F32),
            pltpu.VMEM((count, edge), BF16),
            pltpu.VMEM((count, edge), BF16),
            pltpu.SemaphoreType.DMA((blocks + 1,)),
        ],
        input_output_aliases={8: 2, 9: 3},
        cost_estimate=SMALL,
        compiler_params=params(38),
        name="finish",
    )(scalars, *halves, *before, rows, across)[:2]


def ring_of(chips):
    return list(range(0, chips, 2)) + list(range(chips - 1, 0, -2))


def on_device(tokens, route_ids, route_weights):
    devices = lax.axis_size("tok")
    position = lax.axis_index("tok")
    tok_rows, width = tokens.shape
    grid = math.isqrt(devices)
    edge = width // grid
    group = devices // EXP
    slab = width // group
    chips = devices // CORES
    ring = ring_of(chips)
    ahead = [
        (ring[i] * CORES + c, ring[(i + 1) % chips] * CORES + c)
        for i in range(chips)
        for c in range(CORES)
    ]
    streams = [ahead, [(b, a) for a, b in ahead]]
    pair = [(d, d ^ 1) for d in range(devices)]
    column = position % grid
    scalars = jnp.stack(
        [
            position // group,
            position // grid,
            column,
            column + 1 - 2 * (column % 2),
            position % group,
        ]
    ).astype(jnp.int32)

    def swap(array):
        return lax.ppermute(array, "tok", pair)

    def advance(held):
        return [lax.ppermute(array, "tok", stream) for array, stream in zip(held, streams)]

    rounds = chips // 2
    total = 4 * CAP * rounds

    pieces = [make_message(tokens, route_ids, route_weights)]
    operands, sums = [], []
    half = tok_rows // 2
    for step in range(1, rounds + 1):
        held = pieces * CORES if step == 1 else pieces
        if step == rounds:
            held = [held[0][:half], held[1][half:]]
        moved = advance(held)
        tile, columns, packed = absorb(scalars, pieces, sums, edge)
        sums = [tile] + [swap(array) for array in columns]
        at = 4 * CAP * (step - 2) if step > 1 else total - 4 * CAP
        packs = list(packed) + [swap(array) for array in packed]
        operands = prepare(scalars, packs, at, operands, total, slab)
        if step < rounds:
            moved, operands, sums = lax.optimization_barrier((moved, operands, sums))
        pieces = moved
    pieces, operands, sums = lax.optimization_barrier((pieces, operands, sums))
    others = [swap(piece) for piece in pieces]
    return tuple(finish(scalars, pieces + others, sums, operands, 1.0 / (devices * tok_rows)))


def solution(mesh):
    in_specs = (P(("grp", "tok"), None), P(("grp", "tok"), None), P(("grp", "tok"), None))
    out_specs = (P(("grp", "tok"), None), P(("grp", "tok"), None, None))
    return jax.shard_map(
        on_device, mesh=mesh, in_specs=in_specs, out_specs=out_specs, check_vma=False
    )
```

```python
import functools
import math

import jax
import jax.numpy as jnp
from jax import lax
from jax.experimental import pallas as pl
from jax.experimental.pallas import tpu as pltpu
from jax.sharding import PartitionSpec as P

EXP = 8
CAP = 32
CORES = 2
TABLE = 128
STEP = 512
VMEM = pl.BlockSpec(memory_space=pltpu.VMEM)
SMEM = pl.BlockSpec(memory_space=pltpu.SMEM)
ANY = pl.BlockSpec(memory_space=pl.ANY)
F32 = jnp.float32
BF16 = jnp.bfloat16
ROWS_WITH_ROWS = (((0,), (0,)), ((), ()))
INVERSE = 1.0 / (16.0 * CAP)
SMALL = pl.CostEstimate(flops=1, bytes_accessed=1, transcendentals=0)


def params(mib):
    return pltpu.CompilerParams(vmem_limit_bytes=mib * 2**20)


def message_kernel(tokens, ids, weights, out, arrived):
    rows, width = tokens.shape
    copy = pltpu.make_async_copy(tokens, out.at[:, :width], arrived)
    copy.start()
    row_at = lax.broadcasted_iota(jnp.int32, (TABLE, rows), 0)
    roots = jnp.zeros((TABLE, rows), F32)
    for e in range(EXP):
        weight = jnp.sum(jnp.where(ids[...] == e, weights[...], 0.0), axis=0, keepdims=True)
        roots = jnp.where(row_at % EXP == e, jnp.sqrt(weight), roots)
    high = roots.astype(BF16).astype(F32)
    middle = (roots - high).astype(BF16).astype(F32)
    low = roots - high - middle
    terms = jnp.where(row_at < EXP, high, jnp.where(row_at < 2 * EXP, middle, low))
    out[:, width:] = jnp.where(row_at < 3 * EXP, terms, 0.0).T.astype(BF16)
    copy.wait()


def make_message(tokens, ids, weights):
    rows, width = tokens.shape
    return pl.pallas_call(
        message_kernel,
        out_shape=jax.ShapeDtypeStruct((rows, width + TABLE), BF16),
        in_specs=[ANY, VMEM, VMEM],
        out_specs=VMEM,
        scratch_shapes=[pltpu.SemaphoreType.DMA],
        cost_estimate=SMALL,
        compiler_params=params(8),
        name="make_message",
    )(tokens, ids.T, weights.T)


def choose(expert, table):
    rows = table.shape[0]
    row_at = lax.broadcasted_iota(jnp.int32, (TABLE, rows), 0)
    ours = jnp.logical_and(row_at % EXP == expert, row_at < 3 * EXP)
    root = jnp.sum(jnp.where(ours, table.astype(F32).T, 0.0), axis=0, keepdims=True)
    root = jnp.broadcast_to(root, (CAP, rows))
    member = root > 0.0
    from_at = lax.broadcasted_iota(jnp.int32, (rows, rows), 0)
    to_at = lax.broadcasted_iota(jnp.int32, (rows, rows), 1)
    upto = (from_at <= to_at).astype(F32).astype(BF16)
    counted = jnp.dot(member.astype(F32).astype(BF16), upto, preferred_element_type=F32)
    place = counted.astype(jnp.int32) - 1
    slot_at = lax.broadcasted_iota(jnp.int32, (CAP, rows), 0)
    select = jnp.logical_and(member, place == slot_at)
    scale = jnp.sum(jnp.where(select, root, 0.0), axis=1, keepdims=True)
    return select.astype(F32).astype(BF16), scale


def pack(expert, piece):
    width = piece.shape[1] - TABLE
    select, scale = choose(expert, piece[:, width:])
    picked = jnp.dot(select, piece[:, :width], preferred_element_type=F32)
    return (picked * scale).astype(BF16)


def fetch_tile(index, pieces, scratch):
    edge = scratch.shape[1]
    for b in range((pieces[0].shape[1] - TABLE) // edge):

        @pl.when(index == b)
        def _(b=b):
            row = 0
            for piece in pieces:
                rows = piece.shape[0]
                scratch[row : row + rows, :] = piece[:, b * edge : (b + 1) * edge]
                row += rows


def product(left, right):
    return lax.dot_general(left[...], right[...], ROWS_WITH_ROWS, preferred_element_type=F32)


def absorb_kernel(count, started, *refs):
    scalars, refs = refs[0], refs[1:]
    pieces, before, refs = refs[:count], refs[count : count + 3 * started], refs[count + 3 * started :]
    tile, left, theirs, *packs, mine = refs
    for slot, which in enumerate((left, mine, theirs), start=1):
        fetch_tile(scalars[slot], pieces, which)
    update = product(left, mine)
    if started:
        update = before[0][...] + update + product(before[1], before[2])
    tile[...] = update
    for piece, packed in zip(pieces, packs):
        packed[...] = pack(scalars[0], piece)


def absorb(scalars, pieces, before, edge):
    rows, width = pieces[0].shape
    width -= TABLE
    count = len(pieces)
    columns = jax.ShapeDtypeStruct((count * rows, edge), BF16)
    out = pl.pallas_call(
        functools.partial(absorb_kernel, count, bool(before)),
        out_shape=[jax.ShapeDtypeStruct((edge, edge), F32), columns, columns]
        + [jax.ShapeDtypeStruct((CAP, width), BF16)] * count,
        in_specs=[SMEM] + [VMEM] * (count + len(before)),
        out_specs=[VMEM] * (3 + count),
        scratch_shapes=[pltpu.VMEM((count * rows, edge), BF16)],
        cost_estimate=SMALL,
        input_output_aliases={1 + count: 0} if before else {},
        compiler_params=params(14),
        name="absorb",
    )(scalars, *pieces, *before)
    return out[0], out[1:3], out[3:]


def place_rows(slab_at, packed, at, rows, across):
    count, width = packed.shape
    slab = across.shape[0]
    rows[at : at + count, :] = packed
    for s in range(width // slab):

        @pl.when(slab_at == s)
        def _():
            across[:, at : at + count] = packed[:, s * slab : (s + 1) * slab].T


def prepare_kernel(count, at, *refs):
    scalars, packs, (rows, across) = refs[0], refs[1 : 1 + count], refs[-2:]
    packed = jnp.concatenate([array[...] for array in packs], axis=0)
    place_rows(scalars[4], packed, at, rows, across)


def prepare(scalars, packs, at, operands, total, slab):
    width = packs[0].shape[1]
    return pl.pallas_call(
        functools.partial(prepare_kernel, len(packs), at),
        out_shape=[
            jax.ShapeDtypeStruct((total, width), BF16),
            jax.ShapeDtypeStruct((slab, total), BF16),
        ],
        in_specs=[SMEM] + [VMEM] * (len(packs) + len(operands)),
        out_specs=[VMEM] * 2,
        input_output_aliases={1 + len(packs) + k: k for k in range(len(operands))},
        cost_estimate=SMALL,
        compiler_params=params(12),
        name="prepare_rows",
    )(scalars, *packs, *operands)


def take_in(scalars, halves, at, rows, across, left, right):
    piece = jnp.concatenate([half[...] for half in halves], axis=0)
    place_rows(scalars[4], pack(scalars[0], piece), at, rows, across)
    fetch_tile(scalars[1], halves, left)
    fetch_tile(scalars[2], halves, right)
    return product(left, right)


def take_own_kernel(*refs):
    scalars, halves, before, refs = refs[0], refs[1:3], refs[3:6], refs[8:]
    tile, rows, across, left, right = refs
    update = before[0][...] + product(before[1], before[2])
    at = rows.shape[0] - 2 * CAP
    tile[...] = update + take_in(scalars, halves, at, rows, across, left, right)


def take_own(scalars, halves, sums, operands):
    edge = sums[0].shape[0]
    count = sum(half.shape[0] for half in halves)
    return pl.pallas_call(
        take_own_kernel,
        out_shape=[jax.ShapeDtypeStruct(a.shape, a.dtype) for a in (sums[0], *operands)],
        in_specs=[SMEM] + [VMEM] * 7,
        out_specs=[VMEM] * 3,
        scratch_shapes=[pltpu.VMEM((count, edge), BF16)] * 2,
        input_output_aliases={3: 0, 6: 1, 7: 2},
        cost_estimate=SMALL,
        compiler_params=params(14),
        name="take_own",
    )(scalars, *halves, *sums, *operands)


def finish_kernel(final, *refs):
    scalars, halves, before, (hessian, tile, rows, across, *scratch) = (
        refs[0], refs[1:3], refs[3], refs[6:]
    )
    staging, sums, left, right, sent = scratch
    at = rows.shape[0] - CAP
    copies = []

    def write(source, target):
        copies.append(pltpu.make_async_copy(source, target, sent.at[len(copies)]))
        copies[-1].start()

    update = take_in(scalars, halves, at, rows, across, left, right)
    sums[...] = (before[...] + update) * final
    write(sums, tile.at[0])
    for n in range(staging.shape[0]):
        span = slice(n * STEP, (n + 1) * STEP)
        staging[n, :, :] = (
            jnp.dot(across[...], rows[:, span], preferred_element_type=F32) * INVERSE
        )
        write(staging.at[n], hessian.at[:, span])
    for copy in copies:
        copy.wait()


def finish(scalars, halves, before, operands, final):
    edge = before.shape[0]
    rows, across = operands
    slab, width = across.shape[0], rows.shape[1]
    count = sum(half.shape[0] for half in halves)
    blocks = width // STEP
    return pl.pallas_call(
        functools.partial(finish_kernel, final),
        out_shape=[
            jax.ShapeDtypeStruct((slab, width), F32),
            jax.ShapeDtypeStruct((1, edge, edge), F32),
            jax.ShapeDtypeStruct(rows.shape, BF16),
            jax.ShapeDtypeStruct(across.shape, BF16),
        ],
        in_specs=[SMEM] + [VMEM] * 5,
        out_specs=[ANY, ANY, VMEM, VMEM],
        scratch_shapes=[
            pltpu.VMEM((blocks, slab, STEP), F32),
            pltpu.VMEM((edge, edge), F32),
            pltpu.VMEM((count, edge), BF16),
            pltpu.VMEM((count, edge), BF16),
            pltpu.SemaphoreType.DMA((blocks + 1,)),
        ],
        input_output_aliases={4: 2, 5: 3},
        cost_estimate=SMALL,
        compiler_params=params(38),
        name="finish",
    )(scalars, *halves, before, rows, across)[:2]


def ring_of(chips):
    return list(range(0, chips, 2)) + list(range(chips - 1, 0, -2))


def on_device(tokens, route_ids, route_weights):
    devices = lax.axis_size("tok")
    position = lax.axis_index("tok")
    tok_rows, width = tokens.shape
    grid = math.isqrt(devices)
    edge = width // grid
    group = devices // EXP
    slab = width // group
    chips = devices // CORES
    ring = ring_of(chips)
    ahead = [
        (ring[i] * CORES + c, ring[(i + 1) % chips] * CORES + c)
        for i in range(chips)
        for c in range(CORES)
    ]
    streams = [ahead, [(b, a) for a, b in ahead]]
    pair = [(d, d ^ 1) for d in range(devices)]
    column = position % grid
    scalars = jnp.stack(
        [
            position // group,
            position // grid,
            column,
            column + 1 - 2 * (column % 2),
            position % group,
        ]
    ).astype(jnp.int32)

    def swap(array):
        return lax.ppermute(array, "tok", pair)

    def advance(held):
        return [lax.ppermute(array, "tok", stream) for array, stream in zip(held, streams)]

    rounds = chips // 2
    total = 4 * CAP * rounds

    pieces = [make_message(tokens, route_ids, route_weights)]
    operands, sums = [], []
    half = tok_rows // 2
    for step in range(1, rounds + 1):
        held = pieces * CORES if step == 1 else pieces
        if step == rounds:
            held = [held[0][:half], held[1][half:]]
        moved = advance(held)
        tile, columns, packed = absorb(scalars, pieces, sums, edge)
        sums = [tile] + [swap(array) for array in columns]
        at = 4 * CAP * (step - 2) if step > 1 else total - 4 * CAP
        packs = list(packed) + [swap(array) for array in packed]
        operands = prepare(scalars, packs, at, operands, total, slab)
        if step < rounds:
            ahead_of, operands, sums = lax.optimization_barrier((moved[0], operands, sums))
            back_of, operands, sums = lax.optimization_barrier((moved[1], operands, sums))
            moved = [ahead_of, back_of]
        pieces = moved
    pieces, operands, sums = lax.optimization_barrier((pieces, operands, sums))
    others = [swap(piece) for piece in pieces]
    tile, *operands = take_own(scalars, pieces, sums, operands)
    return tuple(finish(scalars, others, tile, operands, 1.0 / (devices * tok_rows)))


def solution(mesh):
    in_specs = (P(("grp", "tok"), None), P(("grp", "tok"), None), P(("grp", "tok"), None))
    out_specs = (P(("grp", "tok"), None), P(("grp", "tok"), None, None))
    return jax.shard_map(
        on_device, mesh=mesh, in_specs=in_specs, out_specs=out_specs, check_vma=False
    )
```

```python
import functools
import math

import jax
import jax.numpy as jnp
from jax import lax
from jax.experimental import pallas as pl
from jax.experimental.pallas import tpu as pltpu
from jax.sharding import PartitionSpec as P

EXP = 8
CAP = 32
CORES = 2
LANES = 128
TABLE = 32
STEP = 512
SPLITS = 7
VMEM = pl.BlockSpec(memory_space=pltpu.VMEM)
SMEM = pl.BlockSpec(memory_space=pltpu.SMEM)
ANY = pl.BlockSpec(memory_space=pl.ANY)
F32 = jnp.float32
BF16 = jnp.bfloat16
ROWS_WITH_ROWS = (((0,), (0,)), ((), ()))
INVERSE = 1.0 / (16.0 * CAP)
SMALL = pl.CostEstimate(flops=1, bytes_accessed=1, transcendentals=0)


def params(mib):
    return pltpu.CompilerParams(vmem_limit_bytes=mib * 2**20)


def message_kernel(tokens, ids, weights, out):
    rows, width = tokens.shape
    for b in range(width // LANES):
        out[b * rows : (b + 1) * rows, :] = tokens[:, b * LANES : (b + 1) * LANES]
    row_at = lax.broadcasted_iota(jnp.int32, (TABLE, rows), 0)
    roots = jnp.zeros((TABLE, rows), F32)
    for e in range(EXP):
        weight = jnp.sum(jnp.where(ids[...] == e, weights[...], 0.0), axis=0, keepdims=True)
        roots = jnp.where(row_at % EXP == e, jnp.sqrt(weight), roots)
    high = roots.astype(BF16).astype(F32)
    middle = (roots - high).astype(BF16).astype(F32)
    low = roots - high - middle
    terms = jnp.where(row_at < EXP, high, jnp.where(row_at < 2 * EXP, middle, low))
    out[rows * width // LANES :, :] = jnp.where(row_at < 3 * EXP, terms, 0.0).astype(BF16)


def make_message(tokens, ids, weights):
    rows, width = tokens.shape
    return pl.pallas_call(
        message_kernel,
        out_shape=jax.ShapeDtypeStruct((rows * width // LANES + TABLE, LANES), BF16),
        in_specs=[VMEM] * 3,
        out_specs=VMEM,
        cost_estimate=SMALL,
        compiler_params=params(8),
        name="make_message",
    )(tokens, ids.T, weights.T)


def block_of(piece, index):
    for array in piece:
        inside = array.shape[0] // LANES
        if index < inside:
            return array.at[index * LANES : (index + 1) * LANES]
        index -= inside


def choose(expert, piece):
    last = piece[-1]
    table = last[last.shape[0] - TABLE :, :].astype(F32)
    row_at = lax.broadcasted_iota(jnp.int32, (TABLE, LANES), 0)
    ours = jnp.logical_and(row_at % EXP == expert, row_at < 3 * EXP)
    root = jnp.sum(jnp.where(ours, table, 0.0), axis=0, keepdims=True)
    root = jnp.broadcast_to(root, (CAP, LANES))
    member = root > 0.0
    from_at = lax.broadcasted_iota(jnp.int32, (LANES, LANES), 0)
    to_at = lax.broadcasted_iota(jnp.int32, (LANES, LANES), 1)
    upto = (from_at <= to_at).astype(F32).astype(BF16)
    counted = jnp.dot(member.astype(F32).astype(BF16), upto, preferred_element_type=F32)
    place = counted.astype(jnp.int32) - 1
    slot_at = lax.broadcasted_iota(jnp.int32, (CAP, LANES), 0)
    select = jnp.logical_and(member, place == slot_at)
    scale = jnp.sum(jnp.where(select, root, 0.0), axis=1, keepdims=True)
    return select.astype(F32).astype(BF16), scale


def pack(expert, piece):
    select, scale = choose(expert, piece)
    blocks = sum(array.shape[0] // LANES for array in piece)
    groups = []
    for b in range(0, blocks, 4):
        some = jnp.concatenate(
            [block_of(piece, k)[...] for k in range(b, min(b + 4, blocks))], axis=1
        )
        picked = jnp.dot(select, some, preferred_element_type=F32)
        groups.append((picked * scale).astype(BF16))
    return jnp.concatenate(groups, axis=1)


def fetch_tile(index, pieces, scratch):
    edge = scratch.shape[1]
    blocks = sum(array.shape[0] // LANES for array in pieces[0])
    for b in range(blocks * LANES // edge):

        @pl.when(index == b)
        def _(b=b):
            for k, piece in enumerate(pieces):
                at = b * edge
                while at < (b + 1) * edge:
                    first = at % LANES
                    count = min(LANES - first, (b + 1) * edge - at)
                    scratch[k * LANES : (k + 1) * LANES, at - b * edge : at - b * edge + count] = (
                        block_of(piece, at // LANES)[:, first : first + count]
                    )
                    at += count


def product(left, right):
    return lax.dot_general(left[...], right[...], ROWS_WITH_ROWS, preferred_element_type=F32)


def absorb_kernel(count, started, *refs):
    scalars, refs = refs[0], refs[1:]
    pieces, refs = [[ref] for ref in refs[:count]], refs[count:]
    before, refs = refs[: 3 * started], refs[3 * started :]
    tile, left, theirs, *packs, mine = refs
    for slot, which in enumerate((left, mine, theirs), start=1):
        fetch_tile(scalars[slot], pieces, which)
    update = product(left, mine)
    if started:
        update = before[0][...] + update + product(before[1], before[2])
    tile[...] = update
    for piece, packed in zip(pieces, packs):
        packed[...] = pack(scalars[0], piece)


def absorb(scalars, pieces, before, edge):
    rows, width = LANES, pieces[0].shape[0] - TABLE
    count = len(pieces)
    columns = jax.ShapeDtypeStruct((count * rows, edge), BF16)
    out = pl.pallas_call(
        functools.partial(absorb_kernel, count, bool(before)),
        out_shape=[jax.ShapeDtypeStruct((edge, edge), F32), columns, columns]
        + [jax.ShapeDtypeStruct((CAP, width), BF16)] * count,
        in_specs=[SMEM] + [VMEM] * (count + len(before)),
        out_specs=[VMEM] * (3 + count),
        scratch_shapes=[pltpu.VMEM((count * rows, edge), BF16)],
        cost_estimate=SMALL,
        input_output_aliases={1 + count: 0} if before else {},
        compiler_params=params(14),
        name="absorb",
    )(scalars, *pieces, *before)
    return out[0], out[1:3], out[3:]


def place_rows(slab_at, packed, at, rows, across):
    count, width = packed.shape
    slab = across.shape[0]
    rows[at : at + count, :] = packed
    for s in range(width // slab):

        @pl.when(slab_at == s)
        def _():
            across[:, at : at + count] = packed[:, s * slab : (s + 1) * slab].T


def prepare_kernel(count, at, *refs):
    scalars, packs, (rows, across) = refs[0], refs[1 : 1 + count], refs[-2:]
    packed = jnp.concatenate([array[...] for array in packs], axis=0)
    place_rows(scalars[4], packed, at, rows, across)


def prepare(scalars, packs, at, operands, total, slab):
    width = packs[0].shape[1]
    return pl.pallas_call(
        functools.partial(prepare_kernel, len(packs), at),
        out_shape=[
            jax.ShapeDtypeStruct((total, width), BF16),
            jax.ShapeDtypeStruct((slab, total), BF16),
        ],
        in_specs=[SMEM] + [VMEM] * (len(packs) + len(operands)),
        out_specs=[VMEM] * 2,
        input_output_aliases={1 + len(packs) + k: k for k in range(len(operands))},
        cost_estimate=SMALL,
        compiler_params=params(12),
        name="prepare_rows",
    )(scalars, *packs, *operands)


def take_in(scalars, halves, at, rows, across, left, right):
    place_rows(scalars[4], pack(scalars[0], halves), at, rows, across)
    fetch_tile(scalars[1], [halves], left)
    fetch_tile(scalars[2], [halves], right)
    return product(left, right)


def take_own_kernel(*refs):
    scalars, halves, before, refs = refs[0], refs[1:3], refs[3:6], refs[8:]
    tile, rows, across, left, right = refs
    update = before[0][...] + product(before[1], before[2])
    at = rows.shape[0] - 2 * CAP
    tile[...] = update + take_in(scalars, halves, at, rows, across, left, right)


def take_own(scalars, halves, sums, operands):
    edge = sums[0].shape[0]
    return pl.pallas_call(
        take_own_kernel,
        out_shape=[jax.ShapeDtypeStruct(a.shape, a.dtype) for a in (sums[0], *operands)],
        in_specs=[SMEM] + [VMEM] * 7,
        out_specs=[VMEM] * 3,
        scratch_shapes=[pltpu.VMEM((LANES, edge), BF16)] * 2,
        input_output_aliases={3: 0, 6: 1, 7: 2},
        cost_estimate=SMALL,
        compiler_params=params(14),
        name="take_own",
    )(scalars, *halves, *sums, *operands)


def finish_kernel(final, *refs):
    scalars, halves, before, (hessian, tile, rows, across, *scratch) = (
        refs[0], refs[1:3], refs[3], refs[6:]
    )
    staging, sums, left, right, sent = scratch
    at = rows.shape[0] - CAP
    copies = []

    def write(source, target):
        copies.append(pltpu.make_async_copy(source, target, sent.at[len(copies)]))
        copies[-1].start()

    update = take_in(scalars, halves, at, rows, across, left, right)
    sums[...] = (before[...] + update) * final
    write(sums, tile.at[0])
    height = staging.shape[1]
    for m in range(SPLITS):
        span = slice(m * height, (m + 1) * height)
        for n in range(0, rows.shape[1], STEP):
            staging[m, :, n : n + STEP] = (
                jnp.dot(across[span, :], rows[:, n : n + STEP], preferred_element_type=F32)
                * INVERSE
            )
        write(staging.at[m], hessian.at[span, :])
    for copy in copies:
        copy.wait()


def finish(scalars, halves, before, operands, final):
    edge = before.shape[0]
    rows, across = operands
    slab, width = across.shape[0], rows.shape[1]
    return pl.pallas_call(
        functools.partial(finish_kernel, final),
        out_shape=[
            jax.ShapeDtypeStruct((slab, width), F32),
            jax.ShapeDtypeStruct((1, edge, edge), F32),
            jax.ShapeDtypeStruct(rows.shape, BF16),
            jax.ShapeDtypeStruct(across.shape, BF16),
        ],
        in_specs=[SMEM] + [VMEM] * 5,
        out_specs=[ANY, ANY, VMEM, VMEM],
        scratch_shapes=[
            pltpu.VMEM((SPLITS, slab // SPLITS, width), F32),
            pltpu.VMEM((edge, edge), F32),
            pltpu.VMEM((LANES, edge), BF16),
            pltpu.VMEM((LANES, edge), BF16),
            pltpu.SemaphoreType.DMA((SPLITS + 1,)),
        ],
        input_output_aliases={4: 2, 5: 3},
        cost_estimate=SMALL,
        compiler_params=params(38),
        name="finish",
    )(scalars, *halves, before, rows, across)[:2]


def ring_of(chips):
    return list(range(0, chips, 2)) + list(range(chips - 1, 0, -2))


def on_device(tokens, route_ids, route_weights):
    devices = lax.axis_size("tok")
    position = lax.axis_index("tok")
    tok_rows, width = tokens.shape
    grid = math.isqrt(devices)
    edge = width // grid
    group = devices // EXP
    slab = width // group
    chips = devices // CORES
    ring = ring_of(chips)
    ahead = [
        (ring[i] * CORES + c, ring[(i + 1) % chips] * CORES + c)
        for i in range(chips)
        for c in range(CORES)
    ]
    streams = [ahead, [(b, a) for a, b in ahead]]
    pair = [(d, d ^ 1) for d in range(devices)]
    column = position % grid
    scalars = jnp.stack(
        [
            position // group,
            position // grid,
            column,
            column + 1 - 2 * (column % 2),
            position % group,
        ]
    ).astype(jnp.int32)

    def swap(array):
        return lax.ppermute(array, "tok", pair)

    def advance(held):
        return [lax.ppermute(array, "tok", stream) for array, stream in zip(held, streams)]

    rounds = chips // 2
    total = 4 * CAP * rounds

    pieces = [make_message(tokens, route_ids, route_weights)]
    operands, sums = [], []
    half = tok_rows * (width // LANES // 2)
    for step in range(1, rounds + 1):
        held = pieces * CORES if step == 1 else pieces
        if step == rounds:
            held = [held[0][: half + TABLE], held[1][half:]]
        moved = advance(held)
        tile, columns, packed = absorb(scalars, pieces, sums, edge)
        sums = [tile] + [swap(array) for array in columns]
        at = 4 * CAP * (step - 2) if step > 1 else total - 4 * CAP
        packs = list(packed) + [swap(array) for array in packed]
        operands = prepare(scalars, packs, at, operands, total, slab)
        if step < rounds:
            ahead_of, operands, sums = lax.optimization_barrier((moved[0], operands, sums))
            back_of, operands, sums = lax.optimization_barrier((moved[1], operands, sums))
            moved = [ahead_of, back_of]
        pieces = moved
    pieces, operands, sums = lax.optimization_barrier((pieces, operands, sums))
    others = [swap(piece) for piece in pieces]
    tile, *operands = take_own(scalars, pieces, sums, operands)
    return tuple(finish(scalars, others, tile, operands, 1.0 / (devices * tok_rows)))


def solution(mesh):
    in_specs = (P(("grp", "tok"), None), P(("grp", "tok"), None), P(("grp", "tok"), None))
    out_specs = (P(("grp", "tok"), None), P(("grp", "tok"), None, None))
    return jax.shard_map(
        on_device, mesh=mesh, in_specs=in_specs, out_specs=out_specs, check_vma=False
    )
```

```python
import functools
import math

import jax
import jax.numpy as jnp
from jax import lax
from jax.experimental import pallas as pl
from jax.experimental.pallas import tpu as pltpu
from jax.sharding import PartitionSpec as P

EXP = 8
CAP = 32
CORES = 2
LANES = 128
TABLE = 32
STEP = 512
SPLITS = 7
VMEM = pl.BlockSpec(memory_space=pltpu.VMEM)
SMEM = pl.BlockSpec(memory_space=pltpu.SMEM)
ANY = pl.BlockSpec(memory_space=pl.ANY)
F32 = jnp.float32
BF16 = jnp.bfloat16
ROWS_WITH_ROWS = (((0,), (0,)), ((), ()))
INVERSE = 1.0 / (16.0 * CAP)
SMALL = pl.CostEstimate(flops=1, bytes_accessed=1, transcendentals=0)


def params(mib):
    return pltpu.CompilerParams(vmem_limit_bytes=mib * 2**20)


def message_kernel(tokens, weights, out):
    rows, width = tokens.shape
    for b in range(width // LANES):
        out[b * rows : (b + 1) * rows, :] = tokens[:, b * LANES : (b + 1) * LANES]
    row_at = lax.broadcasted_iota(jnp.int32, (TABLE, rows), 0)
    roots = jnp.zeros((TABLE, rows), F32)
    for e in range(EXP):
        roots = jnp.where(row_at % EXP == e, jnp.sqrt(weights[e : e + 1, :]), roots)
    high = roots.astype(BF16).astype(F32)
    middle = (roots - high).astype(BF16).astype(F32)
    low = roots - high - middle
    terms = jnp.where(row_at < EXP, high, jnp.where(row_at < 2 * EXP, middle, low))
    out[rows * width // LANES :, :] = jnp.where(row_at < 3 * EXP, terms, 0.0).astype(BF16)


def make_message(tokens, ids, weights):
    rows, width = tokens.shape
    hits = ids[:, :, None] == jnp.arange(EXP, dtype=jnp.int32)[None, None, :]
    table = jnp.sum(jnp.where(hits, weights[:, :, None], 0.0), axis=1)
    return pl.pallas_call(
        message_kernel,
        out_shape=jax.ShapeDtypeStruct((rows * width // LANES + TABLE, LANES), BF16),
        in_specs=[VMEM] * 2,
        out_specs=VMEM,
        cost_estimate=SMALL,
        compiler_params=params(8),
        name="make_message",
    )(tokens, table.T)


def block_of(piece, index):
    for array in piece:
        inside = array.shape[0] // LANES
        if index < inside:
            return array.at[index * LANES : (index + 1) * LANES]
        index -= inside


def choose(expert, piece):
    last = piece[-1]
    table = last[last.shape[0] - TABLE :, :].astype(F32)
    row_at = lax.broadcasted_iota(jnp.int32, (TABLE, LANES), 0)
    ours = jnp.logical_and(row_at % EXP == expert, row_at < 3 * EXP)
    root = jnp.sum(jnp.where(ours, table, 0.0), axis=0, keepdims=True)
    root = jnp.broadcast_to(root, (CAP, LANES))
    member = root > 0.0
    from_at = lax.broadcasted_iota(jnp.int32, (LANES, LANES), 0)
    to_at = lax.broadcasted_iota(jnp.int32, (LANES, LANES), 1)
    upto = (from_at <= to_at).astype(F32).astype(BF16)
    counted = jnp.dot(member.astype(F32).astype(BF16), upto, preferred_element_type=F32)
    place = counted.astype(jnp.int32) - 1
    slot_at = lax.broadcasted_iota(jnp.int32, (CAP, LANES), 0)
    select = jnp.logical_and(member, place == slot_at)
    scale = jnp.sum(jnp.where(select, root, 0.0), axis=1, keepdims=True)
    return select.astype(F32).astype(BF16), scale


def pack(expert, piece):
    select, scale = choose(expert, piece)
    blocks = sum(array.shape[0] // LANES for array in piece)
    groups = []
    for b in range(0, blocks, 4):
        some = jnp.concatenate(
            [block_of(piece, k)[...] for k in range(b, min(b + 4, blocks))], axis=1
        )
        picked = jnp.dot(select, some, preferred_element_type=F32)
        groups.append((picked * scale).astype(BF16))
    return jnp.concatenate(groups, axis=1)


def fetch_tile(index, pieces, scratch):
    edge = scratch.shape[1]
    blocks = sum(array.shape[0] // LANES for array in pieces[0])
    for b in range(blocks * LANES // edge):

        @pl.when(index == b)
        def _(b=b):
            for k, piece in enumerate(pieces):
                at = b * edge
                while at < (b + 1) * edge:
                    first = at % LANES
                    count = min(LANES - first, (b + 1) * edge - at)
                    scratch[k * LANES : (k + 1) * LANES, at - b * edge : at - b * edge + count] = (
                        block_of(piece, at // LANES)[:, first : first + count]
                    )
                    at += count


def product(left, right):
    return lax.dot_general(left[...], right[...], ROWS_WITH_ROWS, preferred_element_type=F32)


def absorb_kernel(count, started, *refs):
    scalars, refs = refs[0], refs[1:]
    pieces, refs = [[ref] for ref in refs[:count]], refs[count:]
    before, refs = refs[: 3 * started], refs[3 * started :]
    tile, left, theirs, *packs, mine = refs
    for slot, which in enumerate((left, mine, theirs), start=1):
        fetch_tile(scalars[slot], pieces, which)
    update = product(left, mine)
    if started:
        update = before[0][...] + update + product(before[1], before[2])
    tile[...] = update
    for piece, packed in zip(pieces, packs):
        packed[...] = pack(scalars[0], piece)


def absorb(scalars, pieces, before, edge):
    rows, width = LANES, pieces[0].shape[0] - TABLE
    count = len(pieces)
    columns = jax.ShapeDtypeStruct((count * rows, edge), BF16)
    out = pl.pallas_call(
        functools.partial(absorb_kernel, count, bool(before)),
        out_shape=[jax.ShapeDtypeStruct((edge, edge), F32), columns, columns]
        + [jax.ShapeDtypeStruct((CAP, width), BF16)] * count,
        in_specs=[SMEM] + [VMEM] * (count + len(before)),
        out_specs=[VMEM] * (3 + count),
        scratch_shapes=[pltpu.VMEM((count * rows, edge), BF16)],
        cost_estimate=SMALL,
        input_output_aliases={1 + count: 0} if before else {},
        compiler_params=params(14),
        name="absorb",
    )(scalars, *pieces, *before)
    return out[0], out[1:3], out[3:]


def place_rows(slab_at, packed, at, rows, across):
    count, width = packed.shape
    slab = across.shape[0]
    rows[at : at + count, :] = packed
    for s in range(width // slab):

        @pl.when(slab_at == s)
        def _():
            across[:, at : at + count] = packed[:, s * slab : (s + 1) * slab].T


def prepare_kernel(count, at, *refs):
    scalars, packs, (rows, across) = refs[0], refs[1 : 1 + count], refs[-2:]
    packed = jnp.concatenate([array[...] for array in packs], axis=0)
    place_rows(scalars[4], packed, at, rows, across)


def prepare(scalars, packs, at, operands, total, slab):
    width = packs[0].shape[1]
    return pl.pallas_call(
        functools.partial(prepare_kernel, len(packs), at),
        out_shape=[
            jax.ShapeDtypeStruct((total, width), BF16),
            jax.ShapeDtypeStruct((slab, total), BF16),
        ],
        in_specs=[SMEM] + [VMEM] * (len(packs) + len(operands)),
        out_specs=[VMEM] * 2,
        input_output_aliases={1 + len(packs) + k: k for k in range(len(operands))},
        cost_estimate=SMALL,
        compiler_params=params(12),
        name="prepare_rows",
    )(scalars, *packs, *operands)


def take_in(scalars, halves, at, rows, across, left, right):
    place_rows(scalars[4], pack(scalars[0], halves), at, rows, across)
    fetch_tile(scalars[1], [halves], left)
    fetch_tile(scalars[2], [halves], right)
    return product(left, right)


def settle_kernel(before, left, right, tile):
    tile[...] = before[...] + product(left, right)


def settle(sums):
    return pl.pallas_call(
        settle_kernel,
        out_shape=jax.ShapeDtypeStruct(sums[0].shape, F32),
        in_specs=[VMEM] * 3,
        out_specs=VMEM,
        input_output_aliases={0: 0},
        cost_estimate=SMALL,
        compiler_params=params(14),
        name="settle",
    )(*sums)


def take_own_kernel(*refs):
    scalars, halves, before, refs = refs[0], refs[1:3], refs[3], refs[6:]
    tile, rows, across, left, right = refs
    at = rows.shape[0] - 2 * CAP
    tile[...] = before[...] + take_in(scalars, halves, at, rows, across, left, right)


def take_own(scalars, halves, tile, operands):
    edge = tile.shape[0]
    return pl.pallas_call(
        take_own_kernel,
        out_shape=[jax.ShapeDtypeStruct(a.shape, a.dtype) for a in (tile, *operands)],
        in_specs=[SMEM] + [VMEM] * 5,
        out_specs=[VMEM] * 3,
        scratch_shapes=[pltpu.VMEM((LANES, edge), BF16)] * 2,
        input_output_aliases={3: 0, 4: 1, 5: 2},
        cost_estimate=SMALL,
        compiler_params=params(14),
        name="take_own",
    )(scalars, *halves, tile, *operands)


def finish_kernel(final, *refs):
    scalars, halves, before, (hessian, tile, rows, across, *scratch) = (
        refs[0], refs[1:3], refs[3], refs[6:]
    )
    staging, sums, left, right, sent = scratch
    at = rows.shape[0] - CAP
    copies = []

    def write(source, target):
        copies.append(pltpu.make_async_copy(source, target, sent.at[len(copies)]))
        copies[-1].start()

    update = take_in(scalars, halves, at, rows, across, left, right)
    sums[...] = (before[...] + update) * final
    write(sums, tile.at[0])
    height = staging.shape[1]
    for m in range(SPLITS):
        span = slice(m * height, (m + 1) * height)
        for n in range(0, rows.shape[1], STEP):
            staging[m, :, n : n + STEP] = (
                jnp.dot(across[span, :], rows[:, n : n + STEP], preferred_element_type=F32)
                * INVERSE
            )
        write(staging.at[m], hessian.at[span, :])
    for copy in copies:
        copy.wait()


def finish(scalars, halves, before, operands, final):
    edge = before.shape[0]
    rows, across = operands
    slab, width = across.shape[0], rows.shape[1]
    return pl.pallas_call(
        functools.partial(finish_kernel, final),
        out_shape=[
            jax.ShapeDtypeStruct((slab, width), F32),
            jax.ShapeDtypeStruct((1, edge, edge), F32),
            jax.ShapeDtypeStruct(rows.shape, BF16),
            jax.ShapeDtypeStruct(across.shape, BF16),
        ],
        in_specs=[SMEM] + [VMEM] * 5,
        out_specs=[ANY, ANY, VMEM, VMEM],
        scratch_shapes=[
            pltpu.VMEM((SPLITS, slab // SPLITS, width), F32),
            pltpu.VMEM((edge, edge), F32),
            pltpu.VMEM((LANES, edge), BF16),
            pltpu.VMEM((LANES, edge), BF16),
            pltpu.SemaphoreType.DMA((SPLITS + 1,)),
        ],
        input_output_aliases={4: 2, 5: 3},
        cost_estimate=SMALL,
        compiler_params=params(38),
        name="finish",
    )(scalars, *halves, before, rows, across)[:2]


def ring_of(chips):
    return list(range(0, chips, 2)) + list(range(chips - 1, 0, -2))


def on_device(tokens, route_ids, route_weights):
    devices = lax.axis_size("tok")
    position = lax.axis_index("tok")
    tok_rows, width = tokens.shape
    grid = math.isqrt(devices)
    edge = width // grid
    group = devices // EXP
    slab = width // group
    chips = devices // CORES
    ring = ring_of(chips)
    ahead = [
        (ring[i] * CORES + c, ring[(i + 1) % chips] * CORES + c)
        for i in range(chips)
        for c in range(CORES)
    ]
    streams = [ahead, [(b, a) for a, b in ahead]]
    pair = [(d, d ^ 1) for d in range(devices)]
    column = position % grid
    scalars = jnp.stack(
        [
            position // group,
            position // grid,
            column,
            column + 1 - 2 * (column % 2),
            position % group,
        ]
    ).astype(jnp.int32)

    def swap(array):
        return lax.ppermute(array, "tok", pair)

    def advance(held):
        return [lax.ppermute(array, "tok", stream) for array, stream in zip(held, streams)]

    rounds = chips // 2
    total = 4 * CAP * rounds

    pieces = [make_message(tokens, route_ids, route_weights)]
    operands, sums = [], []
    half = tok_rows * (width // LANES // 2)
    for step in range(1, rounds + 1):
        held = pieces * CORES if step == 1 else pieces
        if step == rounds:
            held = [held[0][: half + TABLE], held[1][half:]]
        moved = advance(held)
        tile, columns, packed = absorb(scalars, pieces, sums, edge)
        sums = [tile] + [swap(array) for array in columns]
        at = 4 * CAP * (step - 2) if step > 1 else total - 4 * CAP
        packs = list(packed) + [swap(array) for array in packed]
        operands = prepare(scalars, packs, at, operands, total, slab)
        if step < rounds:
            ahead_of, operands, sums = lax.optimization_barrier((moved[0], operands, sums))
            back_of, operands, sums = lax.optimization_barrier((moved[1], operands, sums))
            moved = [ahead_of, back_of]
        pieces = moved
    pieces, operands, tile = lax.optimization_barrier((pieces, operands, settle(sums)))
    others = [swap(piece) for piece in pieces]
    tile, *operands = take_own(scalars, pieces, tile, operands)
    return tuple(finish(scalars, others, tile, operands, 1.0 / (devices * tok_rows)))


def solution(mesh):
    in_specs = (P(("grp", "tok"), None), P(("grp", "tok"), None), P(("grp", "tok"), None))
    out_specs = (P(("grp", "tok"), None), P(("grp", "tok"), None, None))
    return jax.shard_map(
        on_device, mesh=mesh, in_specs=in_specs, out_specs=out_specs, check_vma=False
    )
```

```python
import functools
import math

import jax
import jax.numpy as jnp
from jax import lax
from jax.experimental import pallas as pl
from jax.experimental.pallas import tpu as pltpu
from jax.sharding import PartitionSpec as P

EXP = 8
CAP = 32
CORES = 2
LANES = 128
TABLE = 32
STEP = 512
SPLITS = 7
VMEM = pl.BlockSpec(memory_space=pltpu.VMEM)
SMEM = pl.BlockSpec(memory_space=pltpu.SMEM)
ANY = pl.BlockSpec(memory_space=pl.ANY)
F32 = jnp.float32
BF16 = jnp.bfloat16
ROWS_WITH_ROWS = (((0,), (0,)), ((), ()))
INVERSE = 1.0 / (16.0 * CAP)
SMALL = pl.CostEstimate(flops=1, bytes_accessed=1, transcendentals=0)


def params(mib):
    return pltpu.CompilerParams(vmem_limit_bytes=mib * 2**20)


def message_kernel(tokens, weights, out):
    rows, width = tokens.shape
    for b in range(width // LANES):
        out[b * rows : (b + 1) * rows, :] = tokens[:, b * LANES : (b + 1) * LANES]
    row_at = lax.broadcasted_iota(jnp.int32, (TABLE, rows), 0)
    roots = jnp.zeros((TABLE, rows), F32)
    for e in range(EXP):
        roots = jnp.where(row_at % EXP == e, jnp.sqrt(weights[e : e + 1, :]), roots)
    high = roots.astype(BF16).astype(F32)
    middle = (roots - high).astype(BF16).astype(F32)
    low = roots - high - middle
    terms = jnp.where(row_at < EXP, high, jnp.where(row_at < 2 * EXP, middle, low))
    out[rows * width // LANES :, :] = jnp.where(row_at < 3 * EXP, terms, 0.0).astype(BF16)


def make_message(tokens, ids, weights):
    rows, width = tokens.shape
    hits = ids[:, :, None] == jnp.arange(EXP, dtype=jnp.int32)[None, None, :]
    table = jnp.sum(jnp.where(hits, weights[:, :, None], 0.0), axis=1)
    return pl.pallas_call(
        message_kernel,
        out_shape=jax.ShapeDtypeStruct((rows * width // LANES + TABLE, LANES), BF16),
        in_specs=[VMEM] * 2,
        out_specs=VMEM,
        cost_estimate=SMALL,
        compiler_params=params(8),
        name="make_message",
    )(tokens, table.T)


def block_of(piece, index):
    for array in piece:
        inside = array.shape[0] // LANES
        if index < inside:
            return array.at[index * LANES : (index + 1) * LANES]
        index -= inside


def choose(expert, piece):
    last = piece[-1]
    table = last[last.shape[0] - TABLE :, :].astype(F32)
    row_at = lax.broadcasted_iota(jnp.int32, (TABLE, LANES), 0)
    ours = jnp.logical_and(row_at % EXP == expert, row_at < 3 * EXP)
    root = jnp.sum(jnp.where(ours, table, 0.0), axis=0, keepdims=True)
    root = jnp.broadcast_to(root, (CAP, LANES))
    member = root > 0.0
    from_at = lax.broadcasted_iota(jnp.int32, (LANES, LANES), 0)
    to_at = lax.broadcasted_iota(jnp.int32, (LANES, LANES), 1)
    upto = (from_at <= to_at).astype(F32).astype(BF16)
    counted = jnp.dot(member.astype(F32).astype(BF16), upto, preferred_element_type=F32)
    place = counted.astype(jnp.int32) - 1
    slot_at = lax.broadcasted_iota(jnp.int32, (CAP, LANES), 0)
    select = jnp.logical_and(member, place == slot_at)
    scale = jnp.sum(jnp.where(select, root, 0.0), axis=1, keepdims=True)
    return select.astype(F32).astype(BF16), scale


def pack(expert, piece):
    select, scale = choose(expert, piece)
    blocks = sum(array.shape[0] // LANES for array in piece)
    groups = []
    for b in range(0, blocks, 4):
        some = jnp.concatenate(
            [block_of(piece, k)[...] for k in range(b, min(b + 4, blocks))], axis=1
        )
        picked = jnp.dot(select, some, preferred_element_type=F32)
        groups.append((picked * scale).astype(BF16))
    return jnp.concatenate(groups, axis=1)


def fetch_tile(index, pieces, scratch):
    edge = scratch.shape[1]
    blocks = sum(array.shape[0] // LANES for array in pieces[0])
    for b in range(blocks * LANES // edge):

        @pl.when(index == b)
        def _(b=b):
            for k, piece in enumerate(pieces):
                at = b * edge
                while at < (b + 1) * edge:
                    first = at % LANES
                    count = min(LANES - first, (b + 1) * edge - at)
                    scratch[k * LANES : (k + 1) * LANES, at - b * edge : at - b * edge + count] = (
                        block_of(piece, at // LANES)[:, first : first + count]
                    )
                    at += count


def product(left, right):
    return lax.dot_general(left[...], right[...], ROWS_WITH_ROWS, preferred_element_type=F32)


def absorb_kernel(count, started, *refs):
    scalars, refs = refs[0], refs[1:]
    pieces, refs = [[ref] for ref in refs[:count]], refs[count:]
    before, refs = refs[: 3 * started], refs[3 * started :]
    tile, left, theirs, *packs, mine = refs
    for slot, which in enumerate((left, mine, theirs), start=1):
        fetch_tile(scalars[slot], pieces, which)
    update = product(left, mine)
    if started:
        update = before[0][...] + update + product(before[1], before[2])
    tile[...] = update
    for piece, packed in zip(pieces, packs):
        packed[...] = pack(scalars[0], piece)


def absorb(scalars, pieces, before, edge):
    rows, width = LANES, pieces[0].shape[0] - TABLE
    count = len(pieces)
    columns = jax.ShapeDtypeStruct((count * rows, edge), BF16)
    out = pl.pallas_call(
        functools.partial(absorb_kernel, count, bool(before)),
        out_shape=[jax.ShapeDtypeStruct((edge, edge), F32), columns, columns]
        + [jax.ShapeDtypeStruct((CAP, width), BF16)] * count,
        in_specs=[SMEM] + [VMEM] * (count + len(before)),
        out_specs=[VMEM] * (3 + count),
        scratch_shapes=[pltpu.VMEM((count * rows, edge), BF16)],
        cost_estimate=SMALL,
        input_output_aliases={1 + count: 0} if before else {},
        compiler_params=params(14),
        name="absorb",
    )(scalars, *pieces, *before)
    return out[0], out[1:3], out[3:]


def place_rows(slab_at, packed, at, rows, across):
    count, width = packed.shape
    slab = across.shape[0]
    rows[at : at + count, :] = packed
    for s in range(width // slab):

        @pl.when(slab_at == s)
        def _():
            across[:, at : at + count] = packed[:, s * slab : (s + 1) * slab].T


def prepare_kernel(count, at, *refs):
    scalars, packs, (rows, across) = refs[0], refs[1 : 1 + count], refs[-2:]
    packed = jnp.concatenate([array[...] for array in packs], axis=0)
    place_rows(scalars[4], packed, at, rows, across)


def prepare(scalars, packs, at, operands, total, slab):
    width = packs[0].shape[1]
    return pl.pallas_call(
        functools.partial(prepare_kernel, len(packs), at),
        out_shape=[
            jax.ShapeDtypeStruct((total, width), BF16),
            jax.ShapeDtypeStruct((slab, total), BF16),
        ],
        in_specs=[SMEM] + [VMEM] * (len(packs) + len(operands)),
        out_specs=[VMEM] * 2,
        input_output_aliases={1 + len(packs) + k: k for k in range(len(operands))},
        cost_estimate=SMALL,
        compiler_params=params(12),
        name="prepare_rows",
    )(scalars, *packs, *operands)


def take_in(scalars, halves, at, rows, across, left, right):
    place_rows(scalars[4], pack(scalars[0], halves), at, rows, across)
    fetch_tile(scalars[1], [halves], left)
    fetch_tile(scalars[2], [halves], right)
    return product(left, right)


def settle_kernel(before, left, right, tile):
    tile[...] = before[...] + product(left, right)


def settle(sums):
    return pl.pallas_call(
        settle_kernel,
        out_shape=jax.ShapeDtypeStruct(sums[0].shape, F32),
        in_specs=[VMEM] * 3,
        out_specs=VMEM,
        input_output_aliases={0: 0},
        cost_estimate=SMALL,
        compiler_params=params(14),
        name="settle",
    )(*sums)


def take_own_kernel(*refs):
    scalars, halves, before, refs = refs[0], refs[1:3], refs[3], refs[6:]
    tile, rows, across, left, right = refs
    at = rows.shape[0] - 2 * CAP
    tile[...] = before[...] + take_in(scalars, halves, at, rows, across, left, right)


def take_own(scalars, halves, tile, operands):
    edge = tile.shape[0]
    return pl.pallas_call(
        take_own_kernel,
        out_shape=[jax.ShapeDtypeStruct(a.shape, a.dtype) for a in (tile, *operands)],
        in_specs=[SMEM] + [VMEM] * 5,
        out_specs=[VMEM] * 3,
        scratch_shapes=[pltpu.VMEM((LANES, edge), BF16)] * 2,
        input_output_aliases={3: 0, 4: 1, 5: 2},
        cost_estimate=SMALL,
        compiler_params=params(14),
        name="take_own",
    )(scalars, *halves, tile, *operands)


def finish_kernel(final, *refs):
    scalars, halves, before, (hessian, tile, rows, across, *scratch) = (
        refs[0], refs[1:3], refs[3], refs[6:]
    )
    staging, sums, left, right, sent = scratch
    at = rows.shape[0] - CAP
    copies = []

    def write(source, target):
        copies.append(pltpu.make_async_copy(source, target, sent.at[len(copies)]))
        copies[-1].start(priority=len(copies) % 2)

    update = take_in(scalars, halves, at, rows, across, left, right)
    sums[...] = (before[...] + update) * final
    write(sums, tile.at[0])
    height = staging.shape[1]
    for m in range(SPLITS):
        span = slice(m * height, (m + 1) * height)
        for n in range(0, rows.shape[1], STEP):
            staging[m, :, n : n + STEP] = (
                jnp.dot(across[span, :], rows[:, n : n + STEP], preferred_element_type=F32)
                * INVERSE
            )
        write(staging.at[m], hessian.at[span, :])
    for copy in copies:
        copy.wait()


def finish(scalars, halves, before, operands, final):
    edge = before.shape[0]
    rows, across = operands
    slab, width = across.shape[0], rows.shape[1]
    return pl.pallas_call(
        functools.partial(finish_kernel, final),
        out_shape=[
            jax.ShapeDtypeStruct((slab, width), F32),
            jax.ShapeDtypeStruct((1, edge, edge), F32),
            jax.ShapeDtypeStruct(rows.shape, BF16),
            jax.ShapeDtypeStruct(across.shape, BF16),
        ],
        in_specs=[SMEM] + [VMEM] * 5,
        out_specs=[ANY, ANY, VMEM, VMEM],
        scratch_shapes=[
            pltpu.VMEM((SPLITS, slab // SPLITS, width), F32),
            pltpu.VMEM((edge, edge), F32),
            pltpu.VMEM((LANES, edge), BF16),
            pltpu.VMEM((LANES, edge), BF16),
            pltpu.SemaphoreType.DMA((SPLITS + 1,)),
        ],
        input_output_aliases={4: 2, 5: 3},
        cost_estimate=SMALL,
        compiler_params=params(38),
        name="finish",
    )(scalars, *halves, before, rows, across)[:2]


def ring_of(chips):
    return list(range(0, chips, 2)) + list(range(chips - 1, 0, -2))


def on_device(tokens, route_ids, route_weights):
    devices = lax.axis_size("tok")
    position = lax.axis_index("tok")
    tok_rows, width = tokens.shape
    grid = math.isqrt(devices)
    edge = width // grid
    group = devices // EXP
    slab = width // group
    chips = devices // CORES
    ring = ring_of(chips)
    ahead = [
        (ring[i] * CORES + c, ring[(i + 1) % chips] * CORES + c)
        for i in range(chips)
        for c in range(CORES)
    ]
    streams = [ahead, [(b, a) for a, b in ahead]]
    pair = [(d, d ^ 1) for d in range(devices)]
    column = position % grid
    scalars = jnp.stack(
        [
            position // group,
            position // grid,
            column,
            column + 1 - 2 * (column % 2),
            position % group,
        ]
    ).astype(jnp.int32)

    def swap(array):
        return lax.ppermute(array, "tok", pair)

    def advance(held):
        return [lax.ppermute(array, "tok", stream) for array, stream in zip(held, streams)]

    rounds = chips // 2
    total = 4 * CAP * rounds

    pieces = [make_message(tokens, route_ids, route_weights)]
    operands, sums = [], []
    half = tok_rows * (width // LANES // 2)
    for step in range(1, rounds + 1):
        held = pieces * CORES if step == 1 else pieces
        if step == rounds:
            held = [held[0][: half + TABLE], held[1][half:]]
        moved = advance(held)
        tile, columns, packed = absorb(scalars, pieces, sums, edge)
        sums = [tile] + [swap(array) for array in columns]
        at = 4 * CAP * (step - 2) if step > 1 else total - 4 * CAP
        packs = list(packed) + [swap(array) for array in packed]
        operands = prepare(scalars, packs, at, operands, total, slab)
        if step < rounds:
            ahead_of, operands, sums = lax.optimization_barrier((moved[0], operands, sums))
            back_of, operands, sums = lax.optimization_barrier((moved[1], operands, sums))
            moved = [ahead_of, back_of]
        pieces = moved
    pieces, operands, tile = lax.optimization_barrier((pieces, operands, settle(sums)))
    others = [swap(piece) for piece in pieces]
    tile, *operands = take_own(scalars, pieces, tile, operands)
    return tuple(finish(scalars, others, tile, operands, 1.0 / (devices * tok_rows)))


def solution(mesh):
    in_specs = (P(("grp", "tok"), None), P(("grp", "tok"), None), P(("grp", "tok"), None))
    out_specs = (P(("grp", "tok"), None), P(("grp", "tok"), None, None))
    return jax.shard_map(
        on_device, mesh=mesh, in_specs=in_specs, out_specs=out_specs, check_vma=False
    )
```

```python
import functools
import math

import jax
import jax.numpy as jnp
from jax import lax
from jax.experimental import pallas as pl
from jax.experimental.pallas import tpu as pltpu
from jax.sharding import PartitionSpec as P

EXP = 8
CAP = 32
CORES = 2
LANES = 128
TABLE = 32
SPLITS = 7
VMEM = pl.BlockSpec(memory_space=pltpu.VMEM)
SMEM = pl.BlockSpec(memory_space=pltpu.SMEM)
ANY = pl.BlockSpec(memory_space=pl.ANY)
F32 = jnp.float32
BF16 = jnp.bfloat16
ROWS_WITH_ROWS = (((0,), (0,)), ((), ()))
INVERSE = 1.0 / (16.0 * CAP)
SMALL = pl.CostEstimate(flops=1, bytes_accessed=1, transcendentals=0)


def params(mib):
    return pltpu.CompilerParams(vmem_limit_bytes=mib * 2**20)


def message_kernel(tokens, weights, out):
    rows, width = tokens.shape
    for b in range(width // LANES):
        out[b * rows : (b + 1) * rows, :] = tokens[:, b * LANES : (b + 1) * LANES]
    row_at = lax.broadcasted_iota(jnp.int32, (TABLE, rows), 0)
    roots = jnp.zeros((TABLE, rows), F32)
    for e in range(EXP):
        roots = jnp.where(row_at % EXP == e, jnp.sqrt(weights[e : e + 1, :]), roots)
    high = roots.astype(BF16).astype(F32)
    middle = (roots - high).astype(BF16).astype(F32)
    low = roots - high - middle
    terms = jnp.where(row_at < EXP, high, jnp.where(row_at < 2 * EXP, middle, low))
    out[rows * width // LANES :, :] = jnp.where(row_at < 3 * EXP, terms, 0.0).astype(BF16)


def make_message(tokens, ids, weights):
    rows, width = tokens.shape
    hits = ids[:, :, None] == jnp.arange(EXP, dtype=jnp.int32)[None, None, :]
    table = jnp.sum(jnp.where(hits, weights[:, :, None], 0.0), axis=1)
    return pl.pallas_call(
        message_kernel,
        out_shape=jax.ShapeDtypeStruct((rows * width // LANES + TABLE, LANES), BF16),
        in_specs=[VMEM] * 2,
        out_specs=VMEM,
        cost_estimate=SMALL,
        compiler_params=params(8),
        name="make_message",
    )(tokens, table.T)


def block_of(piece, index):
    for array in piece:
        inside = array.shape[0] // LANES
        if index < inside:
            return array.at[index * LANES : (index + 1) * LANES]
        index -= inside


def choose(expert, piece):
    last = piece[-1]
    table = last[last.shape[0] - TABLE :, :].astype(F32)
    row_at = lax.broadcasted_iota(jnp.int32, (TABLE, LANES), 0)
    ours = jnp.logical_and(row_at % EXP == expert, row_at < 3 * EXP)
    root = jnp.sum(jnp.where(ours, table, 0.0), axis=0, keepdims=True)
    root = jnp.broadcast_to(root, (CAP, LANES))
    member = root > 0.0
    from_at = lax.broadcasted_iota(jnp.int32, (LANES, LANES), 0)
    to_at = lax.broadcasted_iota(jnp.int32, (LANES, LANES), 1)
    upto = (from_at <= to_at).astype(F32).astype(BF16)
    counted = jnp.dot(member.astype(F32).astype(BF16), upto, preferred_element_type=F32)
    place = counted.astype(jnp.int32) - 1
    slot_at = lax.broadcasted_iota(jnp.int32, (CAP, LANES), 0)
    select = jnp.logical_and(member, place == slot_at)
    scale = jnp.sum(jnp.where(select, root, 0.0), axis=1, keepdims=True)
    return select.astype(F32).astype(BF16), scale


def pack(expert, piece):
    select, scale = choose(expert, piece)
    blocks = sum(array.shape[0] // LANES for array in piece)
    groups = []
    for b in range(0, blocks, 4):
        some = jnp.concatenate(
            [block_of(piece, k)[...] for k in range(b, min(b + 4, blocks))], axis=1
        )
        picked = jnp.dot(select, some, preferred_element_type=F32)
        groups.append((picked * scale).astype(BF16))
    return jnp.concatenate(groups, axis=1)


def fetch_tile(index, pieces, scratch):
    edge = scratch.shape[1]
    blocks = sum(array.shape[0] // LANES for array in pieces[0])
    for b in range(blocks * LANES // edge):

        @pl.when(index == b)
        def _(b=b):
            for k, piece in enumerate(pieces):
                at = b * edge
                while at < (b + 1) * edge:
                    first = at % LANES
                    count = min(LANES - first, (b + 1) * edge - at)
                    scratch[k * LANES : (k + 1) * LANES, at - b * edge : at - b * edge + count] = (
                        block_of(piece, at // LANES)[:, first : first + count]
                    )
                    at += count


def product(left, right):
    return lax.dot_general(left[...], right[...], ROWS_WITH_ROWS, preferred_element_type=F32)


def absorb_kernel(count, started, *refs):
    scalars, refs = refs[0], refs[1:]
    pieces, refs = [[ref] for ref in refs[:count]], refs[count:]
    before, refs = refs[: 3 * started], refs[3 * started :]
    tile, left, theirs, *packs, mine = refs
    for slot, which in enumerate((left, mine, theirs), start=1):
        fetch_tile(scalars[slot], pieces, which)
    update = product(left, mine)
    if started:
        update = before[0][...] + update + product(before[1], before[2])
    tile[...] = update
    for piece, packed in zip(pieces, packs):
        packed[...] = pack(scalars[0], piece)


def absorb(scalars, pieces, before, edge):
    rows, width = LANES, pieces[0].shape[0] - TABLE
    count = len(pieces)
    columns = jax.ShapeDtypeStruct((count * rows, edge), BF16)
    out = pl.pallas_call(
        functools.partial(absorb_kernel, count, bool(before)),
        out_shape=[jax.ShapeDtypeStruct((edge, edge), F32), columns, columns]
        + [jax.ShapeDtypeStruct((CAP, width), BF16)] * count,
        in_specs=[SMEM] + [VMEM] * (count + len(before)),
        out_specs=[VMEM] * (3 + count),
        scratch_shapes=[pltpu.VMEM((count * rows, edge), BF16)],
        cost_estimate=SMALL,
        input_output_aliases={1 + count: 0} if before else {},
        compiler_params=params(14),
        name="absorb",
    )(scalars, *pieces, *before)
    return out[0], out[1:3], out[3:]


def place_rows(slab_at, packed, at, rows, across):
    count, width = packed.shape
    slab = across.shape[0]
    rows[at : at + count, :] = packed
    for s in range(width // slab):

        @pl.when(slab_at == s)
        def _():
            turned = packed[:, s * slab : (s + 1) * slab].T
            across[:, at : at + count] = (turned.astype(F32) * INVERSE).astype(BF16)


def prepare_kernel(count, at, *refs):
    scalars, packs, (rows, across) = refs[0], refs[1 : 1 + count], refs[-2:]
    packed = jnp.concatenate([array[...] for array in packs], axis=0)
    place_rows(scalars[4], packed, at, rows, across)


def prepare(scalars, packs, at, operands, total, slab):
    width = packs[0].shape[1]
    return pl.pallas_call(
        functools.partial(prepare_kernel, len(packs), at),
        out_shape=[
            jax.ShapeDtypeStruct((total, width), BF16),
            jax.ShapeDtypeStruct((slab, total), BF16),
        ],
        in_specs=[SMEM] + [VMEM] * (len(packs) + len(operands)),
        out_specs=[VMEM] * 2,
        input_output_aliases={1 + len(packs) + k: k for k in range(len(operands))},
        cost_estimate=SMALL,
        compiler_params=params(12),
        name="prepare_rows",
    )(scalars, *packs, *operands)


def take_in(scalars, halves, at, rows, across, left, right):
    place_rows(scalars[4], pack(scalars[0], halves), at, rows, across)
    fetch_tile(scalars[1], [halves], left)
    fetch_tile(scalars[2], [halves], right)
    return product(left, right)


def settle_kernel(before, left, right, tile):
    tile[...] = before[...] + product(left, right)


def settle(sums):
    return pl.pallas_call(
        settle_kernel,
        out_shape=jax.ShapeDtypeStruct(sums[0].shape, F32),
        in_specs=[VMEM] * 3,
        out_specs=VMEM,
        input_output_aliases={0: 0},
        cost_estimate=SMALL,
        compiler_params=params(14),
        name="settle",
    )(*sums)


def take_own_kernel(*refs):
    scalars, halves, before, refs = refs[0], refs[1:3], refs[3], refs[6:]
    tile, rows, across, left, right = refs
    at = rows.shape[0] - 2 * CAP
    tile[...] = before[...] + take_in(scalars, halves, at, rows, across, left, right)


def take_own(scalars, halves, tile, operands):
    edge = tile.shape[0]
    return pl.pallas_call(
        take_own_kernel,
        out_shape=[jax.ShapeDtypeStruct(a.shape, a.dtype) for a in (tile, *operands)],
        in_specs=[SMEM] + [VMEM] * 5,
        out_specs=[VMEM] * 3,
        scratch_shapes=[pltpu.VMEM((LANES, edge), BF16)] * 2,
        input_output_aliases={3: 0, 4: 1, 5: 2},
        cost_estimate=SMALL,
        compiler_params=params(14),
        name="take_own",
    )(scalars, *halves, tile, *operands)


def finish_kernel(final, *refs):
    scalars, halves, before, (hessian, tile, rows, across, *scratch) = (
        refs[0], refs[1:3], refs[3], refs[6:]
    )
    staging, sums, left, right, sent = scratch
    at = rows.shape[0] - CAP
    copies = []

    def write(source, target):
        copies.append(pltpu.make_async_copy(source, target, sent.at[len(copies)]))
        copies[-1].start()

    update = take_in(scalars, halves, at, rows, across, left, right)
    sums[...] = (before[...] + update) * final
    write(sums, tile.at[0])
    height = staging.shape[1]
    for m in range(SPLITS):
        span = slice(m * height, (m + 1) * height)
        staging[m, :, :] = jnp.dot(across[span, :], rows[...], preferred_element_type=F32)
        write(staging.at[m], hessian.at[span, :])
    for copy in copies:
        copy.wait()


def finish(scalars, halves, before, operands, final):
    edge = before.shape[0]
    rows, across = operands
    slab, width = across.shape[0], rows.shape[1]
    return pl.pallas_call(
        functools.partial(finish_kernel, final),
        out_shape=[
            jax.ShapeDtypeStruct((slab, width), F32),
            jax.ShapeDtypeStruct((1, edge, edge), F32),
            jax.ShapeDtypeStruct(rows.shape, BF16),
            jax.ShapeDtypeStruct(across.shape, BF16),
        ],
        in_specs=[SMEM] + [VMEM] * 5,
        out_specs=[ANY, ANY, VMEM, VMEM],
        scratch_shapes=[
            pltpu.VMEM((SPLITS, slab // SPLITS, width), F32),
            pltpu.VMEM((edge, edge), F32),
            pltpu.VMEM((LANES, edge), BF16),
            pltpu.VMEM((LANES, edge), BF16),
            pltpu.SemaphoreType.DMA((SPLITS + 1,)),
        ],
        input_output_aliases={4: 2, 5: 3},
        cost_estimate=SMALL,
        compiler_params=params(38),
        name="finish",
    )(scalars, *halves, before, rows, across)[:2]


def ring_of(chips):
    return list(range(0, chips, 2)) + list(range(chips - 1, 0, -2))


def on_device(tokens, route_ids, route_weights):
    devices = lax.axis_size("tok")
    position = lax.axis_index("tok")
    tok_rows, width = tokens.shape
    grid = math.isqrt(devices)
    edge = width // grid
    group = devices // EXP
    slab = width // group
    chips = devices // CORES
    ring = ring_of(chips)
    ahead = [
        (ring[i] * CORES + c, ring[(i + 1) % chips] * CORES + c)
        for i in range(chips)
        for c in range(CORES)
    ]
    streams = [ahead, [(b, a) for a, b in ahead]]
    pair = [(d, d ^ 1) for d in range(devices)]
    column = position % grid
    scalars = jnp.stack(
        [
            position // group,
            position // grid,
            column,
            column + 1 - 2 * (column % 2),
            position % group,
        ]
    ).astype(jnp.int32)

    def swap(array):
        return lax.ppermute(array, "tok", pair)

    def advance(held):
        return [lax.ppermute(array, "tok", stream) for array, stream in zip(held, streams)]

    rounds = chips // 2
    total = 4 * CAP * rounds

    pieces = [make_message(tokens, route_ids, route_weights)]
    operands, sums = [], []
    half = tok_rows * (width // LANES // 2)
    for step in range(1, rounds + 1):
        held = pieces * CORES if step == 1 else pieces
        if step == rounds:
            held = [held[0][: half + TABLE], held[1][half:]]
        moved = advance(held)
        tile, columns, packed = absorb(scalars, pieces, sums, edge)
        sums = [tile] + [swap(array) for array in columns]
        at = 4 * CAP * (step - 2) if step > 1 else total - 4 * CAP
        packs = list(packed) + [swap(array) for array in packed]
        operands = prepare(scalars, packs, at, operands, total, slab)
        if step < rounds:
            ahead_of, operands, sums = lax.optimization_barrier((moved[0], operands, sums))
            back_of, operands, sums = lax.optimization_barrier((moved[1], operands, sums))
            moved = [ahead_of, back_of]
        pieces = moved
    pieces, operands, tile = lax.optimization_barrier((pieces, operands, settle(sums)))
    others = [swap(piece) for piece in pieces]
    tile, *operands = take_own(scalars, pieces, tile, operands)
    return tuple(finish(scalars, others, tile, operands, 1.0 / (devices * tok_rows)))


def solution(mesh):
    in_specs = (P(("grp", "tok"), None), P(("grp", "tok"), None), P(("grp", "tok"), None))
    out_specs = (P(("grp", "tok"), None), P(("grp", "tok"), None, None))
    return jax.shard_map(
        on_device, mesh=mesh, in_specs=in_specs, out_specs=out_specs, check_vma=False
    )
```

```python
import functools
import math

import jax
import jax.numpy as jnp
from jax import lax
from jax.experimental import pallas as pl
from jax.experimental.pallas import tpu as pltpu
from jax.sharding import PartitionSpec as P

EXP = 8
CAP = 32
CORES = 2
LANES = 128
TABLE = 32
STEP = 512
SPLITS = 7
VMEM = pl.BlockSpec(memory_space=pltpu.VMEM)
SMEM = pl.BlockSpec(memory_space=pltpu.SMEM)
ANY = pl.BlockSpec(memory_space=pl.ANY)
F32 = jnp.float32
BF16 = jnp.bfloat16
ROWS_WITH_ROWS = (((0,), (0,)), ((), ()))
INVERSE = 1.0 / (16.0 * CAP)
SMALL = pl.CostEstimate(flops=1, bytes_accessed=1, transcendentals=0)


def params(mib):
    return pltpu.CompilerParams(vmem_limit_bytes=mib * 2**20)


def message_kernel(tokens, weights, out):
    rows, width = tokens.shape
    for b in range(width // LANES):
        out[b * rows : (b + 1) * rows, :] = tokens[:, b * LANES : (b + 1) * LANES]
    row_at = lax.broadcasted_iota(jnp.int32, (TABLE, rows), 0)
    roots = jnp.zeros((TABLE, rows), F32)
    for e in range(EXP):
        roots = jnp.where(row_at % EXP == e, jnp.sqrt(weights[e : e + 1, :]), roots)
    high = roots.astype(BF16).astype(F32)
    middle = (roots - high).astype(BF16).astype(F32)
    low = roots - high - middle
    terms = jnp.where(row_at < EXP, high, jnp.where(row_at < 2 * EXP, middle, low))
    out[rows * width // LANES :, :] = jnp.where(row_at < 3 * EXP, terms, 0.0).astype(BF16)


def make_message(tokens, ids, weights):
    rows, width = tokens.shape
    hits = ids[:, :, None] == jnp.arange(EXP, dtype=jnp.int32)[None, None, :]
    table = jnp.sum(jnp.where(hits, weights[:, :, None], 0.0), axis=1)
    return pl.pallas_call(
        message_kernel,
        out_shape=jax.ShapeDtypeStruct((rows * width // LANES + TABLE, LANES), BF16),
        in_specs=[VMEM] * 2,
        out_specs=VMEM,
        cost_estimate=SMALL,
        compiler_params=params(8),
        name="make_message",
    )(tokens, table.T)


def block_of(piece, index):
    for array in piece:
        inside = array.shape[0] // LANES
        if index < inside:
            return array.at[index * LANES : (index + 1) * LANES]
        index -= inside


def choose(expert, piece):
    last = piece[-1]
    table = last[last.shape[0] - TABLE :, :].astype(F32)
    row_at = lax.broadcasted_iota(jnp.int32, (TABLE, LANES), 0)
    ours = jnp.logical_and(row_at % EXP == expert, row_at < 3 * EXP)
    root = jnp.sum(jnp.where(ours, table, 0.0), axis=0, keepdims=True)
    root = jnp.broadcast_to(root, (CAP, LANES))
    member = root > 0.0
    from_at = lax.broadcasted_iota(jnp.int32, (LANES, LANES), 0)
    to_at = lax.broadcasted_iota(jnp.int32, (LANES, LANES), 1)
    upto = (from_at <= to_at).astype(F32).astype(BF16)
    counted = jnp.dot(member.astype(F32).astype(BF16), upto, preferred_element_type=F32)
    place = counted.astype(jnp.int32) - 1
    slot_at = lax.broadcasted_iota(jnp.int32, (CAP, LANES), 0)
    select = jnp.logical_and(member, place == slot_at)
    scale = jnp.sum(jnp.where(select, root, 0.0), axis=1, keepdims=True)
    return select.astype(F32).astype(BF16), scale


def pack(expert, piece):
    select, scale = choose(expert, piece)
    blocks = sum(array.shape[0] // LANES for array in piece)
    groups = []
    for b in range(0, blocks, 4):
        some = jnp.concatenate(
            [block_of(piece, k)[...] for k in range(b, min(b + 4, blocks))], axis=1
        )
        picked = jnp.dot(select, some, preferred_element_type=F32)
        groups.append((picked * scale).astype(BF16))
    return jnp.concatenate(groups, axis=1)


def fetch_tile(index, pieces, scratch):
    edge = scratch.shape[1]
    blocks = sum(array.shape[0] // LANES for array in pieces[0])
    for b in range(blocks * LANES // edge):

        @pl.when(index == b)
        def _(b=b):
            for k, piece in enumerate(pieces):
                at = b * edge
                while at < (b + 1) * edge:
                    first = at % LANES
                    count = min(LANES - first, (b + 1) * edge - at)
                    scratch[k * LANES : (k + 1) * LANES, at - b * edge : at - b * edge + count] = (
                        block_of(piece, at // LANES)[:, first : first + count]
                    )
                    at += count


def product(left, right):
    return lax.dot_general(left[...], right[...], ROWS_WITH_ROWS, preferred_element_type=F32)


def absorb_kernel(count, started, *refs):
    scalars, refs = refs[0], refs[1:]
    pieces, refs = [[ref] for ref in refs[:count]], refs[count:]
    before, refs = refs[: 3 * started], refs[3 * started :]
    tile, left, theirs, *packs, mine = refs
    for slot, which in enumerate((left, mine, theirs), start=1):
        fetch_tile(scalars[slot], pieces, which)
    update = product(left, mine)
    if started:
        update = before[0][...] + update + product(before[1], before[2])
    tile[...] = update
    for piece, packed in zip(pieces, packs):
        packed[...] = pack(scalars[0], piece)


def absorb(scalars, pieces, before, edge):
    rows, width = LANES, pieces[0].shape[0] - TABLE
    count = len(pieces)
    columns = jax.ShapeDtypeStruct((count * rows, edge), BF16)
    out = pl.pallas_call(
        functools.partial(absorb_kernel, count, bool(before)),
        out_shape=[jax.ShapeDtypeStruct((edge, edge), F32), columns, columns]
        + [jax.ShapeDtypeStruct((CAP, width), BF16)] * count,
        in_specs=[SMEM] + [VMEM] * (count + len(before)),
        out_specs=[VMEM] * (3 + count),
        scratch_shapes=[pltpu.VMEM((count * rows, edge), BF16)],
        cost_estimate=SMALL,
        input_output_aliases={1 + count: 0} if before else {},
        compiler_params=params(14),
        name="absorb",
    )(scalars, *pieces, *before)
    return out[0], out[1:3], out[3:]


def place_rows(slab_at, packed, at, rows, across):
    count, width = packed.shape
    slab = across.shape[0]
    rows[at : at + count, :] = packed
    for s in range(width // slab):

        @pl.when(slab_at == s)
        def _():
            across[:, at : at + count] = packed[:, s * slab : (s + 1) * slab].T


def prepare_kernel(count, at, *refs):
    scalars, packs, (rows, across) = refs[0], refs[1 : 1 + count], refs[-2:]
    packed = jnp.concatenate([array[...] for array in packs], axis=0)
    place_rows(scalars[4], packed, at, rows, across)


def prepare(scalars, packs, at, operands, total, slab):
    width = packs[0].shape[1]
    return pl.pallas_call(
        functools.partial(prepare_kernel, len(packs), at),
        out_shape=[
            jax.ShapeDtypeStruct((total, width), BF16),
            jax.ShapeDtypeStruct((slab, total), BF16),
        ],
        in_specs=[SMEM] + [VMEM] * (len(packs) + len(operands)),
        out_specs=[VMEM] * 2,
        input_output_aliases={1 + len(packs) + k: k for k in range(len(operands))},
        cost_estimate=SMALL,
        compiler_params=params(12),
        name="prepare_rows",
    )(scalars, *packs, *operands)


def take_in(scalars, halves, at, rows, across, left, right):
    place_rows(scalars[4], pack(scalars[0], halves), at, rows, across)
    fetch_tile(scalars[1], [halves], left)
    fetch_tile(scalars[2], [halves], right)
    return product(left, right)


def settle_kernel(before, left, right, tile):
    tile[...] = before[...] + product(left, right)


def settle(sums):
    return pl.pallas_call(
        settle_kernel,
        out_shape=jax.ShapeDtypeStruct(sums[0].shape, F32),
        in_specs=[VMEM] * 3,
        out_specs=VMEM,
        input_output_aliases={0: 0},
        cost_estimate=SMALL,
        compiler_params=params(14),
        name="settle",
    )(*sums)


def take_own_kernel(*refs):
    scalars, halves, before, refs = refs[0], refs[1:3], refs[3], refs[6:]
    tile, rows, across, left, right = refs
    at = rows.shape[0] - 2 * CAP
    tile[...] = before[...] + take_in(scalars, halves, at, rows, across, left, right)


def take_own(scalars, halves, tile, operands):
    edge = tile.shape[0]
    return pl.pallas_call(
        take_own_kernel,
        out_shape=[jax.ShapeDtypeStruct(a.shape, a.dtype) for a in (tile, *operands)],
        in_specs=[SMEM] + [VMEM] * 5,
        out_specs=[VMEM] * 3,
        scratch_shapes=[pltpu.VMEM((LANES, edge), BF16)] * 2,
        input_output_aliases={3: 0, 4: 1, 5: 2},
        cost_estimate=SMALL,
        compiler_params=params(14),
        name="take_own",
    )(scalars, *halves, tile, *operands)


def finish_kernel(final, *refs):
    scalars, halves, before, (hessian, tile, rows, across, *scratch) = (
        refs[0], refs[1:3], refs[3], refs[6:]
    )
    staging, sums, left, right, sent = scratch
    at = rows.shape[0] - CAP
    copies = []

    def write(source, target):
        copies.append(pltpu.make_async_copy(source, target, sent.at[len(copies)]))
        copies[-1].start()

    update = take_in(scalars, halves, at, rows, across, left, right)
    sums[...] = (before[...] + update) * final
    write(sums, tile.at[0])
    height = staging.shape[1]
    for m in range(SPLITS):
        span = slice(m * height, (m + 1) * height)
        for n in range(0, rows.shape[1], STEP):
            staging[m, :, n : n + STEP] = (
                jnp.dot(across[span, :], rows[:, n : n + STEP], preferred_element_type=F32)
                * INVERSE
            )
        write(staging.at[m], hessian.at[span, :])
    for copy in copies:
        copy.wait()


def finish(scalars, halves, before, operands, final):
    edge = before.shape[0]
    rows, across = operands
    slab, width = across.shape[0], rows.shape[1]
    return pl.pallas_call(
        functools.partial(finish_kernel, final),
        out_shape=[
            jax.ShapeDtypeStruct((slab, width), F32),
            jax.ShapeDtypeStruct((1, edge, edge), F32),
            jax.ShapeDtypeStruct(rows.shape, BF16),
            jax.ShapeDtypeStruct(across.shape, BF16),
        ],
        in_specs=[SMEM] + [VMEM] * 5,
        out_specs=[ANY, ANY, VMEM, VMEM],
        scratch_shapes=[
            pltpu.VMEM((SPLITS, slab // SPLITS, width), F32),
            pltpu.VMEM((edge, edge), F32),
            pltpu.VMEM((LANES, edge), BF16),
            pltpu.VMEM((LANES, edge), BF16),
            pltpu.SemaphoreType.DMA((SPLITS + 1,)),
        ],
        input_output_aliases={4: 2, 5: 3},
        cost_estimate=SMALL,
        compiler_params=params(38),
        name="finish",
    )(scalars, *halves, before, rows, across)[:2]


def ring_of(chips):
    return list(range(0, chips, 2)) + list(range(chips - 1, 0, -2))


def on_device(tokens, route_ids, route_weights):
    devices = lax.axis_size("tok")
    position = lax.axis_index("tok")
    tok_rows, width = tokens.shape
    grid = math.isqrt(devices)
    edge = width // grid
    group = devices // EXP
    slab = width // group
    chips = devices // CORES
    ring = ring_of(chips)
    ahead = [
        (ring[i] * CORES + c, ring[(i + 1) % chips] * CORES + c)
        for i in range(chips)
        for c in range(CORES)
    ]
    streams = [ahead, [(b, a) for a, b in ahead]]
    pair = [(d, d ^ 1) for d in range(devices)]
    column = position % grid
    scalars = jnp.stack(
        [
            position // group,
            position // grid,
            column,
            column + 1 - 2 * (column % 2),
            position % group,
        ]
    ).astype(jnp.int32)

    def swap(array):
        return lax.ppermute(array, "tok", pair)

    def advance(held):
        return [lax.ppermute(array, "tok", stream) for array, stream in zip(held, streams)]

    rounds = chips // 2
    total = 4 * CAP * rounds

    pieces = [make_message(tokens, route_ids, route_weights)]
    operands, sums = [], []
    half = tok_rows * (width // LANES // 2)
    for step in range(1, rounds + 1):
        held = pieces * CORES if step == 1 else pieces
        if step == rounds:
            held = [held[0][: half + TABLE], held[1][half:]]
        moved = advance(held)
        tile, columns, packed = absorb(scalars, pieces, sums, edge)
        sums = [tile] + [swap(array) for array in columns]
        at = 4 * CAP * (step - 2) if step > 1 else total - 4 * CAP
        packs = list(packed) + [swap(array) for array in packed]
        operands = prepare(scalars, packs, at, operands, total, slab)
        if step < rounds:
            ahead_of, operands, sums = lax.optimization_barrier((moved[0], operands, sums))
            back_of, operands, sums = lax.optimization_barrier((moved[1], operands, sums))
            moved = [ahead_of, back_of]
        pieces = moved
    tile, pieces = settle(sums), list(pieces)
    for k in range(len(pieces)):
        pieces[k], operands, tile = lax.optimization_barrier((pieces[k], operands, tile))
    others = [swap(piece) for piece in pieces]
    tile, *operands = take_own(scalars, pieces, tile, operands)
    return tuple(finish(scalars, others, tile, operands, 1.0 / (devices * tok_rows)))


def solution(mesh):
    in_specs = (P(("grp", "tok"), None), P(("grp", "tok"), None), P(("grp", "tok"), None))
    out_specs = (P(("grp", "tok"), None), P(("grp", "tok"), None, None))
    return jax.shard_map(
        on_device, mesh=mesh, in_specs=in_specs, out_specs=out_specs, check_vma=False
    )
```

```python
import functools
import math

import jax
import jax.numpy as jnp
from jax import lax
from jax.experimental import pallas as pl
from jax.experimental.pallas import tpu as pltpu
from jax.sharding import PartitionSpec as P

EXP = 8
CAP = 32
CORES = 2
LANES = 128
TABLE = 32
STEP = 512
SPLITS = 7
VMEM = pl.BlockSpec(memory_space=pltpu.VMEM)
SMEM = pl.BlockSpec(memory_space=pltpu.SMEM)
ANY = pl.BlockSpec(memory_space=pl.ANY)
F32 = jnp.float32
BF16 = jnp.bfloat16
ROWS_WITH_ROWS = (((0,), (0,)), ((), ()))
INVERSE = 1.0 / (16.0 * CAP)
SMALL = pl.CostEstimate(flops=1, bytes_accessed=1, transcendentals=0)


def params(mib):
    return pltpu.CompilerParams(vmem_limit_bytes=mib * 2**20)


def message_kernel(tokens, weights, out):
    rows, width = tokens.shape
    for b in range(width // LANES):
        out[b * rows : (b + 1) * rows, :] = tokens[:, b * LANES : (b + 1) * LANES]
    row_at = lax.broadcasted_iota(jnp.int32, (TABLE, rows), 0)
    roots = jnp.zeros((TABLE, rows), F32)
    for e in range(EXP):
        roots = jnp.where(row_at % EXP == e, jnp.sqrt(weights[e : e + 1, :]), roots)
    high = roots.astype(BF16).astype(F32)
    middle = (roots - high).astype(BF16).astype(F32)
    low = roots - high - middle
    terms = jnp.where(row_at < EXP, high, jnp.where(row_at < 2 * EXP, middle, low))
    out[rows * width // LANES :, :] = jnp.where(row_at < 3 * EXP, terms, 0.0).astype(BF16)


def make_message(tokens, ids, weights):
    rows, width = tokens.shape
    hits = ids[:, :, None] == jnp.arange(EXP, dtype=jnp.int32)[None, None, :]
    table = jnp.sum(jnp.where(hits, weights[:, :, None], 0.0), axis=1)
    return pl.pallas_call(
        message_kernel,
        out_shape=jax.ShapeDtypeStruct((rows * width // LANES + TABLE, LANES), BF16),
        in_specs=[VMEM] * 2,
        out_specs=VMEM,
        cost_estimate=SMALL,
        compiler_params=params(8),
        name="make_message",
    )(tokens, table.T)


def block_of(piece, index):
    for array in piece:
        inside = array.shape[0] // LANES
        if index < inside:
            return array.at[index * LANES : (index + 1) * LANES]
        index -= inside


def choose(expert, piece):
    last = piece[-1]
    table = last[last.shape[0] - TABLE :, :].astype(F32)
    row_at = lax.broadcasted_iota(jnp.int32, (TABLE, LANES), 0)
    ours = jnp.logical_and(row_at % EXP == expert, row_at < 3 * EXP)
    root = jnp.sum(jnp.where(ours, table, 0.0), axis=0, keepdims=True)
    root = jnp.broadcast_to(root, (CAP, LANES))
    member = root > 0.0
    from_at = lax.broadcasted_iota(jnp.int32, (LANES, LANES), 0)
    to_at = lax.broadcasted_iota(jnp.int32, (LANES, LANES), 1)
    upto = (from_at <= to_at).astype(F32).astype(BF16)
    counted = jnp.dot(member.astype(F32).astype(BF16), upto, preferred_element_type=F32)
    place = counted.astype(jnp.int32) - 1
    slot_at = lax.broadcasted_iota(jnp.int32, (CAP, LANES), 0)
    select = jnp.logical_and(member, place == slot_at)
    scale = jnp.sum(jnp.where(select, root, 0.0), axis=1, keepdims=True)
    return select.astype(F32).astype(BF16), scale


def pack(expert, piece):
    select, scale = choose(expert, piece)
    blocks = sum(array.shape[0] // LANES for array in piece)
    groups = []
    for b in range(0, blocks, 4):
        some = jnp.concatenate(
            [block_of(piece, k)[...] for k in range(b, min(b + 4, blocks))], axis=1
        )
        picked = jnp.dot(select, some, preferred_element_type=F32)
        groups.append((picked * scale).astype(BF16))
    return jnp.concatenate(groups, axis=1)


def fetch_tile(index, pieces, scratch):
    edge = scratch.shape[1]
    blocks = sum(array.shape[0] // LANES for array in pieces[0])
    for b in range(blocks * LANES // edge):

        @pl.when(index == b)
        def _(b=b):
            for k, piece in enumerate(pieces):
                at = b * edge
                while at < (b + 1) * edge:
                    first = at % LANES
                    count = min(LANES - first, (b + 1) * edge - at)
                    scratch[k * LANES : (k + 1) * LANES, at - b * edge : at - b * edge + count] = (
                        block_of(piece, at // LANES)[:, first : first + count]
                    )
                    at += count


def product(left, right):
    return lax.dot_general(left[...], right[...], ROWS_WITH_ROWS, preferred_element_type=F32)


def absorb_kernel(count, started, *refs):
    scalars, refs = refs[0], refs[1:]
    pieces, refs = [[ref] for ref in refs[:count]], refs[count:]
    before, refs = refs[: 3 * started], refs[3 * started :]
    tile, left, theirs, *packs, mine = refs
    for slot, which in enumerate((left, mine, theirs), start=1):
        fetch_tile(scalars[slot], pieces, which)
    update = product(left, mine)
    if started:
        update = before[0][...] + update + product(before[1], before[2])
    tile[...] = update
    for piece, packed in zip(pieces, packs):
        packed[...] = pack(scalars[0], piece)


def absorb(scalars, pieces, before, edge):
    rows, width = LANES, pieces[0].shape[0] - TABLE
    count = len(pieces)
    columns = jax.ShapeDtypeStruct((count * rows, edge), BF16)
    out = pl.pallas_call(
        functools.partial(absorb_kernel, count, bool(before)),
        out_shape=[jax.ShapeDtypeStruct((edge, edge), F32), columns, columns]
        + [jax.ShapeDtypeStruct((CAP, width), BF16)] * count,
        in_specs=[SMEM] + [VMEM] * (count + len(before)),
        out_specs=[VMEM] * (3 + count),
        scratch_shapes=[pltpu.VMEM((count * rows, edge), BF16)],
        cost_estimate=SMALL,
        input_output_aliases={1 + count: 0} if before else {},
        compiler_params=params(14),
        name="absorb",
    )(scalars, *pieces, *before)
    return out[0], out[1:3], out[3:]


def place_rows(slab_at, packed, at, rows, across):
    count, width = packed.shape
    slab = across.shape[0]
    rows[at : at + count, :] = packed
    for s in range(width // slab):

        @pl.when(slab_at == s)
        def _():
            across[:, at : at + count] = packed[:, s * slab : (s + 1) * slab].T


def prepare_kernel(count, at, *refs):
    scalars, packs, (rows, across) = refs[0], refs[1 : 1 + count], refs[-2:]
    packed = jnp.concatenate([array[...] for array in packs], axis=0)
    place_rows(scalars[4], packed, at, rows, across)


def prepare(scalars, packs, at, operands, total, slab):
    width = packs[0].shape[1]
    return pl.pallas_call(
        functools.partial(prepare_kernel, len(packs), at),
        out_shape=[
            jax.ShapeDtypeStruct((total, width), BF16),
            jax.ShapeDtypeStruct((slab, total), BF16),
        ],
        in_specs=[SMEM] + [VMEM] * (len(packs) + len(operands)),
        out_specs=[VMEM] * 2,
        input_output_aliases={1 + len(packs) + k: k for k in range(len(operands))},
        cost_estimate=SMALL,
        compiler_params=params(12),
        name="prepare_rows",
    )(scalars, *packs, *operands)


def settle_kernel(before, left, right, tile):
    tile[...] = before[...] + product(left, right)


def settle(sums):
    return pl.pallas_call(
        settle_kernel,
        out_shape=jax.ShapeDtypeStruct(sums[0].shape, F32),
        in_specs=[VMEM] * 3,
        out_specs=VMEM,
        input_output_aliases={0: 0},
        cost_estimate=SMALL,
        compiler_params=params(14),
        name="settle",
    )(*sums)


def take_own_kernel(*refs):
    scalars, piece, (rows, across) = refs[0], refs[1:3], refs[5:]
    place_rows(scalars[4], pack(scalars[0], piece), rows.shape[0] - 2 * CAP, rows, across)


def take_own(scalars, piece, operands):
    return pl.pallas_call(
        take_own_kernel,
        out_shape=[jax.ShapeDtypeStruct(a.shape, a.dtype) for a in operands],
        in_specs=[SMEM] + [VMEM] * 4,
        out_specs=[VMEM] * 2,
        input_output_aliases={3: 0, 4: 1},
        cost_estimate=SMALL,
        compiler_params=params(14),
        name="take_own",
    )(scalars, *piece, *operands)


def finish_kernel(final, *refs):
    scalars, own, other, before, (hessian, tile, rows, across, *scratch) = (
        refs[0], refs[1:3], refs[3:5], refs[5], refs[8:]
    )
    staging, sums, left, right, sent = scratch
    copies = []

    def write(source, target):
        copies.append(pltpu.make_async_copy(source, target, sent.at[len(copies)]))
        copies[-1].start()

    fetch_tile(scalars[1], [own, other], left)
    fetch_tile(scalars[2], [own, other], right)
    sums[...] = (before[...] + product(left, right)) * final
    write(sums, tile.at[0])
    place_rows(scalars[4], pack(scalars[0], other), rows.shape[0] - CAP, rows, across)
    height = staging.shape[1]
    for m in range(SPLITS):
        span = slice(m * height, (m + 1) * height)
        for n in range(0, rows.shape[1], STEP):
            staging[m, :, n : n + STEP] = (
                jnp.dot(across[span, :], rows[:, n : n + STEP], preferred_element_type=F32)
                * INVERSE
            )
        write(staging.at[m], hessian.at[span, :])
    for copy in copies:
        copy.wait()


def finish(scalars, own, other, before, operands, final):
    edge = before.shape[0]
    rows, across = operands
    slab, width = across.shape[0], rows.shape[1]
    return pl.pallas_call(
        functools.partial(finish_kernel, final),
        out_shape=[
            jax.ShapeDtypeStruct((slab, width), F32),
            jax.ShapeDtypeStruct((1, edge, edge), F32),
            jax.ShapeDtypeStruct(rows.shape, BF16),
            jax.ShapeDtypeStruct(across.shape, BF16),
        ],
        in_specs=[SMEM] + [VMEM] * 7,
        out_specs=[ANY, ANY, VMEM, VMEM],
        scratch_shapes=[
            pltpu.VMEM((SPLITS, slab // SPLITS, width), F32),
            pltpu.VMEM((edge, edge), F32),
            pltpu.VMEM((2 * LANES, edge), BF16),
            pltpu.VMEM((2 * LANES, edge), BF16),
            pltpu.SemaphoreType.DMA((SPLITS + 1,)),
        ],
        input_output_aliases={6: 2, 7: 3},
        cost_estimate=SMALL,
        compiler_params=params(38),
        name="finish",
    )(scalars, *own, *other, before, rows, across)[:2]


def ring_of(chips):
    return list(range(0, chips, 2)) + list(range(chips - 1, 0, -2))


def on_device(tokens, route_ids, route_weights):
    devices = lax.axis_size("tok")
    position = lax.axis_index("tok")
    tok_rows, width = tokens.shape
    grid = math.isqrt(devices)
    edge = width // grid
    group = devices // EXP
    slab = width // group
    chips = devices // CORES
    ring = ring_of(chips)
    ahead = [
        (ring[i] * CORES + c, ring[(i + 1) % chips] * CORES + c)
        for i in range(chips)
        for c in range(CORES)
    ]
    streams = [ahead, [(b, a) for a, b in ahead]]
    pair = [(d, d ^ 1) for d in range(devices)]
    column = position % grid
    scalars = jnp.stack(
        [
            position // group,
            position // grid,
            column,
            column + 1 - 2 * (column % 2),
            position % group,
        ]
    ).astype(jnp.int32)

    def swap(array):
        return lax.ppermute(array, "tok", pair)

    def advance(held):
        return [lax.ppermute(array, "tok", stream) for array, stream in zip(held, streams)]

    rounds = chips // 2
    total = 4 * CAP * rounds

    pieces = [make_message(tokens, route_ids, route_weights)]
    operands, sums = [], []
    half = tok_rows * (width // LANES // 2)
    for step in range(1, rounds + 1):
        held = pieces * CORES if step == 1 else pieces
        if step == rounds:
            held = [held[0][: half + TABLE], held[1][half:]]
        moved = advance(held)
        tile, columns, packed = absorb(scalars, pieces, sums, edge)
        sums = [tile] + [swap(array) for array in columns]
        at = 4 * CAP * (step - 2) if step > 1 else total - 4 * CAP
        packs = list(packed) + [swap(array) for array in packed]
        operands = prepare(scalars, packs, at, operands, total, slab)
        if step < rounds:
            ahead_of, operands, sums = lax.optimization_barrier((moved[0], operands, sums))
            back_of, operands, sums = lax.optimization_barrier((moved[1], operands, sums))
            moved = [ahead_of, back_of]
        pieces = moved
    tile, pieces = settle(sums), list(pieces)
    for k in range(len(pieces)):
        pieces[k], operands, tile = lax.optimization_barrier((pieces[k], operands, tile))
    others = [swap(piece) for piece in pieces]
    operands = take_own(scalars, pieces, operands)
    return tuple(finish(scalars, pieces, others, tile, operands, 1.0 / (devices * tok_rows)))


def solution(mesh):
    in_specs = (P(("grp", "tok"), None), P(("grp", "tok"), None), P(("grp", "tok"), None))
    out_specs = (P(("grp", "tok"), None), P(("grp", "tok"), None, None))
    return jax.shard_map(
        on_device, mesh=mesh, in_specs=in_specs, out_specs=out_specs, check_vma=False
    )
```

```python
import functools
import math

import jax
import jax.numpy as jnp
from jax import lax
from jax.experimental import pallas as pl
from jax.experimental.pallas import tpu as pltpu
from jax.sharding import PartitionSpec as P

EXP = 8
CAP = 32
CORES = 2
LANES = 128
TABLE = 32
STEP = 512
SPLITS = 14
VMEM = pl.BlockSpec(memory_space=pltpu.VMEM)
SMEM = pl.BlockSpec(memory_space=pltpu.SMEM)
ANY = pl.BlockSpec(memory_space=pl.ANY)
F32 = jnp.float32
BF16 = jnp.bfloat16
ROWS_WITH_ROWS = (((0,), (0,)), ((), ()))
INVERSE = 1.0 / (16.0 * CAP)
SMALL = pl.CostEstimate(flops=1, bytes_accessed=1, transcendentals=0)


def params(mib):
    return pltpu.CompilerParams(vmem_limit_bytes=mib * 2**20)


def message_kernel(tokens, weights, out):
    rows, width = tokens.shape
    for b in range(width // LANES):
        out[b * rows : (b + 1) * rows, :] = tokens[:, b * LANES : (b + 1) * LANES]
    row_at = lax.broadcasted_iota(jnp.int32, (TABLE, rows), 0)
    roots = jnp.zeros((TABLE, rows), F32)
    for e in range(EXP):
        roots = jnp.where(row_at % EXP == e, jnp.sqrt(weights[e : e + 1, :]), roots)
    high = roots.astype(BF16).astype(F32)
    middle = (roots - high).astype(BF16).astype(F32)
    low = roots - high - middle
    terms = jnp.where(row_at < EXP, high, jnp.where(row_at < 2 * EXP, middle, low))
    out[rows * width // LANES :, :] = jnp.where(row_at < 3 * EXP, terms, 0.0).astype(BF16)


def make_message(tokens, ids, weights):
    rows, width = tokens.shape
    hits = ids[:, :, None] == jnp.arange(EXP, dtype=jnp.int32)[None, None, :]
    table = jnp.sum(jnp.where(hits, weights[:, :, None], 0.0), axis=1)
    return pl.pallas_call(
        message_kernel,
        out_shape=jax.ShapeDtypeStruct((rows * width // LANES + TABLE, LANES), BF16),
        in_specs=[VMEM] * 2,
        out_specs=VMEM,
        cost_estimate=SMALL,
        compiler_params=params(8),
        name="make_message",
    )(tokens, table.T)


def block_of(piece, index):
    for array in piece:
        inside = array.shape[0] // LANES
        if index < inside:
            return array.at[index * LANES : (index + 1) * LANES]
        index -= inside


def choose(expert, piece):
    last = piece[-1]
    table = last[last.shape[0] - TABLE :, :].astype(F32)
    row_at = lax.broadcasted_iota(jnp.int32, (TABLE, LANES), 0)
    ours = jnp.logical_and(row_at % EXP == expert, row_at < 3 * EXP)
    root = jnp.sum(jnp.where(ours, table, 0.0), axis=0, keepdims=True)
    root = jnp.broadcast_to(root, (CAP, LANES))
    member = root > 0.0
    from_at = lax.broadcasted_iota(jnp.int32, (LANES, LANES), 0)
    to_at = lax.broadcasted_iota(jnp.int32, (LANES, LANES), 1)
    upto = (from_at <= to_at).astype(F32).astype(BF16)
    counted = jnp.dot(member.astype(F32).astype(BF16), upto, preferred_element_type=F32)
    place = counted.astype(jnp.int32) - 1
    slot_at = lax.broadcasted_iota(jnp.int32, (CAP, LANES), 0)
    select = jnp.logical_and(member, place == slot_at)
    scale = jnp.sum(jnp.where(select, root, 0.0), axis=1, keepdims=True)
    return select.astype(F32).astype(BF16), scale


def pack(expert, piece):
    select, scale = choose(expert, piece)
    blocks = sum(array.shape[0] // LANES for array in piece)
    groups = []
    for b in range(0, blocks, 4):
        some = jnp.concatenate(
            [block_of(piece, k)[...] for k in range(b, min(b + 4, blocks))], axis=1
        )
        picked = jnp.dot(select, some, preferred_element_type=F32)
        groups.append((picked * scale).astype(BF16))
    return jnp.concatenate(groups, axis=1)


def fetch_tile(index, pieces, scratch):
    edge = scratch.shape[1]
    blocks = sum(array.shape[0] // LANES for array in pieces[0])
    for b in range(blocks * LANES // edge):

        @pl.when(index == b)
        def _(b=b):
            for k, piece in enumerate(pieces):
                at = b * edge
                while at < (b + 1) * edge:
                    first = at % LANES
                    count = min(LANES - first, (b + 1) * edge - at)
                    scratch[k * LANES : (k + 1) * LANES, at - b * edge : at - b * edge + count] = (
                        block_of(piece, at // LANES)[:, first : first + count]
                    )
                    at += count


def product(left, right):
    return lax.dot_general(left[...], right[...], ROWS_WITH_ROWS, preferred_element_type=F32)


def absorb_kernel(count, started, *refs):
    scalars, refs = refs[0], refs[1:]
    pieces, refs = [[ref] for ref in refs[:count]], refs[count:]
    before, refs = refs[: 3 * started], refs[3 * started :]
    tile, left, theirs, *packs, mine = refs
    for slot, which in enumerate((left, mine, theirs), start=1):
        fetch_tile(scalars[slot], pieces, which)
    update = product(left, mine)
    if started:
        update = before[0][...] + update + product(before[1], before[2])
    tile[...] = update
    for piece, packed in zip(pieces, packs):
        packed[...] = pack(scalars[0], piece)


def absorb(scalars, pieces, before, edge):
    rows, width = LANES, pieces[0].shape[0] - TABLE
    count = len(pieces)
    columns = jax.ShapeDtypeStruct((count * rows, edge), BF16)
    out = pl.pallas_call(
        functools.partial(absorb_kernel, count, bool(before)),
        out_shape=[jax.ShapeDtypeStruct((edge, edge), F32), columns, columns]
        + [jax.ShapeDtypeStruct((CAP, width), BF16)] * count,
        in_specs=[SMEM] + [VMEM] * (count + len(before)),
        out_specs=[VMEM] * (3 + count),
        scratch_shapes=[pltpu.VMEM((count * rows, edge), BF16)],
        cost_estimate=SMALL,
        input_output_aliases={1 + count: 0} if before else {},
        compiler_params=params(14),
        name="absorb",
    )(scalars, *pieces, *before)
    return out[0], out[1:3], out[3:]


def place_rows(slab_at, packed, at, rows, across):
    count, width = packed.shape
    slab = across.shape[0]
    rows[at : at + count, :] = packed
    for s in range(width // slab):

        @pl.when(slab_at == s)
        def _():
            across[:, at : at + count] = packed[:, s * slab : (s + 1) * slab].T


def prepare_kernel(count, at, *refs):
    scalars, packs, (rows, across) = refs[0], refs[1 : 1 + count], refs[-2:]
    packed = jnp.concatenate([array[...] for array in packs], axis=0)
    place_rows(scalars[4], packed, at, rows, across)


def prepare(scalars, packs, at, operands, total, slab):
    width = packs[0].shape[1]
    return pl.pallas_call(
        functools.partial(prepare_kernel, len(packs), at),
        out_shape=[
            jax.ShapeDtypeStruct((total, width), BF16),
            jax.ShapeDtypeStruct((slab, total), BF16),
        ],
        in_specs=[SMEM] + [VMEM] * (len(packs) + len(operands)),
        out_specs=[VMEM] * 2,
        input_output_aliases={1 + len(packs) + k: k for k in range(len(operands))},
        cost_estimate=SMALL,
        compiler_params=params(12),
        name="prepare_rows",
    )(scalars, *packs, *operands)


def settle_kernel(before, left, right, tile):
    tile[...] = before[...] + product(left, right)


def settle(sums):
    return pl.pallas_call(
        settle_kernel,
        out_shape=jax.ShapeDtypeStruct(sums[0].shape, F32),
        in_specs=[VMEM] * 3,
        out_specs=VMEM,
        input_output_aliases={0: 0},
        cost_estimate=SMALL,
        compiler_params=params(14),
        name="settle",
    )(*sums)


def take_own_kernel(*refs):
    scalars, piece, (rows, across) = refs[0], refs[1:3], refs[5:]
    place_rows(scalars[4], pack(scalars[0], piece), rows.shape[0] - 2 * CAP, rows, across)


def take_own(scalars, piece, operands):
    return pl.pallas_call(
        take_own_kernel,
        out_shape=[jax.ShapeDtypeStruct(a.shape, a.dtype) for a in operands],
        in_specs=[SMEM] + [VMEM] * 4,
        out_specs=[VMEM] * 2,
        input_output_aliases={3: 0, 4: 1},
        cost_estimate=SMALL,
        compiler_params=params(14),
        name="take_own",
    )(scalars, *piece, *operands)


def finish_kernel(final, *refs):
    scalars, own, other, before, (hessian, tile, rows, across, *scratch) = (
        refs[0], refs[1:3], refs[3:5], refs[5], refs[8:]
    )
    staging, sums, left, right, sent = scratch
    copies = []

    def write(source, target):
        copies.append(pltpu.make_async_copy(source, target, sent.at[len(copies)]))
        copies[-1].start()

    fetch_tile(scalars[1], [own, other], left)
    fetch_tile(scalars[2], [own, other], right)
    sums[...] = (before[...] + product(left, right)) * final
    write(sums, tile.at[0])
    place_rows(scalars[4], pack(scalars[0], other), rows.shape[0] - CAP, rows, across)
    height = staging.shape[1]
    for m in range(SPLITS):
        span = slice(m * height, (m + 1) * height)
        for n in range(0, rows.shape[1], STEP):
            staging[m, :, n : n + STEP] = (
                jnp.dot(across[span, :], rows[:, n : n + STEP], preferred_element_type=F32)
                * INVERSE
            )
        write(staging.at[m], hessian.at[span, :])
    for copy in copies:
        copy.wait()


def finish(scalars, own, other, before, operands, final):
    edge = before.shape[0]
    rows, across = operands
    slab, width = across.shape[0], rows.shape[1]
    return pl.pallas_call(
        functools.partial(finish_kernel, final),
        out_shape=[
            jax.ShapeDtypeStruct((slab, width), F32),
            jax.ShapeDtypeStruct((1, edge, edge), F32),
            jax.ShapeDtypeStruct(rows.shape, BF16),
            jax.ShapeDtypeStruct(across.shape, BF16),
        ],
        in_specs=[SMEM] + [VMEM] * 7,
        out_specs=[ANY, ANY, VMEM, VMEM],
        scratch_shapes=[
            pltpu.VMEM((SPLITS, slab // SPLITS, width), F32),
            pltpu.VMEM((edge, edge), F32),
            pltpu.VMEM((2 * LANES, edge), BF16),
            pltpu.VMEM((2 * LANES, edge), BF16),
            pltpu.SemaphoreType.DMA((SPLITS + 1,)),
        ],
        input_output_aliases={6: 2, 7: 3},
        cost_estimate=SMALL,
        compiler_params=params(38),
        name="finish",
    )(scalars, *own, *other, before, rows, across)[:2]


def ring_of(chips):
    return list(range(0, chips, 2)) + list(range(chips - 1, 0, -2))


def on_device(tokens, route_ids, route_weights):
    devices = lax.axis_size("tok")
    position = lax.axis_index("tok")
    tok_rows, width = tokens.shape
    grid = math.isqrt(devices)
    edge = width // grid
    group = devices // EXP
    slab = width // group
    chips = devices // CORES
    ring = ring_of(chips)
    ahead = [
        (ring[i] * CORES + c, ring[(i + 1) % chips] * CORES + c)
        for i in range(chips)
        for c in range(CORES)
    ]
    streams = [ahead, [(b, a) for a, b in ahead]]
    pair = [(d, d ^ 1) for d in range(devices)]
    column = position % grid
    scalars = jnp.stack(
        [
            position // group,
            position // grid,
            column,
            column + 1 - 2 * (column % 2),
            position % group,
        ]
    ).astype(jnp.int32)

    def swap(array):
        return lax.ppermute(array, "tok", pair)

    def advance(held):
        return [lax.ppermute(array, "tok", stream) for array, stream in zip(held, streams)]

    rounds = chips // 2
    total = 4 * CAP * rounds

    pieces = [make_message(tokens, route_ids, route_weights)]
    operands, sums = [], []
    half = tok_rows * (width // LANES // 2)
    for step in range(1, rounds + 1):
        held = pieces * CORES if step == 1 else pieces
        if step == rounds:
            held = [held[0][: half + TABLE], held[1][half:]]
        moved = advance(held)
        tile, columns, packed = absorb(scalars, pieces, sums, edge)
        sums = [tile] + [swap(array) for array in columns]
        at = 4 * CAP * (step - 2) if step > 1 else total - 4 * CAP
        packs = list(packed) + [swap(array) for array in packed]
        operands = prepare(scalars, packs, at, operands, total, slab)
        if step < rounds:
            ahead_of, operands, sums = lax.optimization_barrier((moved[0], operands, sums))
            back_of, operands, sums = lax.optimization_barrier((moved[1], operands, sums))
            moved = [ahead_of, back_of]
        pieces = moved
    tile, pieces = settle(sums), list(pieces)
    for k in range(len(pieces)):
        pieces[k], operands, tile = lax.optimization_barrier((pieces[k], operands, tile))
    others = [swap(piece) for piece in pieces]
    operands = take_own(scalars, pieces, operands)
    return tuple(finish(scalars, pieces, others, tile, operands, 1.0 / (devices * tok_rows)))


def solution(mesh):
    in_specs = (P(("grp", "tok"), None), P(("grp", "tok"), None), P(("grp", "tok"), None))
    out_specs = (P(("grp", "tok"), None), P(("grp", "tok"), None, None))
    return jax.shard_map(
        on_device, mesh=mesh, in_specs=in_specs, out_specs=out_specs, check_vma=False
    )
```

```python
import functools
import math

import jax
import jax.numpy as jnp
from jax import lax
from jax.experimental import pallas as pl
from jax.experimental.pallas import tpu as pltpu
from jax.sharding import PartitionSpec as P

EXP = 8
CAP = 32
CORES = 2
LANES = 128
TABLE = 32
STEP = 512
SPLITS = 14
VMEM = pl.BlockSpec(memory_space=pltpu.VMEM)
SMEM = pl.BlockSpec(memory_space=pltpu.SMEM)
ANY = pl.BlockSpec(memory_space=pl.ANY)
F32 = jnp.float32
BF16 = jnp.bfloat16
ROWS_WITH_ROWS = (((0,), (0,)), ((), ()))
INVERSE = 1.0 / (16.0 * CAP)
SMALL = pl.CostEstimate(flops=1, bytes_accessed=1, transcendentals=0)


def params(mib):
    return pltpu.CompilerParams(vmem_limit_bytes=mib * 2**20)


def message_kernel(tokens, weights, out):
    rows, width = tokens.shape
    for b in range(width // LANES):
        out[b * rows : (b + 1) * rows, :] = tokens[:, b * LANES : (b + 1) * LANES]
    row_at = lax.broadcasted_iota(jnp.int32, (TABLE, rows), 0)
    roots = jnp.zeros((TABLE, rows), F32)
    for e in range(EXP):
        roots = jnp.where(row_at % EXP == e, jnp.sqrt(weights[e : e + 1, :]), roots)
    high = roots.astype(BF16).astype(F32)
    middle = (roots - high).astype(BF16).astype(F32)
    low = roots - high - middle
    terms = jnp.where(row_at < EXP, high, jnp.where(row_at < 2 * EXP, middle, low))
    out[rows * width // LANES :, :] = jnp.where(row_at < 3 * EXP, terms, 0.0).astype(BF16)


def make_message(tokens, ids, weights):
    rows, width = tokens.shape
    hits = ids[:, :, None] == jnp.arange(EXP, dtype=jnp.int32)[None, None, :]
    table = jnp.sum(jnp.where(hits, weights[:, :, None], 0.0), axis=1)
    return pl.pallas_call(
        message_kernel,
        out_shape=jax.ShapeDtypeStruct((rows * width // LANES + TABLE, LANES), BF16),
        in_specs=[VMEM] * 2,
        out_specs=VMEM,
        cost_estimate=SMALL,
        compiler_params=params(8),
        name="make_message",
    )(tokens, table.T)


def block_of(piece, index):
    for array in piece:
        inside = array.shape[0] // LANES
        if index < inside:
            return array.at[index * LANES : (index + 1) * LANES]
        index -= inside


def choose(expert, piece):
    last = piece[-1]
    table = last[last.shape[0] - TABLE :, :].astype(F32)
    row_at = lax.broadcasted_iota(jnp.int32, (TABLE, LANES), 0)
    ours = jnp.logical_and(row_at % EXP == expert, row_at < 3 * EXP)
    root = jnp.sum(jnp.where(ours, table, 0.0), axis=0, keepdims=True)
    root = jnp.broadcast_to(root, (CAP, LANES))
    member = root > 0.0
    from_at = lax.broadcasted_iota(jnp.int32, (LANES, LANES), 0)
    to_at = lax.broadcasted_iota(jnp.int32, (LANES, LANES), 1)
    upto = (from_at <= to_at).astype(F32).astype(BF16)
    counted = jnp.dot(member.astype(F32).astype(BF16), upto, preferred_element_type=F32)
    place = counted.astype(jnp.int32) - 1
    slot_at = lax.broadcasted_iota(jnp.int32, (CAP, LANES), 0)
    select = jnp.logical_and(member, place == slot_at)
    scale = jnp.sum(jnp.where(select, root, 0.0), axis=1, keepdims=True)
    return select.astype(F32).astype(BF16), scale


def pack(expert, piece):
    select, scale = choose(expert, piece)
    blocks = sum(array.shape[0] // LANES for array in piece)
    groups = []
    for b in range(0, blocks, 4):
        some = jnp.concatenate(
            [block_of(piece, k)[...] for k in range(b, min(b + 4, blocks))], axis=1
        )
        picked = jnp.dot(select, some, preferred_element_type=F32)
        groups.append((picked * scale).astype(BF16))
    return jnp.concatenate(groups, axis=1)


def fetch_tile(index, pieces, scratch):
    edge = scratch.shape[1]
    blocks = sum(array.shape[0] // LANES for array in pieces[0])
    for b in range(blocks * LANES // edge):

        @pl.when(index == b)
        def _(b=b):
            for k, piece in enumerate(pieces):
                at = b * edge
                while at < (b + 1) * edge:
                    first = at % LANES
                    count = min(LANES - first, (b + 1) * edge - at)
                    scratch[k * LANES : (k + 1) * LANES, at - b * edge : at - b * edge + count] = (
                        block_of(piece, at // LANES)[:, first : first + count]
                    )
                    at += count


def product(left, right):
    return lax.dot_general(left[...], right[...], ROWS_WITH_ROWS, preferred_element_type=F32)


def absorb_kernel(count, started, *refs):
    scalars, refs = refs[0], refs[1:]
    pieces, refs = [[ref] for ref in refs[:count]], refs[count:]
    before, refs = refs[: 3 * started], refs[3 * started :]
    tile, left, theirs, packs, mine = refs
    for slot, which in enumerate((left, mine, theirs), start=1):
        fetch_tile(scalars[slot], pieces, which)
    update = product(left, mine)
    if started:
        update = before[0][...] + update + product(before[1], before[2])
    tile[...] = update
    for k, piece in enumerate(pieces):
        packs[k * CAP : (k + 1) * CAP, :] = pack(scalars[0], piece)


def absorb(scalars, pieces, before, edge):
    rows, width = LANES, pieces[0].shape[0] - TABLE
    count = len(pieces)
    columns = jax.ShapeDtypeStruct((count * rows, edge), BF16)
    out = pl.pallas_call(
        functools.partial(absorb_kernel, count, bool(before)),
        out_shape=[jax.ShapeDtypeStruct((edge, edge), F32), columns, columns]
        + [jax.ShapeDtypeStruct((count * CAP, width), BF16)],
        in_specs=[SMEM] + [VMEM] * (count + len(before)),
        out_specs=[VMEM] * 4,
        scratch_shapes=[pltpu.VMEM((count * rows, edge), BF16)],
        cost_estimate=SMALL,
        input_output_aliases={1 + count: 0} if before else {},
        compiler_params=params(14),
        name="absorb",
    )(scalars, *pieces, *before)
    return out[0], out[1:3], out[3:]


def place_rows(slab_at, packed, at, rows, across):
    count, width = packed.shape
    slab = across.shape[0]
    rows[at : at + count, :] = packed
    for s in range(width // slab):

        @pl.when(slab_at == s)
        def _():
            across[:, at : at + count] = packed[:, s * slab : (s + 1) * slab].T


def prepare_kernel(count, at, *refs):
    scalars, packs, (rows, across) = refs[0], refs[1 : 1 + count], refs[-2:]
    packed = jnp.concatenate([array[...] for array in packs], axis=0)
    place_rows(scalars[4], packed, at, rows, across)


def prepare(scalars, packs, at, operands, total, slab):
    width = packs[0].shape[1]
    return pl.pallas_call(
        functools.partial(prepare_kernel, len(packs), at),
        out_shape=[
            jax.ShapeDtypeStruct((total, width), BF16),
            jax.ShapeDtypeStruct((slab, total), BF16),
        ],
        in_specs=[SMEM] + [VMEM] * (len(packs) + len(operands)),
        out_specs=[VMEM] * 2,
        input_output_aliases={1 + len(packs) + k: k for k in range(len(operands))},
        cost_estimate=SMALL,
        compiler_params=params(12),
        name="prepare_rows",
    )(scalars, *packs, *operands)


def settle_kernel(before, left, right, tile):
    tile[...] = before[...] + product(left, right)


def settle(sums):
    return pl.pallas_call(
        settle_kernel,
        out_shape=jax.ShapeDtypeStruct(sums[0].shape, F32),
        in_specs=[VMEM] * 3,
        out_specs=VMEM,
        input_output_aliases={0: 0},
        cost_estimate=SMALL,
        compiler_params=params(14),
        name="settle",
    )(*sums)


def take_own_kernel(*refs):
    scalars, piece, (rows, across) = refs[0], refs[1:3], refs[5:]
    place_rows(scalars[4], pack(scalars[0], piece), rows.shape[0] - 2 * CAP, rows, across)


def take_own(scalars, piece, operands):
    return pl.pallas_call(
        take_own_kernel,
        out_shape=[jax.ShapeDtypeStruct(a.shape, a.dtype) for a in operands],
        in_specs=[SMEM] + [VMEM] * 4,
        out_specs=[VMEM] * 2,
        input_output_aliases={3: 0, 4: 1},
        cost_estimate=SMALL,
        compiler_params=params(14),
        name="take_own",
    )(scalars, *piece, *operands)


def finish_kernel(final, *refs):
    scalars, own, other, before, (hessian, tile, rows, across, *scratch) = (
        refs[0], refs[1:3], refs[3:5], refs[5], refs[8:]
    )
    staging, sums, left, right, sent = scratch
    copies = []

    def write(source, target):
        copies.append(pltpu.make_async_copy(source, target, sent.at[len(copies)]))
        copies[-1].start()

    fetch_tile(scalars[1], [own, other], left)
    fetch_tile(scalars[2], [own, other], right)
    sums[...] = (before[...] + product(left, right)) * final
    write(sums, tile.at[0])
    place_rows(scalars[4], pack(scalars[0], other), rows.shape[0] - CAP, rows, across)
    height = staging.shape[1]
    for m in range(SPLITS):
        span = slice(m * height, (m + 1) * height)
        for n in range(0, rows.shape[1], STEP):
            staging[m, :, n : n + STEP] = (
                jnp.dot(across[span, :], rows[:, n : n + STEP], preferred_element_type=F32)
                * INVERSE
            )
        write(staging.at[m], hessian.at[span, :])
    for copy in copies:
        copy.wait()


def finish(scalars, own, other, before, operands, final):
    edge = before.shape[0]
    rows, across = operands
    slab, width = across.shape[0], rows.shape[1]
    return pl.pallas_call(
        functools.partial(finish_kernel, final),
        out_shape=[
            jax.ShapeDtypeStruct((slab, width), F32),
            jax.ShapeDtypeStruct((1, edge, edge), F32),
            jax.ShapeDtypeStruct(rows.shape, BF16),
            jax.ShapeDtypeStruct(across.shape, BF16),
        ],
        in_specs=[SMEM] + [VMEM] * 7,
        out_specs=[ANY, ANY, VMEM, VMEM],
        scratch_shapes=[
            pltpu.VMEM((SPLITS, slab // SPLITS, width), F32),
            pltpu.VMEM((edge, edge), F32),
            pltpu.VMEM((2 * LANES, edge), BF16),
            pltpu.VMEM((2 * LANES, edge), BF16),
            pltpu.SemaphoreType.DMA((SPLITS + 1,)),
        ],
        input_output_aliases={6: 2, 7: 3},
        cost_estimate=SMALL,
        compiler_params=params(38),
        name="finish",
    )(scalars, *own, *other, before, rows, across)[:2]


def ring_of(chips):
    return list(range(0, chips, 2)) + list(range(chips - 1, 0, -2))


def on_device(tokens, route_ids, route_weights):
    devices = lax.axis_size("tok")
    position = lax.axis_index("tok")
    tok_rows, width = tokens.shape
    grid = math.isqrt(devices)
    edge = width // grid
    group = devices // EXP
    slab = width // group
    chips = devices // CORES
    ring = ring_of(chips)
    ahead = [
        (ring[i] * CORES + c, ring[(i + 1) % chips] * CORES + c)
        for i in range(chips)
        for c in range(CORES)
    ]
    streams = [ahead, [(b, a) for a, b in ahead]]
    pair = [(d, d ^ 1) for d in range(devices)]
    column = position % grid
    scalars = jnp.stack(
        [
            position // group,
            position // grid,
            column,
            column + 1 - 2 * (column % 2),
            position % group,
        ]
    ).astype(jnp.int32)

    def swap(array):
        return lax.ppermute(array, "tok", pair)

    def advance(held):
        return [lax.ppermute(array, "tok", stream) for array, stream in zip(held, streams)]

    rounds = chips // 2
    total = 4 * CAP * rounds

    pieces = [make_message(tokens, route_ids, route_weights)]
    operands, sums = [], []
    half = tok_rows * (width // LANES // 2)
    for step in range(1, rounds + 1):
        held = pieces * CORES if step == 1 else pieces
        if step == rounds:
            held = [held[0][: half + TABLE], held[1][half:]]
        moved = advance(held)
        tile, columns, packed = absorb(scalars, pieces, sums, edge)
        sums = [tile] + [swap(array) for array in columns]
        at = 4 * CAP * (step - 2) if step > 1 else total - 4 * CAP
        packs = list(packed) + [swap(array) for array in packed]
        operands = prepare(scalars, packs, at, operands, total, slab)
        if step < rounds:
            ahead_of, operands, sums = lax.optimization_barrier((moved[0], operands, sums))
            back_of, operands, sums = lax.optimization_barrier((moved[1], operands, sums))
            moved = [ahead_of, back_of]
        pieces = moved
    tile, pieces = settle(sums), list(pieces)
    for k in range(len(pieces)):
        pieces[k], operands, tile = lax.optimization_barrier((pieces[k], operands, tile))
    others = [swap(piece) for piece in pieces]
    operands = take_own(scalars, pieces, operands)
    return tuple(finish(scalars, pieces, others, tile, operands, 1.0 / (devices * tok_rows)))


def solution(mesh):
    in_specs = (P(("grp", "tok"), None), P(("grp", "tok"), None), P(("grp", "tok"), None))
    out_specs = (P(("grp", "tok"), None), P(("grp", "tok"), None, None))
    return jax.shard_map(
        on_device, mesh=mesh, in_specs=in_specs, out_specs=out_specs, check_vma=False
    )
```
